32 devices in a mesh: groups: 2 (over x), frames: 16 (over z, y, core).
Axes of the slice: x: 2, y: 2, z: 4, core: 2. Of those that a mesh axis runs over, the one named last changes fastest.
Arguments:
- features: bfloat16 [4096, 1024], P(('groups', 'frames')), parts along dimension 0, may hold values from -6 to 6
- valid_length: int32 [2], P('groups'), parts along dimension 0, may hold values from 1024 to 2048
- ln1_gain: float32 [1024], replicated, may hold values from 0.5 to 1.5
- w_qkv: bfloat16 [1024, 1536], P('frames'), may hold values from -3 to 3
- w_out: bfloat16 [512, 1024], P('frames'), may hold values from -0.25 to 0.25
- ln2_gain: float32 [1024], replicated, may hold values from 0.5 to 1.5
- w_pw1: bfloat16 [1024, 2048], P('frames'), may hold values from -0.1875 to 0.1875
- w_dw: float32 [9, 1024], replicated, may hold values from -2 to 2
- bn_scale: float32 [1024], replicated, may hold values from 0.5 to 2
- bn_shift: float32 [1024], replicated, may hold values from -3 to 3
- w_pw2: bfloat16 [1024, 1024], P('frames'), may hold values from -0.1875 to 0.1875
Outputs:
- block_out: bfloat16 [4096, 1024], P(('groups', 'frames')), parts along dimension 0
The draws below stay inside these ranges and needn't reach their ends.
There are 2 independent parts, one for each index of `groups`. The reference program is written for one: setup_inputs(seed, part) draws one part's arguments, and reference() takes and returns one part's arrays. A program takes and returns all parts, laid end to end along the dimension named above; an argument that names none is the same for every part. Nothing has to cross between parts.
All inputs are finite; a program needn't handle non-finite values.
Results may differ from the reference program's by a relative error of at most 0.0098.
Values may be sent and summed in bfloat16 or wider, within the bound.
A program may use at most 128 MiB of HBM per device.

```python
import math
import jax
import jax.numpy as jnp
from jax import lax

D = 1024
HEADS = 4
HD = 128
KERNEL = 9
FRAMES = 2048
ATT = 512
HALF = 4


def draw_w_qkv(key, part):
    first, second, third = jax.random.split(key, 3)
    root = 1.0 / math.sqrt(D)
    w_query = jax.random.normal(first, (D, ATT), jnp.float32) * (1.5 * root)
    w_key = jax.random.normal(second, (D, ATT), jnp.float32) * (1.5 * root)
    w_value = jax.random.normal(third, (D, ATT), jnp.float32) * root
    joined = jnp.concatenate([w_query, w_key, w_value], axis=1)
    return jnp.clip(joined, -3.0, 3.0).astype(jnp.bfloat16)


def block_scale(stream_key, dims, cuts, smallest, high):
    level = 1.0
    for axis_at, blocks in cuts:
        steps = jax.random.uniform(jax.random.fold_in(jax.random.fold_in(stream_key, 6), axis_at), (blocks,), jnp.float32, smallest / len(cuts), high / len(cuts))
        level = level * jnp.repeat(jnp.exp(steps), dims[axis_at] // blocks).reshape((-1,) + (1,) * (len(dims) - 1 - axis_at))
    return level


def gaussian(own_key, extent, deviation, most, pieces=(), held_as=jnp.bfloat16):
    factor_of = block_scale(own_key, extent, pieces, -0.22, 0.18) if pieces else 1.0
    array = jax.random.normal(own_key, extent, jnp.float32) * deviation * factor_of
    return jnp.minimum(jnp.maximum(array, -most), most).astype(held_as)


def setup_inputs(seed: int = 0, part: int = 0) -> dict:
    arg_keys = jax.random.split(jax.random.key(seed), 12)
    part_splits = jax.random.split(jax.random.fold_in(arg_keys[11], part), 12)
    features = gaussian(part_splits[0], (FRAMES, D), 1.0, 6.0, ((0, 16),))
    valid_length = jax.random.randint(part_splits[1], (1,), FRAMES // 2, FRAMES + 1).astype(jnp.int32)
    ln1_gain = jnp.clip(1.0 + 0.1 * jax.random.normal(arg_keys[2], (D,), jnp.float32), 0.5, 1.5)
    w_qkv = draw_w_qkv(jax.random.fold_in(arg_keys[11], 71), part)
    w_out = gaussian(arg_keys[4], (ATT, D), ATT ** -0.5, 0.25, ((0, 16),))
    ln2_gain = jnp.clip(1.0 + 0.1 * jax.random.normal(arg_keys[5], (D,), jnp.float32), 0.5, 1.5)
    w_pw1 = gaussian(arg_keys[6], (D, 2 * D), D ** -0.5, 0.1875, ((0, 16),))
    w_dw = gaussian(arg_keys[7], (KERNEL, D), KERNEL ** -0.5, 2.0, (), jnp.float32)
    bn_scale = jnp.clip(jnp.exp(jax.random.uniform(arg_keys[8], (D,), jnp.float32, math.log(0.5), math.log(2.0))), 0.5, 2.0)
    bn_shift = gaussian(arg_keys[9], (D,), 0.5, 3.0, (), jnp.float32)
    w_pw2 = gaussian(arg_keys[10], (D, D), D ** -0.5, 0.1875, ((0, 16),))
    return dict(features=features, valid_length=valid_length, ln1_gain=ln1_gain, w_qkv=w_qkv, w_out=w_out, ln2_gain=ln2_gain, w_pw1=w_pw1, w_dw=w_dw, bn_scale=bn_scale, bn_shift=bn_shift, w_pw2=w_pw2)


EPSILON = 1e-05

def layer_norm(values, gain):
    values = values.astype(jnp.float32)
    mean = lax.optimization_barrier(jnp.mean(values, axis=-1, keepdims=True))
    centred = values - mean
    variance = lax.optimization_barrier(jnp.mean(centred * centred, axis=-1, keepdims=True))
    return (centred * lax.rsqrt(variance + EPSILON) * gain).astype(jnp.bfloat16)

def reference(features, valid_length, ln1_gain, w_qkv, w_out, ln2_gain, w_pw1, w_dw, bn_scale, bn_shift, w_pw2):
    limit = valid_length[0]
    normed1 = layer_norm(features, ln1_gain)
    qkv = jnp.dot(normed1, w_qkv, preferred_element_type=jnp.float32).astype(jnp.bfloat16)
    queries = qkv[:, :ATT].reshape(FRAMES, HEADS, HD).transpose(1, 0, 2)
    keys = qkv[:, ATT:2 * ATT].reshape(FRAMES, HEADS, HD).transpose(1, 0, 2)
    values = qkv[:, 2 * ATT:].reshape(FRAMES, HEADS, HD).transpose(1, 0, 2)
    key_valid = (jnp.arange(FRAMES, dtype=jnp.int32) < limit)[None, :]
    scale = 1.0 / math.sqrt(HD)
    block = math.gcd(FRAMES, 512)

    def one_head(triple):
        head_q, head_k, head_v = triple
        blocks_q = head_q.reshape(FRAMES // block, block, HD)

        def one_block(query_rows):
            scores = jnp.dot(query_rows, head_k.T, preferred_element_type=jnp.float32) * scale
            scores = jnp.where(key_valid, scores, -1e+30)
            peak = lax.optimization_barrier(jnp.max(scores, axis=-1, keepdims=True))
            weights = jnp.where(key_valid, jnp.exp(scores - peak), 0.0)
            totals = lax.optimization_barrier(jnp.sum(weights, axis=-1, keepdims=True))
            summed = jnp.dot(weights.astype(jnp.bfloat16), head_v, preferred_element_type=jnp.float32)
            return summed / totals
        return lax.map(one_block, blocks_q).reshape(FRAMES, HD)
    context = lax.map(one_head, (queries, keys, values))
    context = context.transpose(1, 0, 2).reshape(FRAMES, ATT).astype(jnp.bfloat16)
    attended = features.astype(jnp.float32) + jnp.dot(context, w_out, preferred_element_type=jnp.float32)
    normed2 = layer_norm(attended, ln2_gain)
    both = jnp.dot(normed2, w_pw1, preferred_element_type=jnp.float32)
    frame_valid = (jnp.arange(FRAMES, dtype=jnp.int32) < limit)[:, None]
    gated = jnp.where(frame_valid, both[:, :D] * jax.nn.sigmoid(both[:, D:]), 0.0).astype(jnp.bfloat16)
    padded = jnp.pad(gated.astype(jnp.float32), ((HALF, HALF), (0, 0)))
    conv = jnp.zeros((FRAMES, D), jnp.float32)
    for tap in range(KERNEL):
        conv = conv + w_dw[tap][None, :] * padded[tap:tap + FRAMES]
    activated = jax.nn.silu(bn_scale * conv + bn_shift).astype(jnp.bfloat16)
    result = attended + jnp.dot(activated, w_pw2, preferred_element_type=jnp.float32)
    return result.astype(jnp.bfloat16)
```

```python
import functools
import math

import jax
import jax.numpy as jnp
from jax import lax
from jax.experimental import pallas as pl
from jax.experimental.pallas import tpu as pltpu
from jax.sharding import PartitionSpec as P

HEADS = 4
HD = 128


EPSILON = 1e-05


def extended(cells, sides, width):
    for axis, dim in sides:
        count = lax.axis_size(axis)
        ends = count - 1
        head = lax.slice_in_dim(cells, 0, width, axis=dim)
        tail = lax.slice_in_dim(cells, cells.shape[dim] - width, cells.shape[dim], axis=dim)
        cells = jnp.concatenate(
            [
                lax.ppermute(tail, axis, [(i, (i + 1) % count) for i in range(ends)]),
                cells,
                lax.ppermute(head, axis, [((i + 1) % count, i) for i in range(ends)]),
            ],
            axis=dim,
        )
    return cells


def layer_norm(values, gain):
    values = values.astype(jnp.float32)
    mean = jnp.mean(values, axis=-1, keepdims=True)
    centred = values - mean
    variance = jnp.mean(centred * centred, axis=-1, keepdims=True)
    return (centred * lax.rsqrt(variance + EPSILON) * gain).astype(jnp.bfloat16)


def per_device_xla(
    features, valid_length, ln1_gain, w_qkv, w_out, ln2_gain, w_pw1, w_dw, bn_scale, bn_shift, w_pw2
):
    limit = valid_length[0]
    local_rows = features.shape[0]
    width = features.shape[1]
    att_width = w_qkv.shape[1] // 3
    scale = 1.0 / math.sqrt(HD)
    tails = (
        lax.all_gather(w_out, "frames", axis=0, tiled=True),
        lax.all_gather(w_pw1, "frames", axis=0, tiled=True),
        lax.all_gather(w_pw2, "frames", axis=0, tiled=True),
    )
    full_out, full_pw1, full_pw2 = tails
    normed1 = layer_norm(features, ln1_gain)
    qkv = jnp.dot(
        normed1,
        lax.all_gather(w_qkv, "frames", axis=0, tiled=True),
        preferred_element_type=jnp.float32,
    ).astype(jnp.bfloat16)
    query_heads = qkv[:, :att_width].reshape(local_rows, HEADS, HD)
    keys = qkv[:, att_width : 2 * att_width]
    values = qkv[:, 2 * att_width :]
    maxima = jnp.full((HEADS, local_rows), -1e30, jnp.float32)
    key_rows = lax.all_gather(keys, "frames", axis=0, tiled=True)
    value_rows = lax.all_gather(values, "frames", axis=0, tiled=True)
    count = key_rows.shape[0]
    key_heads = key_rows.reshape(count, HEADS, HD)
    value_heads = value_rows.reshape(count, HEADS, HD)
    scores = (
        jnp.einsum("qhd,khd->hqk", query_heads, key_heads, preferred_element_type=jnp.float32)
        * scale
    )
    position = jnp.arange(count, dtype=jnp.int32)
    valid = (position < limit)[None, None, :]
    scores = jnp.where(valid, scores, -1e30)
    fresh = jnp.maximum(maxima, jnp.max(scores, axis=-1))
    weights = jnp.where(valid, jnp.exp(scores - fresh[..., None]), 0.0)
    totals = jnp.sum(weights, axis=-1)
    update = jnp.einsum(
        "hqk,khd->hqd",
        weights.astype(jnp.bfloat16),
        value_heads,
        preferred_element_type=jnp.float32,
    )
    summed = update
    maxima, totals, summed = (fresh, totals, summed)
    context = (
        (summed / totals[..., None])
        .transpose(1, 0, 2)
        .reshape(local_rows, att_width)
        .astype(jnp.bfloat16)
    )
    attended = features.astype(jnp.float32) + jnp.dot(
        context, full_out, preferred_element_type=jnp.float32
    )
    normed2 = layer_norm(attended, ln2_gain)
    both = jnp.dot(normed2, full_pw1, preferred_element_type=jnp.float32)
    frame_index = lax.axis_index("frames") * local_rows + jnp.arange(local_rows, dtype=jnp.int32)
    frame_valid = (frame_index < limit)[:, None]
    gated = jnp.where(frame_valid, both[:, :width] * jax.nn.sigmoid(both[:, width:]), 0.0).astype(
        jnp.bfloat16
    )
    half_window = (w_dw.shape[0] - 1) // 2
    widened = extended(gated, (("frames", 0),), half_window)
    widened = widened.astype(jnp.float32)
    conv = jnp.zeros((local_rows, width), jnp.float32)
    for tap in range(w_dw.shape[0]):
        conv = conv + w_dw[tap][None, :] * widened[tap : tap + local_rows]
    activated = jax.nn.silu(bn_scale * conv + bn_shift).astype(jnp.bfloat16)
    result = attended + jnp.dot(activated, full_pw2, preferred_element_type=jnp.float32)
    return result.astype(jnp.bfloat16)


ZS = 4
CHUNK = 256
PAD = 16
QKV, FEAT, OUT, PW1, PW2 = range(5)
WHOLE, CROSS, SPLIT = range(3)
KIND = (CROSS, WHOLE, CROSS, SPLIT, CROSS)


def norm_rows(values, gain):
    values = values.astype(jnp.float32)
    mean = jnp.mean(values, axis=-1, keepdims=True)
    centred = values - mean
    variance = jnp.mean(centred * centred, axis=-1, keepdims=True)
    return (centred * lax.rsqrt(variance + EPSILON) * gain).astype(jnp.bfloat16)


def block_kernel(
    limit_ref, feat_ref, ln1_ref, qkv_ref, out_w_ref, ln2_ref, pw1_ref, dw_ref, bns_ref, bnb_ref, pw2_ref,
    result_ref,
    g_qkv, g_feat, g_out, g_pw1, g_pw2, kv, rows_n, ext, ext_n, query, context, attended, gate, act,
    local_sem, zp_send, zm_send, z_recv, y_send, y_recv, x_send, x_recv, c_send, c_recv,
):
    twin = lax.axis_index("groups")
    me = lax.axis_index("frames")
    z, y, c = me // 4, (me // 2) % 2, me % 2
    gathered = (g_qkv, g_feat, g_out, g_pw1, g_pw2)
    shards = (qkv_ref, feat_ref, out_w_ref, pw1_ref, pw2_ref)
    above, below = {"frames": me + 4}, {"frames": me - 4}
    across = {"frames": me + 2 - 4 * y}
    core = {"frames": me + 1 - 2 * c}
    other = {"groups": 1 - twin}
    att = query.shape[1]
    width = ext.shape[1]
    local_rows = feat_ref.shape[0]

    own = []
    for q in range(5):
        if KIND[q] == SPLIT:
            own.append(
                pltpu.make_async_copy(shards[q].at[twin], gathered[q].at[z, y, c, twin], local_sem.at[q])
            )
        else:
            own.append(pltpu.make_async_copy(shards[q], gathered[q].at[z, y, c], local_sem.at[q]))
        own[-1].start()

    barrier = pltpu.get_barrier_semaphore()

    def greet(device):
        pl.semaphore_signal(barrier, inc=1, device_id=device, device_id_type=pl.DeviceIdType.MESH)

    greet(across)
    greet(core)
    greet(other)
    pl.when(z > 0)(lambda: greet(below))
    pl.when(z < ZS - 1)(lambda: greet(above))
    pl.semaphore_wait(
        barrier, 3 + jnp.where(z > 0, 1, 0) + jnp.where(z < ZS - 1, 1, 0)
    )

    def remote(src, dst, send, recv, device):
        return pltpu.make_async_remote_copy(
            src_ref=src, dst_ref=dst, send_sem=send, recv_sem=recv,
            device_id=device, device_id_type=pl.DeviceIdType.MESH,
        )

    def along_z(q, source, up):
        part = gathered[q].at[source, y, c]
        if KIND[q] == SPLIT:
            part = part.at[twin]
        send = zp_send if up else zm_send
        return remote(part, part, send.at[q, source], z_recv.at[q, source], above if up else below)

    def along_y(q, source, column):
        part = gathered[q].at[source, column, c]
        if KIND[q] != WHOLE:
            part = part.at[twin]
        return remote(part, part, y_send.at[q, source], y_recv.at[q, source], across)

    def along_x(q, half):
        if KIND[q] == SPLIT:
            part = gathered[q].at[:, :, c, half]
        else:
            part = gathered[q].at[:, 1 - y, c, half]
        return remote(part, part, x_send.at[q], x_recv.at[q], other)

    def to_core(q, which):
        part = gathered[q].at[:, :, which]
        return remote(part, part, c_send.at[q], c_recv.at[q], core)

    def begin(q):
        own[q].wait()
        pl.when(z < ZS - 1)(lambda: along_z(q, z, True).start())
        pl.when(z > 0)(lambda: along_z(q, z, False).start())
        along_y(q, z, y).start()

    def pass_on(q, s):
        @pl.when(z >= s)
        def _():
            source = z - s
            along_z(q, source, True).wait_recv()
            pl.when(z < ZS - 1)(lambda: along_z(q, source, True).start())
            along_y(q, source, y).start()

        @pl.when(z + s <= ZS - 1)
        def _():
            source = z + s
            along_z(q, source, False).wait_recv()
            pl.when(z > 0)(lambda: along_z(q, source, False).start())
            along_y(q, source, y).start()

    def cross(q):
        for source in range(ZS):
            along_y(q, source, 1 - y).wait_recv()
        if KIND[q] == WHOLE:
            to_core(q, c).start()
        else:
            along_x(q, twin).start()

    def swap(q):
        along_x(q, 1 - twin).wait_recv()
        to_core(q, c).start()

    def arrive(q):
        to_core(q, 1 - c).wait_recv()

    def finish(q):
        pl.when(z < ZS - 1)(lambda: along_z(q, z, True).wait_send())
        pl.when(z > 0)(lambda: along_z(q, z, False).wait_send())
        for s in range(1, ZS):
            pl.when((z >= s) & (z < ZS - 1))(lambda: along_z(q, z - s, True).wait_send())
            pl.when((z + s <= ZS - 1) & (z > 0))(lambda: along_z(q, z + s, False).wait_send())
        for source in range(ZS):
            along_y(q, source, y).wait_send()
        if KIND[q] != WHOLE:
            along_x(q, twin).wait_send()
        to_core(q, c).wait_send()

    def columns(ref, start):
        block = ref[:, :, :, :, :, pl.ds(start, CHUNK)]
        return block.reshape(-1, CHUNK)

    def at(j):
        return pl.multiple_of(j * CHUNK, CHUNK)

    def key_values(r):
        rows_n[...] = norm_rows(g_feat[r].reshape(rows_n.shape), ln1_ref[...])

        def some(j, carry):
            product = jnp.dot(
                rows_n[...], columns(g_qkv, at(j) + att), preferred_element_type=jnp.float32
            )
            kv[r, :, pl.ds(at(j), CHUNK)] = product.astype(jnp.bfloat16)
            return carry

        lax.fori_loop(0, 2 * att // CHUNK, some, 0)

    def queries():
        before = jnp.maximum(me - 1, 0)
        after = jnp.minimum(me + 1, 4 * ZS - 1)
        ext[pl.ds(0, PAD), :] = g_feat[before // 4, (before // 2) % 2, before % 2, pl.ds(local_rows - PAD, PAD), :]
        ext[pl.ds(PAD, local_rows), :] = g_feat[z, y, c]
        ext[pl.ds(PAD + local_rows, PAD), :] = g_feat[after // 4, (after // 2) % 2, after % 2, pl.ds(0, PAD), :]
        ext_n[...] = norm_rows(ext[...], ln1_ref[...])

        def some(j, carry):
            product = jnp.dot(ext_n[...], columns(g_qkv, at(j)), preferred_element_type=jnp.float32)
            query[:, pl.ds(at(j), CHUNK)] = product.astype(jnp.bfloat16)
            return carry

        lax.fori_loop(0, att // CHUNK, some, 0)

    def attend(h):
        keys = kv[:, :, pl.ds(h * HD, HD)].reshape(-1, HD)
        scores = lax.dot_general(
            query[:, pl.ds(h * HD, HD)], keys, (((1,), (1,)), ((), ())), preferred_element_type=jnp.float32
        ) * (1.0 / math.sqrt(HD))
        valid = lax.broadcasted_iota(jnp.int32, scores.shape, 1) < limit_ref[0]
        scores = jnp.where(valid, scores, -1e30)
        peak = jnp.max(scores, axis=-1, keepdims=True)
        weights = jnp.where(valid, jnp.exp(scores - peak), 0.0)
        totals = jnp.sum(weights, axis=-1, keepdims=True)
        values = kv[:, :, pl.ds(att + h * HD, HD)].reshape(-1, HD)
        summed = jnp.dot(weights.astype(jnp.bfloat16), values, preferred_element_type=jnp.float32)
        context[:, pl.ds(h * HD, HD)] = (summed / totals).astype(jnp.bfloat16)

    def project():
        def some(j, carry):
            product = jnp.dot(context[...], columns(g_out, at(j)), preferred_element_type=jnp.float32)
            attended[:, pl.ds(at(j), CHUNK)] = ext[:, pl.ds(at(j), CHUNK)].astype(jnp.float32) + product
            return carry

        lax.fori_loop(0, width // CHUNK, some, 0)
        ext_n[...] = norm_rows(attended[...], ln2_ref[...])

    def convolve():
        def some(j, carry):
            value = jnp.dot(ext_n[...], columns(g_pw1, at(j)), preferred_element_type=jnp.float32)
            gates = jnp.dot(ext_n[...], columns(g_pw1, at(j) + width), preferred_element_type=jnp.float32)
            frame = me * local_rows - PAD + lax.broadcasted_iota(jnp.int32, value.shape, 0)
            valid = (frame >= 0) & (frame < limit_ref[0])
            gated = jnp.where(valid, value * jax.nn.sigmoid(gates), 0.0)
            gate[...] = gated.astype(jnp.bfloat16).astype(jnp.float32)
            taps = dw_ref.shape[0]
            cols = pl.ds(at(j), CHUNK)
            conv = jnp.zeros((local_rows, CHUNK), jnp.float32)
            for tap in range(taps):
                conv = conv + dw_ref[pl.ds(tap, 1), cols] * gate[pl.ds(PAD - taps // 2 + tap, local_rows), :]
            shifted = bns_ref[:, cols] * conv + bnb_ref[:, cols]
            act[:, cols] = (shifted / (1.0 + jnp.exp(-shifted))).astype(jnp.bfloat16)
            return carry

        lax.fori_loop(0, width // CHUNK, some, 0)

    def close():
        def some(j, carry):
            cols = pl.ds(at(j), CHUNK)
            product = jnp.dot(act[...], columns(g_pw2, at(j)), preferred_element_type=jnp.float32)
            result_ref[:, cols] = (attended[pl.ds(PAD, local_rows), cols] + product).astype(jnp.bfloat16)
            return carry

        lax.fori_loop(0, width // CHUNK, some, 0)

    begin(QKV)
    begin(FEAT)
    pass_on(QKV, 1)
    pass_on(FEAT, 1)
    pass_on(QKV, 2)
    pass_on(FEAT, 2)
    pass_on(QKV, 3)
    begin(OUT)
    pass_on(FEAT, 3)
    begin(PW1)
    cross(QKV)
    cross(FEAT)
    swap(QKV)
    pass_on(OUT, 1)
    arrive(QKV)
    arrive(FEAT)
    key_values(0)
    pass_on(PW1, 1)
    pass_on(OUT, 2)
    begin(PW2)
    key_values(1)
    pass_on(PW1, 2)
    pass_on(OUT, 3)
    pass_on(PW2, 1)
    key_values(2)
    pass_on(PW1, 3)
    pass_on(PW2, 2)
    key_values(3)
    cross(OUT)
    pass_on(PW2, 3)
    queries()
    attend(0)
    cross(PW1)
    swap(OUT)
    attend(1)
    cross(PW2)
    swap(PW1)
    attend(2)
    swap(PW2)
    attend(3)
    arrive(OUT)
    project()
    arrive(PW1)
    convolve()
    arrive(PW2)
    close()
    for q in range(5):
        finish(q)


def per_device_kernel(
    features, valid_length, ln1_gain, w_qkv, w_out, ln2_gain, w_pw1, w_dw, bn_scale, bn_shift, w_pw2
):
    local_rows, width = features.shape
    att = w_qkv.shape[1] // 3
    wide = local_rows + 2 * PAD

    def halves(weight):
        return weight.reshape(2, weight.shape[0] // 2, weight.shape[1])

    shards = [halves(w) for w in (w_qkv, w_out, w_pw1, w_pw2)]
    grid = (ZS, 2, 2)
    bf16, f32 = jnp.bfloat16, jnp.float32
    dma = pltpu.SemaphoreType.DMA
    hbm = pl.BlockSpec(memory_space=pl.ANY)
    vmem = pl.BlockSpec(memory_space=pltpu.VMEM)
    return pl.pallas_call(
        block_kernel,
        out_shape=jax.ShapeDtypeStruct((local_rows, width), bf16),
        in_specs=[
            pl.BlockSpec(memory_space=pltpu.SMEM), hbm, vmem, hbm, hbm, vmem, hbm, vmem, vmem, vmem, hbm,
        ],
        out_specs=vmem,
        scratch_shapes=[
            pltpu.VMEM(grid + shards[0].shape, bf16),
            pltpu.VMEM(grid + features.shape, bf16),
            pltpu.VMEM(grid + shards[1].shape, bf16),
            pltpu.VMEM(grid + shards[2].shape, bf16),
            pltpu.VMEM(grid + shards[3].shape, bf16),
            pltpu.VMEM((ZS, 4 * local_rows, 2 * att), bf16),
            pltpu.VMEM((4 * local_rows, width), bf16),
            pltpu.VMEM((wide, width), bf16),
            pltpu.VMEM((wide, width), bf16),
            pltpu.VMEM((wide, att), bf16),
            pltpu.VMEM((wide, att), bf16),
            pltpu.VMEM((wide, width), f32),
            pltpu.VMEM((wide, CHUNK), f32),
            pltpu.VMEM((local_rows, width), bf16),
            dma((5,)),
        ]
        + [dma((5, ZS))] * 5
        + [dma((5,))] * 4,
        compiler_params=pltpu.CompilerParams(
            collective_id=0, has_side_effects=True, vmem_limit_bytes=56 * 1024 * 1024
        ),
    )(
        valid_length, features, ln1_gain[None], shards[0], shards[1], ln2_gain[None], shards[2], w_dw,
        bn_scale[None], bn_shift[None], shards[3],
    )


def per_device(*arguments):
    if lax.axis_size("frames") == 4 * ZS and lax.axis_size("groups") == 2:
        return per_device_kernel(*arguments)
    return per_device_xla(*arguments)


def solution(mesh):
    placed = (
        P(("groups", "frames"), None),
        P("groups"),
        P(),
        P("frames", None),
        P("frames", None),
        P(),
        P("frames", None),
        P(),
        P(),
        P(),
        P("frames", None),
    )
    return jax.shard_map(
        per_device,
        mesh=mesh,
        in_specs=placed,
        out_specs=P(("groups", "frames"), None),
        check_vma=False,
    )
```

```python
import functools
import math

import jax
import jax.numpy as jnp
from jax import lax
from jax.experimental import pallas as pl
from jax.experimental.pallas import tpu as pltpu
from jax.sharding import PartitionSpec as P

HEADS = 4
HD = 128


EPSILON = 1e-05


def extended(cells, sides, width):
    for axis, dim in sides:
        count = lax.axis_size(axis)
        ends = count - 1
        head = lax.slice_in_dim(cells, 0, width, axis=dim)
        tail = lax.slice_in_dim(cells, cells.shape[dim] - width, cells.shape[dim], axis=dim)
        cells = jnp.concatenate(
            [
                lax.ppermute(tail, axis, [(i, (i + 1) % count) for i in range(ends)]),
                cells,
                lax.ppermute(head, axis, [((i + 1) % count, i) for i in range(ends)]),
            ],
            axis=dim,
        )
    return cells


def layer_norm(values, gain):
    values = values.astype(jnp.float32)
    mean = jnp.mean(values, axis=-1, keepdims=True)
    centred = values - mean
    variance = jnp.mean(centred * centred, axis=-1, keepdims=True)
    return (centred * lax.rsqrt(variance + EPSILON) * gain).astype(jnp.bfloat16)


def per_device_xla(
    features, valid_length, ln1_gain, w_qkv, w_out, ln2_gain, w_pw1, w_dw, bn_scale, bn_shift, w_pw2
):
    limit = valid_length[0]
    local_rows = features.shape[0]
    width = features.shape[1]
    att_width = w_qkv.shape[1] // 3
    scale = 1.0 / math.sqrt(HD)
    tails = (
        lax.all_gather(w_out, "frames", axis=0, tiled=True),
        lax.all_gather(w_pw1, "frames", axis=0, tiled=True),
        lax.all_gather(w_pw2, "frames", axis=0, tiled=True),
    )
    full_out, full_pw1, full_pw2 = tails
    normed1 = layer_norm(features, ln1_gain)
    qkv = jnp.dot(
        normed1,
        lax.all_gather(w_qkv, "frames", axis=0, tiled=True),
        preferred_element_type=jnp.float32,
    ).astype(jnp.bfloat16)
    query_heads = qkv[:, :att_width].reshape(local_rows, HEADS, HD)
    keys = qkv[:, att_width : 2 * att_width]
    values = qkv[:, 2 * att_width :]
    maxima = jnp.full((HEADS, local_rows), -1e30, jnp.float32)
    key_rows = lax.all_gather(keys, "frames", axis=0, tiled=True)
    value_rows = lax.all_gather(values, "frames", axis=0, tiled=True)
    count = key_rows.shape[0]
    key_heads = key_rows.reshape(count, HEADS, HD)
    value_heads = value_rows.reshape(count, HEADS, HD)
    scores = (
        jnp.einsum("qhd,khd->hqk", query_heads, key_heads, preferred_element_type=jnp.float32)
        * scale
    )
    position = jnp.arange(count, dtype=jnp.int32)
    valid = (position < limit)[None, None, :]
    scores = jnp.where(valid, scores, -1e30)
    fresh = jnp.maximum(maxima, jnp.max(scores, axis=-1))
    weights = jnp.where(valid, jnp.exp(scores - fresh[..., None]), 0.0)
    totals = jnp.sum(weights, axis=-1)
    update = jnp.einsum(
        "hqk,khd->hqd",
        weights.astype(jnp.bfloat16),
        value_heads,
        preferred_element_type=jnp.float32,
    )
    summed = update
    maxima, totals, summed = (fresh, totals, summed)
    context = (
        (summed / totals[..., None])
        .transpose(1, 0, 2)
        .reshape(local_rows, att_width)
        .astype(jnp.bfloat16)
    )
    attended = features.astype(jnp.float32) + jnp.dot(
        context, full_out, preferred_element_type=jnp.float32
    )
    normed2 = layer_norm(attended, ln2_gain)
    both = jnp.dot(normed2, full_pw1, preferred_element_type=jnp.float32)
    frame_index = lax.axis_index("frames") * local_rows + jnp.arange(local_rows, dtype=jnp.int32)
    frame_valid = (frame_index < limit)[:, None]
    gated = jnp.where(frame_valid, both[:, :width] * jax.nn.sigmoid(both[:, width:]), 0.0).astype(
        jnp.bfloat16
    )
    half_window = (w_dw.shape[0] - 1) // 2
    widened = extended(gated, (("frames", 0),), half_window)
    widened = widened.astype(jnp.float32)
    conv = jnp.zeros((local_rows, width), jnp.float32)
    for tap in range(w_dw.shape[0]):
        conv = conv + w_dw[tap][None, :] * widened[tap : tap + local_rows]
    activated = jax.nn.silu(bn_scale * conv + bn_shift).astype(jnp.bfloat16)
    result = attended + jnp.dot(activated, full_pw2, preferred_element_type=jnp.float32)
    return result.astype(jnp.bfloat16)


ZS = 4
CHUNK = 256
PAD = 16
HALO = 8
KVW, FEAT, QW, OUT, PW1, PW2 = range(6)
COLUMN, CROSS, SPLIT = range(3)
KIND = (CROSS, COLUMN, CROSS, CROSS, SPLIT, CROSS)
COUNT = len(KIND)


def norm_rows(values, gain):
    values = values.astype(jnp.float32)
    mean = jnp.mean(values, axis=-1, keepdims=True)
    centred = values - mean
    variance = jnp.mean(centred * centred, axis=-1, keepdims=True)
    return (centred * lax.rsqrt(variance + EPSILON) * gain).astype(jnp.bfloat16)


def block_kernel(
    limit_ref, feat_ref, ln1_ref, qkv_ref, out_w_ref, ln2_ref, pw1_ref, dw_ref, bns_ref, bnb_ref, pw2_ref,
    result_ref,
    g_kvw, g_feat, g_qw, g_out, g_pw1, g_pw2, kv, halo, rows_n, ext, ext_n, query, context, attended, gate, act,
    local_sem, zp_send, zm_send, z_recv, y_send, y_recv, x_send, x_recv, c_send, c_recv, kvc_send, kvc_recv,
    halo_send, halo_recv,
):
    twin = lax.axis_index("groups")
    me = lax.axis_index("frames")
    z, y, c = me // 4, (me // 2) % 2, me % 2
    att = query.shape[1]
    width = ext.shape[1]
    local_rows = feat_ref.shape[0]
    last = 4 * ZS - 1
    gathered = (g_kvw, g_feat, g_qw, g_out, g_pw1, g_pw2)
    shards = (
        qkv_ref.at[:, :, pl.ds(att, 2 * att)], feat_ref, qkv_ref.at[:, :, pl.ds(0, att)], out_w_ref, pw1_ref, pw2_ref,
    )
    above, below = {"frames": me + 4}, {"frames": me - 4}
    across = {"frames": me + 2 - 4 * y}
    core = {"frames": me + 1 - 2 * c}
    other = {"groups": 1 - twin}

    own = []
    for q in range(COUNT):
        if KIND[q] == SPLIT:
            own.append(
                pltpu.make_async_copy(shards[q].at[twin], gathered[q].at[z, y, c, twin], local_sem.at[q])
            )
        else:
            part = gathered[q].at[z] if KIND[q] == COLUMN else gathered[q].at[z, y, c]
            own.append(pltpu.make_async_copy(shards[q], part, local_sem.at[q]))
        own[-1].start()

    halo[...] = jnp.zeros_like(halo)
    barrier = pltpu.get_barrier_semaphore()

    def greet(device):
        pl.semaphore_signal(barrier, inc=1, device_id=device, device_id_type=pl.DeviceIdType.MESH)

    greet(across)
    greet(core)
    greet(other)
    pl.when(z > 0)(lambda: greet(below))
    pl.when(z < ZS - 1)(lambda: greet(above))
    pl.when(me > 0)(lambda: greet({"frames": me - 1}))
    pl.when(me < last)(lambda: greet({"frames": me + 1}))
    greeted = 3
    for there in (z > 0, z < ZS - 1, me > 0, me < last):
        greeted = greeted + jnp.where(there, 1, 0)
    pl.semaphore_wait(barrier, greeted)

    def remote(src, dst, send, recv, device):
        return pltpu.make_async_remote_copy(
            src_ref=src, dst_ref=dst, send_sem=send, recv_sem=recv,
            device_id=device, device_id_type=pl.DeviceIdType.MESH,
        )

    def along_z(q, source, up):
        part = gathered[q].at[source] if KIND[q] == COLUMN else gathered[q].at[source, y, c]
        if KIND[q] == SPLIT:
            part = part.at[twin]
        send = zp_send if up else zm_send
        return remote(part, part, send.at[q, source], z_recv.at[q, source], above if up else below)

    def along_y(q, source, column):
        if KIND[q] == COLUMN:
            part = kv.at[source, column, c]
        else:
            part = gathered[q].at[source, column, c, twin]
        return remote(part, part, y_send.at[q, source], y_recv.at[q, source], across)

    def along_x(q, half):
        if KIND[q] == SPLIT:
            part = gathered[q].at[:, :, c, half]
        else:
            part = gathered[q].at[:, 1 - y, c, half]
        return remote(part, part, x_send.at[q], x_recv.at[q], other)

    def to_core(q, which):
        part = gathered[q].at[:, :, which]
        return remote(part, part, c_send.at[q], c_recv.at[q], core)

    def begin(q):
        own[q].wait()
        pl.when(z < ZS - 1)(lambda: along_z(q, z, True).start())
        pl.when(z > 0)(lambda: along_z(q, z, False).start())
        if KIND[q] != COLUMN:
            along_y(q, z, y).start()

    def pass_on(q, s):
        @pl.when(z >= s)
        def _():
            source = z - s
            along_z(q, source, True).wait_recv()
            pl.when(z < ZS - 1)(lambda: along_z(q, source, True).start())
            if KIND[q] != COLUMN:
                along_y(q, source, y).start()

        @pl.when(z + s <= ZS - 1)
        def _():
            source = z + s
            along_z(q, source, False).wait_recv()
            pl.when(z > 0)(lambda: along_z(q, source, False).start())
            if KIND[q] != COLUMN:
                along_y(q, source, y).start()

    def cross(q):
        for source in range(ZS):
            along_y(q, source, 1 - y).wait_recv()
        along_x(q, twin).start()

    def swap(q):
        along_x(q, 1 - twin).wait_recv()
        to_core(q, c).start()

    def arrive(q):
        to_core(q, 1 - c).wait_recv()

    def finish(q):
        pl.when(z < ZS - 1)(lambda: along_z(q, z, True).wait_send())
        pl.when(z > 0)(lambda: along_z(q, z, False).wait_send())
        for s in range(1, ZS):
            pl.when((z >= s) & (z < ZS - 1))(lambda: along_z(q, z - s, True).wait_send())
            pl.when((z + s <= ZS - 1) & (z > 0))(lambda: along_z(q, z + s, False).wait_send())
        for source in range(ZS):
            along_y(q, source, y).wait_send()
        if KIND[q] != COLUMN:
            along_x(q, twin).wait_send()
            to_core(q, c).wait_send()

    def kv_to_core(source, column, which):
        part = kv.at[source, column, which]
        slot = (source, column)
        return remote(part, part, kvc_send.at[slot], kvc_recv.at[slot], core)

    def in_round(s, do):
        if s == 0:
            do(z)
        else:
            pl.when(z >= s)(lambda: do(z - s))
            pl.when(z + s <= ZS - 1)(lambda: do(z + s))

    def edge(up):
        rows = pl.ds(local_rows - PAD, PAD) if up else pl.ds(0, PAD)
        slot = 0 if up else 1
        device = {"frames": me + 1 if up else me - 1}
        return remote(feat_ref.at[rows], halo.at[slot], halo_send.at[slot], halo_recv.at[slot], device)

    def columns(ref, start):
        block = ref[:, :, :, :, :, pl.ds(start, CHUNK)]
        return block.reshape(-1, CHUNK)

    def at(j):
        return pl.multiple_of(j * CHUNK, CHUNK)

    def key_values(source):
        rows_n[...] = norm_rows(g_feat[source], ln1_ref[...])

        def some(j, carry):
            product = jnp.dot(rows_n[...], columns(g_kvw, at(j)), preferred_element_type=jnp.float32)
            kv[source, y, c, :, pl.ds(at(j), CHUNK)] = product.astype(jnp.bfloat16)
            return carry

        lax.fori_loop(0, 2 * att // CHUNK, some, 0)
        along_y(FEAT, source, y).start()
        kv_to_core(source, y, c).start()

    def kv_cross(source):
        along_y(FEAT, source, 1 - y).wait_recv()
        kv_to_core(source, 1 - y, c).start()

    def queries():
        pl.when(me > 0)(lambda: edge(True).wait_recv())
        pl.when(me < last)(lambda: edge(False).wait_recv())
        ext[pl.ds(0, HALO), :] = halo[0].astype(jnp.float32)[PAD - HALO :]
        ext[pl.ds(HALO, local_rows), :] = g_feat[z].astype(jnp.float32)
        ext[pl.ds(HALO + local_rows, HALO), :] = halo[1].astype(jnp.float32)[:HALO]
        ext_n[...] = norm_rows(ext[...], ln1_ref[...])

        def some(j, carry):
            product = jnp.dot(ext_n[...], columns(g_qw, at(j)), preferred_element_type=jnp.float32)
            query[:, pl.ds(at(j), CHUNK)] = product.astype(jnp.bfloat16)
            return carry

        lax.fori_loop(0, att // CHUNK, some, 0)

    def attend(h):
        keys = kv[:, :, :, :, pl.ds(h * HD, HD)].reshape(-1, HD)
        scores = lax.dot_general(
            query[:, pl.ds(h * HD, HD)], keys, (((1,), (1,)), ((), ())), preferred_element_type=jnp.float32
        )
        position = lax.broadcasted_iota(jnp.int32, (1, scores.shape[1]), 1)
        scores = scores + jnp.where(position < limit_ref[0], 0.0, -1e30)
        peak = jnp.max(scores, axis=-1, keepdims=True)
        weights = jnp.exp2((scores - peak) * (math.log2(math.e) / math.sqrt(HD)))
        totals = jnp.sum(weights, axis=-1, keepdims=True)
        values = kv[:, :, :, :, pl.ds(att + h * HD, HD)].reshape(-1, HD)
        summed = jnp.dot(weights.astype(jnp.bfloat16), values, preferred_element_type=jnp.float32)
        context[:, pl.ds(h * HD, HD)] = (summed / totals).astype(jnp.bfloat16)

    def project():
        def some(j, carry):
            product = jnp.dot(context[...], columns(g_out, at(j)), preferred_element_type=jnp.float32)
            attended[:, pl.ds(at(j), CHUNK)] = ext[:, pl.ds(at(j), CHUNK)] + product
            return carry

        lax.fori_loop(0, width // CHUNK, some, 0)
        ext_n[...] = norm_rows(attended[...], ln2_ref[...])

    def convolve():
        def some(j, carry):
            value = jnp.dot(ext_n[...], columns(g_pw1, at(j)), preferred_element_type=jnp.float32)
            gates = jnp.dot(ext_n[...], columns(g_pw1, at(j) + width), preferred_element_type=jnp.float32)
            frame = me * local_rows - HALO + lax.broadcasted_iota(jnp.int32, value.shape, 0)
            valid = (frame >= 0) & (frame < limit_ref[0])
            gated = jnp.where(valid, value * jax.nn.sigmoid(gates), 0.0)
            gate[...] = gated.astype(jnp.bfloat16).astype(jnp.float32)
            taps = dw_ref.shape[0]
            cols = pl.ds(at(j), CHUNK)
            conv = jnp.zeros((local_rows, CHUNK), jnp.float32)
            for tap in range(taps):
                conv = conv + dw_ref[pl.ds(tap, 1), cols] * gate[pl.ds(HALO - taps // 2 + tap, local_rows), :]
            shifted = bns_ref[:, cols] * conv + bnb_ref[:, cols]
            act[:, cols] = (shifted / (1.0 + jnp.exp(-shifted))).astype(jnp.bfloat16)
            return carry

        lax.fori_loop(0, width // CHUNK, some, 0)

    def close():
        def some(j, carry):
            cols = pl.ds(at(j), CHUNK)
            product = jnp.dot(act[...], columns(g_pw2, at(j)), preferred_element_type=jnp.float32)
            result_ref[:, cols] = (attended[pl.ds(HALO, local_rows), cols] + product).astype(jnp.bfloat16)
            return carry

        lax.fori_loop(0, width // CHUNK, some, 0)

    begin(KVW)
    begin(FEAT)
    pl.when(me < last)(lambda: edge(True).start())
    pl.when(me > 0)(lambda: edge(False).start())
    pass_on(KVW, 1)
    pass_on(KVW, 2)
    pass_on(FEAT, 1)
    pass_on(KVW, 3)
    begin(QW)
    begin(OUT)
    cross(KVW)
    swap(KVW)
    pass_on(FEAT, 2)
    begin(PW1)
    arrive(KVW)
    in_round(0, key_values)
    in_round(1, key_values)
    pass_on(QW, 1)
    pass_on(OUT, 1)
    in_round(2, key_values)
    in_round(0, kv_cross)
    pass_on(FEAT, 3)
    in_round(3, key_values)
    begin(PW2)
    pass_on(QW, 2)
    pass_on(OUT, 2)
    pass_on(PW1, 1)
    in_round(1, kv_cross)
    pass_on(QW, 3)
    pass_on(OUT, 3)
    pass_on(PW1, 2)
    pass_on(PW2, 1)
    cross(QW)
    in_round(2, kv_cross)
    pass_on(PW1, 3)
    pass_on(PW2, 2)
    swap(QW)
    cross(OUT)
    in_round(3, kv_cross)
    pass_on(PW2, 3)
    swap(OUT)
    arrive(QW)
    queries()
    for source in range(ZS):
        for column in range(2):
            kv_to_core(source, column, 1 - c).wait_recv()
    cross(PW1)
    attend(0)
    cross(PW2)
    attend(1)
    swap(PW1)
    attend(2)
    swap(PW2)
    attend(3)
    arrive(OUT)
    project()
    arrive(PW1)
    convolve()
    arrive(PW2)
    close()

    for q in range(COUNT):
        finish(q)
    for source in range(ZS):
        for column in range(2):
            kv_to_core(source, column, c).wait_send()
    pl.when(me < last)(lambda: edge(True).wait_send())
    pl.when(me > 0)(lambda: edge(False).wait_send())


def per_device_kernel(
    features, valid_length, ln1_gain, w_qkv, w_out, ln2_gain, w_pw1, w_dw, bn_scale, bn_shift, w_pw2
):
    local_rows, width = features.shape
    att = w_qkv.shape[1] // 3
    wide = local_rows + 2 * HALO

    def halves(weight):
        return weight.reshape(2, weight.shape[0] // 2, weight.shape[1])

    shards = [halves(w) for w in (w_qkv, w_out, w_pw1, w_pw2)]
    grid = (ZS, 2, 2)
    bf16, f32 = jnp.bfloat16, jnp.float32
    dma = pltpu.SemaphoreType.DMA
    hbm = pl.BlockSpec(memory_space=pl.ANY)
    vmem = pl.BlockSpec(memory_space=pltpu.VMEM)
    return pl.pallas_call(
        block_kernel,
        out_shape=jax.ShapeDtypeStruct((local_rows, width), bf16),
        in_specs=[
            pl.BlockSpec(memory_space=pltpu.SMEM), hbm, vmem, hbm, hbm, vmem, hbm, vmem, vmem, vmem, hbm,
        ],
        out_specs=vmem,
        scratch_shapes=[
            pltpu.VMEM(grid + shards[0].shape[:2] + (2 * att,), bf16),
            pltpu.VMEM((ZS,) + features.shape, bf16),
            pltpu.VMEM(grid + shards[0].shape[:2] + (att,), bf16),
            pltpu.VMEM(grid + shards[1].shape, bf16),
            pltpu.VMEM(grid + shards[2].shape, bf16),
            pltpu.VMEM(grid + shards[3].shape, bf16),
            pltpu.VMEM(grid + (local_rows, 2 * att), bf16),
            pltpu.VMEM((2, PAD, width), bf16),
            pltpu.VMEM((local_rows, width), bf16),
            pltpu.VMEM((wide, width), f32),
            pltpu.VMEM((wide, width), bf16),
            pltpu.VMEM((wide, att), bf16),
            pltpu.VMEM((wide, att), bf16),
            pltpu.VMEM((wide, width), f32),
            pltpu.VMEM((wide, CHUNK), f32),
            pltpu.VMEM((local_rows, width), bf16),
            dma((COUNT,)),
        ]
        + [dma((COUNT, ZS))] * 5
        + [dma((COUNT,))] * 4
        + [dma((ZS, 2))] * 2
        + [dma((2,))] * 2,
        compiler_params=pltpu.CompilerParams(
            collective_id=0, has_side_effects=True, vmem_limit_bytes=56 * 1024 * 1024
        ),
    )(
        valid_length, features, ln1_gain[None], shards[0], shards[1], ln2_gain[None], shards[2], w_dw,
        bn_scale[None], bn_shift[None], shards[3],
    )


def per_device(*arguments):
    if lax.axis_size("frames") == 4 * ZS and lax.axis_size("groups") == 2:
        return per_device_kernel(*arguments)
    return per_device_xla(*arguments)


def solution(mesh):
    placed = (
        P(("groups", "frames"), None),
        P("groups"),
        P(),
        P("frames", None),
        P("frames", None),
        P(),
        P("frames", None),
        P(),
        P(),
        P(),
        P("frames", None),
    )
    return jax.shard_map(
        per_device,
        mesh=mesh,
        in_specs=placed,
        out_specs=P(("groups", "frames"), None),
        check_vma=False,
    )
```

```python
import functools
import math

import jax
import jax.numpy as jnp
from jax import lax
from jax.experimental import pallas as pl
from jax.experimental.pallas import tpu as pltpu
from jax.sharding import PartitionSpec as P

HEADS = 4
HD = 128


EPSILON = 1e-05


def extended(cells, sides, width):
    for axis, dim in sides:
        count = lax.axis_size(axis)
        ends = count - 1
        head = lax.slice_in_dim(cells, 0, width, axis=dim)
        tail = lax.slice_in_dim(cells, cells.shape[dim] - width, cells.shape[dim], axis=dim)
        cells = jnp.concatenate(
            [
                lax.ppermute(tail, axis, [(i, (i + 1) % count) for i in range(ends)]),
                cells,
                lax.ppermute(head, axis, [((i + 1) % count, i) for i in range(ends)]),
            ],
            axis=dim,
        )
    return cells


def layer_norm(values, gain):
    values = values.astype(jnp.float32)
    mean = jnp.mean(values, axis=-1, keepdims=True)
    centred = values - mean
    variance = jnp.mean(centred * centred, axis=-1, keepdims=True)
    return (centred * lax.rsqrt(variance + EPSILON) * gain).astype(jnp.bfloat16)


def per_device_xla(
    features, valid_length, ln1_gain, w_qkv, w_out, ln2_gain, w_pw1, w_dw, bn_scale, bn_shift, w_pw2
):
    limit = valid_length[0]
    local_rows = features.shape[0]
    width = features.shape[1]
    att_width = w_qkv.shape[1] // 3
    scale = 1.0 / math.sqrt(HD)
    tails = (
        lax.all_gather(w_out, "frames", axis=0, tiled=True),
        lax.all_gather(w_pw1, "frames", axis=0, tiled=True),
        lax.all_gather(w_pw2, "frames", axis=0, tiled=True),
    )
    full_out, full_pw1, full_pw2 = tails
    normed1 = layer_norm(features, ln1_gain)
    qkv = jnp.dot(
        normed1,
        lax.all_gather(w_qkv, "frames", axis=0, tiled=True),
        preferred_element_type=jnp.float32,
    ).astype(jnp.bfloat16)
    query_heads = qkv[:, :att_width].reshape(local_rows, HEADS, HD)
    keys = qkv[:, att_width : 2 * att_width]
    values = qkv[:, 2 * att_width :]
    maxima = jnp.full((HEADS, local_rows), -1e30, jnp.float32)
    key_rows = lax.all_gather(keys, "frames", axis=0, tiled=True)
    value_rows = lax.all_gather(values, "frames", axis=0, tiled=True)
    count = key_rows.shape[0]
    key_heads = key_rows.reshape(count, HEADS, HD)
    value_heads = value_rows.reshape(count, HEADS, HD)
    scores = (
        jnp.einsum("qhd,khd->hqk", query_heads, key_heads, preferred_element_type=jnp.float32)
        * scale
    )
    position = jnp.arange(count, dtype=jnp.int32)
    valid = (position < limit)[None, None, :]
    scores = jnp.where(valid, scores, -1e30)
    fresh = jnp.maximum(maxima, jnp.max(scores, axis=-1))
    weights = jnp.where(valid, jnp.exp(scores - fresh[..., None]), 0.0)
    totals = jnp.sum(weights, axis=-1)
    update = jnp.einsum(
        "hqk,khd->hqd",
        weights.astype(jnp.bfloat16),
        value_heads,
        preferred_element_type=jnp.float32,
    )
    summed = update
    maxima, totals, summed = (fresh, totals, summed)
    context = (
        (summed / totals[..., None])
        .transpose(1, 0, 2)
        .reshape(local_rows, att_width)
        .astype(jnp.bfloat16)
    )
    attended = features.astype(jnp.float32) + jnp.dot(
        context, full_out, preferred_element_type=jnp.float32
    )
    normed2 = layer_norm(attended, ln2_gain)
    both = jnp.dot(normed2, full_pw1, preferred_element_type=jnp.float32)
    frame_index = lax.axis_index("frames") * local_rows + jnp.arange(local_rows, dtype=jnp.int32)
    frame_valid = (frame_index < limit)[:, None]
    gated = jnp.where(frame_valid, both[:, :width] * jax.nn.sigmoid(both[:, width:]), 0.0).astype(
        jnp.bfloat16
    )
    half_window = (w_dw.shape[0] - 1) // 2
    widened = extended(gated, (("frames", 0),), half_window)
    widened = widened.astype(jnp.float32)
    conv = jnp.zeros((local_rows, width), jnp.float32)
    for tap in range(w_dw.shape[0]):
        conv = conv + w_dw[tap][None, :] * widened[tap : tap + local_rows]
    activated = jax.nn.silu(bn_scale * conv + bn_shift).astype(jnp.bfloat16)
    result = attended + jnp.dot(activated, full_pw2, preferred_element_type=jnp.float32)
    return result.astype(jnp.bfloat16)


ZS = 4
QUAD = 4
CHUNK = 256
PAD = 16
HALO = 8
BLOCK = 176
OUT, PW1, PW2 = range(3)
COUNT = 3


def norm_rows(values, gain):
    values = values.astype(jnp.float32)
    mean = jnp.mean(values, axis=-1, keepdims=True)
    centred = values - mean
    variance = jnp.mean(centred * centred, axis=-1, keepdims=True)
    return (centred * lax.rsqrt(variance + EPSILON) * gain).astype(jnp.bfloat16)


def block_kernel(
    limit_ref, feat_ref, ln1_ref, qkv_ref, out_w_ref, ln2_ref, pw1_ref, dw_ref, bns_ref, bnb_ref, pw2_ref,
    result_ref,
    stage, g_qkv, g_feat, kv, g_out, g_pw1, g_pw2, rows_n, query, ctx, ctx_out, g_ctx, context, ext, ext_n, attended,
    gate, act,
    local_sem, zp_send, zm_send, z_recv, y_send, y_recv, x_send, x_recv, c_send, c_recv,
    peer_send, peer_recv, feat_send, feat_recv, edge_send, edge_recv, chain_p, chain_m, chain_recv,
):
    twin = lax.axis_index("groups")
    me = lax.axis_index("frames")
    z, y, c = me // 4, (me // 2) % 2, me % 2
    p = me % QUAD
    width = ext.shape[1]
    local_rows = feat_ref.shape[0]
    quad_rows = QUAD * local_rows
    gathered = (g_out, g_pw1, g_pw2)
    shards = (out_w_ref, pw1_ref, pw2_ref)
    above, below = {"frames": me + 4}, {"frames": me - 4}
    partners = (QUAD // 2 * (1 - y) + c, 2 * y + 1 - c, QUAD // 2 * (1 - y) + 1 - c)
    quad = [{"frames": z * QUAD + partner} for partner in partners]
    across, core = quad[0], quad[1]
    other = {"groups": 1 - twin}

    own = [
        pltpu.make_async_copy(shards[q].at[twin], gathered[q].at[z, y, c, twin], local_sem.at[q])
        for q in range(COUNT)
    ]
    own_feat = pltpu.make_async_copy(feat_ref, g_feat.at[p + 1], local_sem.at[COUNT])
    for copy in own + [own_feat]:
        copy.start()
    for head in range(QUAD):
        for kind in range(3):
            stage[head, :, pl.ds(kind * HD, HD)] = qkv_ref[:, pl.ds((kind * QUAD + head) * HD, HD)]
    g_qkv[z, p] = stage[p]
    g_feat[0, pl.ds(local_rows - PAD, PAD), :] = jnp.zeros((PAD, width), jnp.bfloat16)
    g_feat[QUAD + 1, pl.ds(0, PAD), :] = jnp.zeros((PAD, width), jnp.bfloat16)

    barrier = pltpu.get_barrier_semaphore()

    def greet(device):
        pl.semaphore_signal(barrier, inc=1, device_id=device, device_id_type=pl.DeviceIdType.MESH)

    for device in quad:
        greet(device)
    greet(other)
    pl.when(z > 0)(lambda: greet(below))
    pl.when(z < ZS - 1)(lambda: greet(above))
    pl.semaphore_wait(barrier, 4 + jnp.where(z > 0, 1, 0) + jnp.where(z < ZS - 1, 1, 0))

    def remote(src, dst, send, recv, device):
        return pltpu.make_async_remote_copy(
            src_ref=src, dst_ref=dst, send_sem=send, recv_sem=recv,
            device_id=device, device_id_type=pl.DeviceIdType.MESH,
        )

    def along_z(q, source, up):
        part = gathered[q].at[source, y, c, twin]
        send = zp_send if up else zm_send
        return remote(part, part, send.at[q, source], z_recv.at[q, source], above if up else below)

    def along_y(q, source, column):
        part = gathered[q].at[source, column, c, twin]
        return remote(part, part, y_send.at[q, source], y_recv.at[q, source], across)

    def along_x(q, half):
        part = gathered[q].at[:, :, c, half]
        return remote(part, part, x_send.at[q], x_recv.at[q], other)

    def to_core(q, which):
        part = gathered[q].at[:, :, which]
        return remote(part, part, c_send.at[q], c_recv.at[q], core)

    def chain(i, source, up):
        part = (g_qkv, kv)[i].at[source]
        send = chain_p if up else chain_m
        return remote(part, part, send.at[i, source], chain_recv.at[i, source], above if up else below)

    def columns_to(i, sender, receiver):
        return remote(stage.at[receiver], g_qkv.at[z, sender], peer_send.at[0, i], peer_recv.at[0, i], quad[i])

    def features_to(i, block):
        part = g_feat.at[block + 1]
        return remote(part, part, feat_send.at[i], feat_recv.at[i], across if i == 0 else core)

    def context_to(i, sender, receiver):
        rows = pl.ds(pl.multiple_of(receiver * local_rows, local_rows), local_rows + 2 * HALO)
        return remote(ctx_out.at[rows], g_ctx.at[sender], peer_send.at[1, i], peer_recv.at[1, i], quad[i])

    def edge(up):
        rows = pl.ds(local_rows - PAD, PAD) if up else pl.ds(0, PAD)
        src, dst = (QUAD, 0) if up else (1, QUAD + 1)
        slot = 0 if up else 1
        return remote(
            g_feat.at[src, rows], g_feat.at[dst, rows], edge_send.at[slot], edge_recv.at[slot],
            above if up else below,
        )

    def spread(piece, item):
        pl.when(z < ZS - 1)(lambda: piece(item, z, True).start())
        pl.when(z > 0)(lambda: piece(item, z, False).start())

    def onward(piece, item, s, after=None):
        @pl.when(z >= s)
        def _():
            piece(item, z - s, True).wait_recv()
            pl.when(z < ZS - 1)(lambda: piece(item, z - s, True).start())
            if after is not None:
                after(z - s)

        @pl.when(z + s <= ZS - 1)
        def _():
            piece(item, z + s, False).wait_recv()
            pl.when(z > 0)(lambda: piece(item, z + s, False).start())
            if after is not None:
                after(z + s)

    def sent(piece, item):
        for s in range(ZS):
            pl.when((z >= s) & (z < ZS - 1))(lambda: piece(item, z - s, True).wait_send())
            if s == 0:
                pl.when(z > 0)(lambda: piece(item, z, False).wait_send())
            else:
                pl.when((z + s <= ZS - 1) & (z > 0))(lambda: piece(item, z + s, False).wait_send())

    def begin(q):
        own[q].wait()
        spread(along_z, q)
        along_y(q, z, y).start()

    def pass_on(q, s):
        onward(along_z, q, s, lambda source: along_y(q, source, y).start())

    def cross(q):
        for source in range(ZS):
            along_y(q, source, 1 - y).wait_recv()
        along_x(q, twin).start()

    def swap(q):
        along_x(q, 1 - twin).wait_recv()
        to_core(q, c).start()

    def arrive(q):
        to_core(q, 1 - c).wait_recv()

    def finish(q):
        sent(along_z, q)
        for source in range(ZS):
            along_y(q, source, y).wait_send()
        along_x(q, twin).wait_send()
        to_core(q, c).wait_send()

    def columns(ref, start):
        block = ref[:, :, :, :, :, pl.ds(start, CHUNK)]
        return block.reshape(-1, CHUNK)

    def at(j):
        return pl.multiple_of(j * CHUNK, CHUNK)

    def normalise():
        def some(i, carry):
            rows_n[pl.ds(pl.multiple_of(i * local_rows, local_rows), local_rows), :] = norm_rows(
                g_feat[i + 1], ln1_ref[...]
            )
            return carry

        lax.fori_loop(0, QUAD, some, 0)

    def key_values():
        weight = g_qkv[:, :, :, pl.ds(HD, 2 * HD)].reshape(-1, 2 * HD)
        kv[z] = jnp.dot(rows_n[...], weight, preferred_element_type=jnp.float32).astype(jnp.bfloat16)

    def queries():
        weight = g_qkv[:, :, :, pl.ds(0, HD)].reshape(-1, HD)
        query[pl.ds(0, quad_rows), :] = jnp.dot(
            rows_n[...], weight, preferred_element_type=jnp.float32
        ).astype(jnp.bfloat16)
        pl.when(z > 0)(lambda: edge(True).wait_recv())
        pl.when(z < ZS - 1)(lambda: edge(False).wait_recv())
        before = g_feat[0, pl.ds(local_rows - PAD, PAD), :].astype(jnp.float32)[PAD - HALO :]
        after = g_feat[QUAD + 1, pl.ds(0, PAD), :].astype(jnp.float32)[:HALO]
        edges = norm_rows(jnp.concatenate([before, after], axis=0), ln1_ref[...])
        query[pl.ds(quad_rows, 2 * HALO), :] = jnp.dot(
            edges, weight, preferred_element_type=jnp.float32
        ).astype(jnp.bfloat16)
        before = g_feat[p, pl.ds(local_rows - PAD, PAD), :].astype(jnp.float32)[PAD - HALO :]
        after = g_feat[p + 2, pl.ds(0, PAD), :].astype(jnp.float32)[:HALO]
        ext[pl.ds(0, HALO), :] = before
        ext[pl.ds(HALO, local_rows), :] = g_feat[p + 1].astype(jnp.float32)
        ext[pl.ds(HALO + local_rows, HALO), :] = after

    def attend(i):
        rows = pl.ds(i * BLOCK, BLOCK)
        keys = kv[:, :, pl.ds(0, HD)].reshape(-1, HD)
        scores = lax.dot_general(
            query[rows, :], keys, (((1,), (1,)), ((), ())), preferred_element_type=jnp.float32
        )
        position = lax.broadcasted_iota(jnp.int32, (1, scores.shape[1]), 1)
        scores = scores + jnp.where(position < limit_ref[0], 0.0, -1e30)
        peak = jnp.max(scores, axis=-1, keepdims=True)
        weights = jnp.exp2((scores - peak) * (math.log2(math.e) / math.sqrt(HD)))
        totals = jnp.sum(weights, axis=-1, keepdims=True)
        values = kv[:, :, pl.ds(HD, HD)].reshape(-1, HD)
        summed = jnp.dot(weights.astype(jnp.bfloat16), values, preferred_element_type=jnp.float32)
        ctx[rows, :] = summed / totals

    def share_context():
        ctx_out[...] = jnp.concatenate(
            [ctx[pl.ds(quad_rows, HALO), :], ctx[pl.ds(0, quad_rows), :], ctx[pl.ds(quad_rows + HALO, HALO), :]], axis=0
        ).astype(jnp.bfloat16)
        for i, partner in enumerate(partners):
            context_to(i, p, partner).start()
        rows = pl.ds(pl.multiple_of(p * local_rows, local_rows), local_rows + 2 * HALO)
        g_ctx[p] = ctx_out[rows, :]

    def collect_context():
        for i, partner in enumerate(partners):
            context_to(i, partner, p).wait_recv()
        for head in range(QUAD):
            context[:, pl.ds(head * HD, HD)] = g_ctx[head]

    def project():
        def some(j, carry):
            product = jnp.dot(context[...], columns(g_out, at(j)), preferred_element_type=jnp.float32)
            attended[:, pl.ds(at(j), CHUNK)] = ext[:, pl.ds(at(j), CHUNK)] + product
            return carry

        lax.fori_loop(0, width // CHUNK, some, 0)
        ext_n[...] = norm_rows(attended[...], ln2_ref[...])

    def convolve():
        def some(j, carry):
            value = jnp.dot(ext_n[...], columns(g_pw1, at(j)), preferred_element_type=jnp.float32)
            gates = jnp.dot(ext_n[...], columns(g_pw1, at(j) + width), preferred_element_type=jnp.float32)
            frame = me * local_rows - HALO + lax.broadcasted_iota(jnp.int32, value.shape, 0)
            valid = (frame >= 0) & (frame < limit_ref[0])
            gated = jnp.where(valid, value * jax.nn.sigmoid(gates), 0.0)
            gate[...] = gated.astype(jnp.bfloat16).astype(jnp.float32)
            taps = dw_ref.shape[0]
            cols = pl.ds(at(j), CHUNK)
            conv = jnp.zeros((local_rows, CHUNK), jnp.float32)
            for tap in range(taps):
                conv = conv + dw_ref[pl.ds(tap, 1), cols] * gate[pl.ds(HALO - taps // 2 + tap, local_rows), :]
            shifted = bns_ref[:, cols] * conv + bnb_ref[:, cols]
            act[:, cols] = (shifted / (1.0 + jnp.exp(-shifted))).astype(jnp.bfloat16)
            return carry

        lax.fori_loop(0, width // CHUNK, some, 0)

    def close():
        def some(j, carry):
            cols = pl.ds(at(j), CHUNK)
            product = jnp.dot(act[...], columns(g_pw2, at(j)), preferred_element_type=jnp.float32)
            result_ref[:, cols] = (attended[pl.ds(HALO, local_rows), cols] + product).astype(jnp.bfloat16)
            return carry

        lax.fori_loop(0, width // CHUNK, some, 0)

    for i, partner in enumerate(partners):
        columns_to(i, p, partner).start()
    own_feat.wait()
    features_to(0, p).start()
    features_to(1, p).start()
    begin(OUT)
    for i, partner in enumerate(partners):
        columns_to(i, partner, p).wait_recv()
    spread(chain, 0)
    features_to(0, partners[0]).wait_recv()
    features_to(2, partners[0]).start()
    begin(PW1)
    features_to(1, partners[1]).wait_recv()
    features_to(2, partners[2]).wait_recv()
    pl.when(z < ZS - 1)(lambda: edge(True).start())
    pl.when(z > 0)(lambda: edge(False).start())
    onward(chain, 0, 1)
    pass_on(OUT, 1)
    normalise()
    onward(chain, 0, 2)
    pass_on(OUT, 2)
    pass_on(PW1, 1)
    onward(chain, 0, 3)
    key_values()
    spread(chain, 1)
    begin(PW2)
    queries()
    pass_on(OUT, 3)
    pass_on(PW1, 2)
    onward(chain, 1, 1)
    cross(OUT)
    pass_on(PW1, 3)
    pass_on(PW2, 1)
    onward(chain, 1, 2)
    swap(OUT)
    pass_on(PW2, 2)
    onward(chain, 1, 3)
    attend(0)
    cross(PW1)
    pass_on(PW2, 3)
    attend(1)
    cross(PW2)
    attend(2)
    share_context()
    swap(PW1)
    swap(PW2)
    arrive(OUT)
    collect_context()
    project()
    arrive(PW1)
    convolve()
    arrive(PW2)
    close()

    for q in range(COUNT):
        finish(q)
    for i in range(2):
        sent(chain, i)
    for i, partner in enumerate(partners):
        columns_to(i, p, partner).wait_send()
        context_to(i, p, partner).wait_send()
    for i, block in enumerate((p, p, partners[0])):
        features_to(i, block).wait_send()
    pl.when(z < ZS - 1)(lambda: edge(True).wait_send())
    pl.when(z > 0)(lambda: edge(False).wait_send())


def per_device_kernel(
    features, valid_length, ln1_gain, w_qkv, w_out, ln2_gain, w_pw1, w_dw, bn_scale, bn_shift, w_pw2
):
    local_rows, width = features.shape
    att = w_qkv.shape[1] // 3
    wide = local_rows + 2 * HALO

    def halves(weight):
        return weight.reshape(2, weight.shape[0] // 2, weight.shape[1])

    shards = [halves(w) for w in (w_out, w_pw1, w_pw2)]
    grid = (ZS, 2, 2)
    bf16, f32 = jnp.bfloat16, jnp.float32
    dma = pltpu.SemaphoreType.DMA
    hbm = pl.BlockSpec(memory_space=pl.ANY)
    vmem = pl.BlockSpec(memory_space=pltpu.VMEM)
    return pl.pallas_call(
        block_kernel,
        out_shape=jax.ShapeDtypeStruct((local_rows, width), bf16),
        in_specs=[
            pl.BlockSpec(memory_space=pltpu.SMEM), hbm, vmem, vmem, hbm, vmem, hbm, vmem, vmem, vmem, hbm,
        ],
        out_specs=vmem,
        scratch_shapes=[
            pltpu.VMEM((QUAD, w_qkv.shape[0], 3 * HD), bf16),
            pltpu.VMEM((ZS, QUAD, w_qkv.shape[0], 3 * HD), bf16),
            pltpu.VMEM((QUAD + 2, local_rows, width), bf16),
            pltpu.VMEM((ZS, QUAD * local_rows, 2 * HD), bf16),
            pltpu.VMEM(grid + shards[0].shape, bf16),
            pltpu.VMEM(grid + shards[1].shape, bf16),
            pltpu.VMEM(grid + shards[2].shape, bf16),
            pltpu.VMEM((QUAD * local_rows, width), bf16),
            pltpu.VMEM((QUAD * local_rows + 2 * HALO, HD), bf16),
            pltpu.VMEM((QUAD * local_rows + 2 * HALO, HD), f32),
            pltpu.VMEM((QUAD * local_rows + 2 * HALO, HD), bf16),
            pltpu.VMEM((QUAD, wide, HD), bf16),
            pltpu.VMEM((wide, att), bf16),
            pltpu.VMEM((wide, width), f32),
            pltpu.VMEM((wide, width), bf16),
            pltpu.VMEM((wide, width), f32),
            pltpu.VMEM((wide, CHUNK), f32),
            pltpu.VMEM((local_rows, width), bf16),
            dma((COUNT + 1,)),
        ]
        + [dma((COUNT, ZS))] * 5
        + [dma((COUNT,))] * 4
        + [dma((2, 3))] * 2
        + [dma((3,))] * 2
        + [dma((2,))] * 2
        + [dma((2, ZS))] * 3,
        compiler_params=pltpu.CompilerParams(
            collective_id=0, has_side_effects=True, vmem_limit_bytes=56 * 1024 * 1024
        ),
    )(
        valid_length, features, ln1_gain[None], w_qkv, shards[0], ln2_gain[None], shards[1], w_dw,
        bn_scale[None], bn_shift[None], shards[2],
    )


def per_device(*arguments):
    if lax.axis_size("frames") == 4 * ZS and lax.axis_size("groups") == 2:
        return per_device_kernel(*arguments)
    return per_device_xla(*arguments)


def solution(mesh):
    placed = (
        P(("groups", "frames"), None),
        P("groups"),
        P(),
        P("frames", None),
        P("frames", None),
        P(),
        P("frames", None),
        P(),
        P(),
        P(),
        P("frames", None),
    )
    return jax.shard_map(
        per_device,
        mesh=mesh,
        in_specs=placed,
        out_specs=P(("groups", "frames"), None),
        check_vma=False,
    )
```

```python
import functools
import math

import jax
import jax.numpy as jnp
from jax import lax
from jax.experimental import pallas as pl
from jax.experimental.pallas import tpu as pltpu
from jax.sharding import PartitionSpec as P

HEADS = 4
HD = 128


EPSILON = 1e-05


def extended(cells, sides, width):
    for axis, dim in sides:
        count = lax.axis_size(axis)
        ends = count - 1
        head = lax.slice_in_dim(cells, 0, width, axis=dim)
        tail = lax.slice_in_dim(cells, cells.shape[dim] - width, cells.shape[dim], axis=dim)
        cells = jnp.concatenate(
            [
                lax.ppermute(tail, axis, [(i, (i + 1) % count) for i in range(ends)]),
                cells,
                lax.ppermute(head, axis, [((i + 1) % count, i) for i in range(ends)]),
            ],
            axis=dim,
        )
    return cells


def layer_norm(values, gain):
    values = values.astype(jnp.float32)
    mean = jnp.mean(values, axis=-1, keepdims=True)
    centred = values - mean
    variance = jnp.mean(centred * centred, axis=-1, keepdims=True)
    return (centred * lax.rsqrt(variance + EPSILON) * gain).astype(jnp.bfloat16)


def per_device_xla(
    features, valid_length, ln1_gain, w_qkv, w_out, ln2_gain, w_pw1, w_dw, bn_scale, bn_shift, w_pw2
):
    limit = valid_length[0]
    local_rows = features.shape[0]
    width = features.shape[1]
    att_width = w_qkv.shape[1] // 3
    scale = 1.0 / math.sqrt(HD)
    tails = (
        lax.all_gather(w_out, "frames", axis=0, tiled=True),
        lax.all_gather(w_pw1, "frames", axis=0, tiled=True),
        lax.all_gather(w_pw2, "frames", axis=0, tiled=True),
    )
    full_out, full_pw1, full_pw2 = tails
    normed1 = layer_norm(features, ln1_gain)
    qkv = jnp.dot(
        normed1,
        lax.all_gather(w_qkv, "frames", axis=0, tiled=True),
        preferred_element_type=jnp.float32,
    ).astype(jnp.bfloat16)
    query_heads = qkv[:, :att_width].reshape(local_rows, HEADS, HD)
    keys = qkv[:, att_width : 2 * att_width]
    values = qkv[:, 2 * att_width :]
    maxima = jnp.full((HEADS, local_rows), -1e30, jnp.float32)
    key_rows = lax.all_gather(keys, "frames", axis=0, tiled=True)
    value_rows = lax.all_gather(values, "frames", axis=0, tiled=True)
    count = key_rows.shape[0]
    key_heads = key_rows.reshape(count, HEADS, HD)
    value_heads = value_rows.reshape(count, HEADS, HD)
    scores = (
        jnp.einsum("qhd,khd->hqk", query_heads, key_heads, preferred_element_type=jnp.float32)
        * scale
    )
    position = jnp.arange(count, dtype=jnp.int32)
    valid = (position < limit)[None, None, :]
    scores = jnp.where(valid, scores, -1e30)
    fresh = jnp.maximum(maxima, jnp.max(scores, axis=-1))
    weights = jnp.where(valid, jnp.exp(scores - fresh[..., None]), 0.0)
    totals = jnp.sum(weights, axis=-1)
    update = jnp.einsum(
        "hqk,khd->hqd",
        weights.astype(jnp.bfloat16),
        value_heads,
        preferred_element_type=jnp.float32,
    )
    summed = update
    maxima, totals, summed = (fresh, totals, summed)
    context = (
        (summed / totals[..., None])
        .transpose(1, 0, 2)
        .reshape(local_rows, att_width)
        .astype(jnp.bfloat16)
    )
    attended = features.astype(jnp.float32) + jnp.dot(
        context, full_out, preferred_element_type=jnp.float32
    )
    normed2 = layer_norm(attended, ln2_gain)
    both = jnp.dot(normed2, full_pw1, preferred_element_type=jnp.float32)
    frame_index = lax.axis_index("frames") * local_rows + jnp.arange(local_rows, dtype=jnp.int32)
    frame_valid = (frame_index < limit)[:, None]
    gated = jnp.where(frame_valid, both[:, :width] * jax.nn.sigmoid(both[:, width:]), 0.0).astype(
        jnp.bfloat16
    )
    half_window = (w_dw.shape[0] - 1) // 2
    widened = extended(gated, (("frames", 0),), half_window)
    widened = widened.astype(jnp.float32)
    conv = jnp.zeros((local_rows, width), jnp.float32)
    for tap in range(w_dw.shape[0]):
        conv = conv + w_dw[tap][None, :] * widened[tap : tap + local_rows]
    activated = jax.nn.silu(bn_scale * conv + bn_shift).astype(jnp.bfloat16)
    result = attended + jnp.dot(activated, full_pw2, preferred_element_type=jnp.float32)
    return result.astype(jnp.bfloat16)


ZS = 4
QUAD = 4
CHUNK = 256
PAD = 16
HALO = 8
BLOCK = 176
OUT, PW1, PW2 = range(3)
COUNT = 3


def norm_rows(values, gain):
    values = values.astype(jnp.float32)
    mean = jnp.mean(values, axis=-1, keepdims=True)
    centred = values - mean
    variance = jnp.mean(centred * centred, axis=-1, keepdims=True)
    return (centred * lax.rsqrt(variance + EPSILON) * gain).astype(jnp.bfloat16)


def block_kernel(
    limit_ref, feat_ref, ln1_ref, qkv_ref, out_w_ref, ln2_ref, pw1_ref, dw_ref, bns_ref, bnb_ref, pw2_ref,
    result_ref,
    stage, g_qkv, g_feat, kv, g_out, g_pw1, g_pw2, rows_n, query, ctx, peaks, totals, ctx_out, g_ctx, context, ext, ext_n, attended,
    gate, act,
    local_sem, zp_send, zm_send, z_recv, y_send, y_recv, x_send, x_recv, c_send, c_recv,
    peer_send, peer_recv, feat_send, feat_recv, edge_send, edge_recv, chain_p, chain_m, chain_recv,
):
    twin = lax.axis_index("groups")
    me = lax.axis_index("frames")
    z, y, c = me // 4, (me // 2) % 2, me % 2
    p = me % QUAD
    width = ext.shape[1]
    local_rows = feat_ref.shape[0]
    quad_rows = QUAD * local_rows
    gathered = (g_out, g_pw1, g_pw2)
    shards = (out_w_ref, pw1_ref, pw2_ref)
    above, below = {"frames": me + 4}, {"frames": me - 4}
    partners = (QUAD // 2 * (1 - y) + c, 2 * y + 1 - c, QUAD // 2 * (1 - y) + 1 - c)
    quad = [{"frames": z * QUAD + partner} for partner in partners]
    across, core = quad[0], quad[1]
    other = {"groups": 1 - twin}

    own = [
        pltpu.make_async_copy(shards[q], gathered[q].at[z, y, c], local_sem.at[q])
        for q in range(COUNT)
    ]
    own_feat = pltpu.make_async_copy(feat_ref, g_feat.at[p + 1], local_sem.at[COUNT])
    for copy in own + [own_feat]:
        copy.start()
    for head in range(QUAD):
        for kind in range(3):
            stage[head, :, pl.ds(kind * HD, HD)] = qkv_ref[:, pl.ds((kind * QUAD + head) * HD, HD)]
    g_qkv[z, p] = stage[p]
    g_feat[0, pl.ds(local_rows - PAD, PAD), :] = jnp.zeros((PAD, width), jnp.bfloat16)
    g_feat[QUAD + 1, pl.ds(0, PAD), :] = jnp.zeros((PAD, width), jnp.bfloat16)

    barrier = pltpu.get_barrier_semaphore()

    def greet(device):
        pl.semaphore_signal(barrier, inc=1, device_id=device, device_id_type=pl.DeviceIdType.MESH)

    for device in quad:
        greet(device)
    greet(other)
    pl.when(z > 0)(lambda: greet(below))
    pl.when(z < ZS - 1)(lambda: greet(above))
    pl.semaphore_wait(barrier, 4 + jnp.where(z > 0, 1, 0) + jnp.where(z < ZS - 1, 1, 0))

    def remote(src, dst, send, recv, device):
        return pltpu.make_async_remote_copy(
            src_ref=src, dst_ref=dst, send_sem=send, recv_sem=recv,
            device_id=device, device_id_type=pl.DeviceIdType.MESH,
        )

    def along_z(q, source, up):
        part = gathered[q].at[source, y, c, twin]
        send = zp_send if up else zm_send
        return remote(part, part, send.at[q, source], z_recv.at[q, source], above if up else below)

    def along_y(q, source, column):
        part = gathered[q].at[source, column, c, twin]
        return remote(part, part, y_send.at[q, source], y_recv.at[q, source], across)

    def own_along_y(q, column):
        part = gathered[q].at[z, column, c]
        return remote(part, part, y_send.at[q, z], y_recv.at[q, z], across)

    def along_x(q, source, column, half):
        part = gathered[q].at[source, column, c, half]
        slot = (q, source, column)
        return remote(part, part, x_send.at[slot], x_recv.at[slot], other)

    def to_core(q, which, half):
        part = gathered[q].at[:, :, which, half]
        return remote(part, part, c_send.at[q, half], c_recv.at[q, half], core)

    def chain(i, source, up):
        part = (g_qkv, kv)[i].at[source]
        send = chain_p if up else chain_m
        return remote(part, part, send.at[i, source], chain_recv.at[i, source], above if up else below)

    def columns_to(i, sender, receiver):
        return remote(stage.at[receiver], g_qkv.at[z, sender], peer_send.at[0, i], peer_recv.at[0, i], quad[i])

    def features_to(i, block):
        part = g_feat.at[block + 1]
        return remote(part, part, feat_send.at[i], feat_recv.at[i], across if i == 0 else core)

    def context_to(i, sender, receiver):
        rows = pl.ds(pl.multiple_of(receiver * local_rows, local_rows), local_rows + 2 * HALO)
        return remote(ctx_out.at[rows], g_ctx.at[sender], peer_send.at[1, i], peer_recv.at[1, i], quad[i])

    def edge(up):
        rows = pl.ds(local_rows - PAD, PAD) if up else pl.ds(0, PAD)
        src, dst = (QUAD, 0) if up else (1, QUAD + 1)
        slot = 0 if up else 1
        return remote(
            g_feat.at[src, rows], g_feat.at[dst, rows], edge_send.at[slot], edge_recv.at[slot],
            above if up else below,
        )

    def spread(piece, item):
        pl.when(z < ZS - 1)(lambda: piece(item, z, True).start())
        pl.when(z > 0)(lambda: piece(item, z, False).start())

    def onward(piece, item, s, after=None):
        @pl.when(z >= s)
        def _():
            piece(item, z - s, True).wait_recv()
            pl.when(z < ZS - 1)(lambda: piece(item, z - s, True).start())
            if after is not None:
                after(z - s)

        @pl.when(z + s <= ZS - 1)
        def _():
            piece(item, z + s, False).wait_recv()
            pl.when(z > 0)(lambda: piece(item, z + s, False).start())
            if after is not None:
                after(z + s)

    def sent(piece, item):
        for s in range(ZS):
            pl.when((z >= s) & (z < ZS - 1))(lambda: piece(item, z - s, True).wait_send())
            if s == 0:
                pl.when(z > 0)(lambda: piece(item, z, False).wait_send())
            else:
                pl.when((z + s <= ZS - 1) & (z > 0))(lambda: piece(item, z + s, False).wait_send())

    def in_round(s, do):
        pl.when(z >= s)(lambda: do(z - s))
        pl.when(z + s <= ZS - 1)(lambda: do(z + s))

    def begin(q):
        own[q].wait()
        spread(along_z, q)
        own_along_y(q, y).start()

    def pass_on(q, s):
        def after(source):
            along_y(q, source, y).start()
            along_x(q, source, y, twin).start()

        onward(along_z, q, s, after)

    def cross(q, s):
        def do(source):
            along_y(q, source, 1 - y).wait_recv()
            along_x(q, source, 1 - y, twin).start()

        in_round(s, do)
        if s == ZS - 1:
            own_along_y(q, 1 - y).wait_recv()
            to_core(q, c, twin).start()

    def swap(q):
        def do(source):
            for column in range(2):
                along_x(q, source, column, 1 - twin).wait_recv()

        for s in range(1, ZS):
            in_round(s, do)
        to_core(q, c, 1 - twin).start()

    def arrive(q):
        for half in range(2):
            to_core(q, 1 - c, half).wait_recv()

    def finish(q):
        def do(source):
            along_y(q, source, y).wait_send()
            for column in range(2):
                along_x(q, source, column, twin).wait_send()

        sent(along_z, q)
        own_along_y(q, y).wait_send()
        for s in range(1, ZS):
            in_round(s, do)
        for half in range(2):
            to_core(q, c, half).wait_send()

    def columns(ref, start):
        block = ref[:, :, :, :, :, pl.ds(start, CHUNK)]
        return block.reshape(-1, CHUNK)

    def at(j):
        return pl.multiple_of(j * CHUNK, CHUNK)

    def normalise():
        def some(i, carry):
            rows_n[pl.ds(pl.multiple_of(i * local_rows, local_rows), local_rows), :] = norm_rows(
                g_feat[i + 1], ln1_ref[...]
            )
            return carry

        lax.fori_loop(0, QUAD, some, 0)

    def key_values():
        weight = g_qkv[:, :, :, pl.ds(HD, 2 * HD)].reshape(-1, 2 * HD)
        kv[z] = jnp.dot(rows_n[...], weight, preferred_element_type=jnp.float32).astype(jnp.bfloat16)

    def queries():
        weight = g_qkv[:, :, :, pl.ds(0, HD)].reshape(-1, HD)
        query[pl.ds(0, quad_rows), :] = jnp.dot(
            rows_n[...], weight, preferred_element_type=jnp.float32
        ).astype(jnp.bfloat16)
        pl.when(z > 0)(lambda: edge(True).wait_recv())
        pl.when(z < ZS - 1)(lambda: edge(False).wait_recv())
        before = g_feat[0, pl.ds(local_rows - PAD, PAD), :].astype(jnp.float32)[PAD - HALO :]
        after = g_feat[QUAD + 1, pl.ds(0, PAD), :].astype(jnp.float32)[:HALO]
        edges = norm_rows(jnp.concatenate([before, after], axis=0), ln1_ref[...])
        query[pl.ds(quad_rows, 2 * HALO), :] = jnp.dot(
            edges, weight, preferred_element_type=jnp.float32
        ).astype(jnp.bfloat16)
        before = g_feat[p, pl.ds(local_rows - PAD, PAD), :].astype(jnp.float32)[PAD - HALO :]
        after = g_feat[p + 2, pl.ds(0, PAD), :].astype(jnp.float32)[:HALO]
        ext[pl.ds(0, HALO), :] = before
        ext[pl.ds(HALO, local_rows), :] = g_feat[p + 1].astype(jnp.float32)
        ext[pl.ds(HALO + local_rows, HALO), :] = after

    nearest = z - 1 + 2 * (1 - (z + 3) // 4)
    farthest = 3 * (1 - z // 2)
    meets = (z, nearest, 6 - z - nearest - farthest, farthest)

    def attend(k):
        source = meets[k]
        keys = kv[source, :, pl.ds(0, HD)]
        values = kv[source, :, pl.ds(HD, HD)]
        factor = math.log2(math.e) / math.sqrt(HD)
        position = source * quad_rows + lax.broadcasted_iota(jnp.int32, (1, quad_rows), 1)
        bias = jnp.where(position < limit_ref[0], 0.0, -1e30)
        for i in range(query.shape[0] // BLOCK):
            rows = pl.ds(i * BLOCK, BLOCK)
            scores = lax.dot_general(
                query[rows, :], keys, (((1,), (1,)), ((), ())), preferred_element_type=jnp.float32
            ) + bias
            peak = jnp.max(scores, axis=-1, keepdims=True)
            if k > 0:
                before = peaks[rows, :][:, :1]
                peak = jnp.maximum(before, peak)
                shrink = jnp.exp2((before - peak) * factor)
            weights = jnp.exp2((scores - peak) * factor)
            total = jnp.sum(weights, axis=-1, keepdims=True)
            summed = jnp.dot(weights.astype(jnp.bfloat16), values, preferred_element_type=jnp.float32)
            if k > 0:
                total = total + totals[rows, :][:, :1] * shrink
                summed = summed + ctx[rows, :] * shrink
            if k < ZS - 1:
                peaks[rows, :] = jnp.broadcast_to(peak, (BLOCK, HD))
                totals[rows, :] = jnp.broadcast_to(total, (BLOCK, HD))
                ctx[rows, :] = summed
            else:
                ctx[rows, :] = summed / total

    def share_context():
        ctx_out[...] = jnp.concatenate(
            [ctx[pl.ds(quad_rows, HALO), :], ctx[pl.ds(0, quad_rows), :], ctx[pl.ds(quad_rows + HALO, HALO), :]], axis=0
        ).astype(jnp.bfloat16)
        for i, partner in enumerate(partners):
            context_to(i, p, partner).start()
        rows = pl.ds(pl.multiple_of(p * local_rows, local_rows), local_rows + 2 * HALO)
        g_ctx[p] = ctx_out[rows, :]

    def collect_context():
        for i, partner in enumerate(partners):
            context_to(i, partner, p).wait_recv()
        for head in range(QUAD):
            context[:, pl.ds(head * HD, HD)] = g_ctx[head]

    def project():
        def some(j, carry):
            product = jnp.dot(context[...], columns(g_out, at(j)), preferred_element_type=jnp.float32)
            attended[:, pl.ds(at(j), CHUNK)] = ext[:, pl.ds(at(j), CHUNK)] + product
            return carry

        lax.fori_loop(0, width // CHUNK, some, 0)
        ext_n[...] = norm_rows(attended[...], ln2_ref[...])

    def convolve():
        def some(j, carry):
            value = jnp.dot(ext_n[...], columns(g_pw1, at(j)), preferred_element_type=jnp.float32)
            gates = jnp.dot(ext_n[...], columns(g_pw1, at(j) + width), preferred_element_type=jnp.float32)
            frame = me * local_rows - HALO + lax.broadcasted_iota(jnp.int32, value.shape, 0)
            valid = (frame >= 0) & (frame < limit_ref[0])
            gated = jnp.where(valid, value * jax.nn.sigmoid(gates), 0.0)
            gate[...] = gated.astype(jnp.bfloat16).astype(jnp.float32)
            taps = dw_ref.shape[0]
            cols = pl.ds(at(j), CHUNK)
            conv = jnp.zeros((local_rows, CHUNK), jnp.float32)
            for tap in range(taps):
                conv = conv + dw_ref[pl.ds(tap, 1), cols] * gate[pl.ds(HALO - taps // 2 + tap, local_rows), :]
            shifted = bns_ref[:, cols] * conv + bnb_ref[:, cols]
            act[:, cols] = (shifted / (1.0 + jnp.exp(-shifted))).astype(jnp.bfloat16)
            return carry

        lax.fori_loop(0, width // CHUNK, some, 0)

    def close():
        def some(j, carry):
            cols = pl.ds(at(j), CHUNK)
            product = jnp.dot(act[...], columns(g_pw2, at(j)), preferred_element_type=jnp.float32)
            result_ref[:, cols] = (attended[pl.ds(HALO, local_rows), cols] + product).astype(jnp.bfloat16)
            return carry

        lax.fori_loop(0, width // CHUNK, some, 0)

    for i, partner in enumerate(partners):
        columns_to(i, p, partner).start()
    own_feat.wait()
    features_to(0, p).start()
    features_to(1, p).start()
    begin(PW1)
    for i, partner in enumerate(partners):
        columns_to(i, partner, p).wait_recv()
    spread(chain, 0)
    begin(OUT)
    begin(PW2)
    features_to(0, partners[0]).wait_recv()
    features_to(2, partners[0]).start()
    features_to(1, partners[1]).wait_recv()
    features_to(2, partners[2]).wait_recv()
    pl.when(z < ZS - 1)(lambda: edge(True).start())
    pl.when(z > 0)(lambda: edge(False).start())
    onward(chain, 0, 1)
    pass_on(PW1, 1)
    normalise()
    onward(chain, 0, 2)
    pass_on(OUT, 1)
    pass_on(PW2, 1)
    cross(PW1, 1)
    pass_on(PW1, 2)
    onward(chain, 0, 3)
    key_values()
    spread(chain, 1)
    queries()
    cross(OUT, 1)
    cross(PW2, 1)
    pass_on(OUT, 2)
    pass_on(PW2, 2)
    cross(PW1, 2)
    pass_on(PW1, 3)
    attend(0)
    onward(chain, 1, 1)
    pass_on(OUT, 3)
    pass_on(PW2, 3)
    attend(1)
    cross(PW1, 3)
    cross(OUT, 2)
    cross(PW2, 2)
    onward(chain, 1, 2)
    attend(2)
    cross(OUT, 3)
    cross(PW2, 3)
    onward(chain, 1, 3)
    attend(3)
    share_context()
    swap(PW1)
    swap(OUT)
    swap(PW2)
    arrive(OUT)
    collect_context()
    project()
    arrive(PW1)
    convolve()
    arrive(PW2)
    close()

    for q in range(COUNT):
        finish(q)
    for i in range(2):
        sent(chain, i)
    for i, partner in enumerate(partners):
        columns_to(i, p, partner).wait_send()
        context_to(i, p, partner).wait_send()
    for i, block in enumerate((p, p, partners[0])):
        features_to(i, block).wait_send()
    pl.when(z < ZS - 1)(lambda: edge(True).wait_send())
    pl.when(z > 0)(lambda: edge(False).wait_send())


def per_device_kernel(
    features, valid_length, ln1_gain, w_qkv, w_out, ln2_gain, w_pw1, w_dw, bn_scale, bn_shift, w_pw2
):
    local_rows, width = features.shape
    att = w_qkv.shape[1] // 3
    wide = local_rows + 2 * HALO

    def halves(weight):
        return weight.reshape(2, weight.shape[0] // 2, weight.shape[1])

    shards = [halves(w) for w in (w_out, w_pw1, w_pw2)]
    grid = (ZS, 2, 2)
    bf16, f32 = jnp.bfloat16, jnp.float32
    dma = pltpu.SemaphoreType.DMA
    hbm = pl.BlockSpec(memory_space=pl.ANY)
    vmem = pl.BlockSpec(memory_space=pltpu.VMEM)
    return pl.pallas_call(
        block_kernel,
        out_shape=jax.ShapeDtypeStruct((local_rows, width), bf16),
        in_specs=[
            pl.BlockSpec(memory_space=pltpu.SMEM), hbm, vmem, vmem, hbm, vmem, hbm, vmem, vmem, vmem, hbm,
        ],
        out_specs=vmem,
        scratch_shapes=[
            pltpu.VMEM((QUAD, w_qkv.shape[0], 3 * HD), bf16),
            pltpu.VMEM((ZS, QUAD, w_qkv.shape[0], 3 * HD), bf16),
            pltpu.VMEM((QUAD + 2, local_rows, width), bf16),
            pltpu.VMEM((ZS, QUAD * local_rows, 2 * HD), bf16),
            pltpu.VMEM(grid + shards[0].shape, bf16),
            pltpu.VMEM(grid + shards[1].shape, bf16),
            pltpu.VMEM(grid + shards[2].shape, bf16),
            pltpu.VMEM((QUAD * local_rows, width), bf16),
            pltpu.VMEM((QUAD * local_rows + 2 * HALO, HD), bf16),
            pltpu.VMEM((QUAD * local_rows + 2 * HALO, HD), f32),
            pltpu.VMEM((QUAD * local_rows + 2 * HALO, HD), f32),
            pltpu.VMEM((QUAD * local_rows + 2 * HALO, HD), f32),
            pltpu.VMEM((QUAD * local_rows + 2 * HALO, HD), bf16),
            pltpu.VMEM((QUAD, wide, HD), bf16),
            pltpu.VMEM((wide, att), bf16),
            pltpu.VMEM((wide, width), f32),
            pltpu.VMEM((wide, width), bf16),
            pltpu.VMEM((wide, width), f32),
            pltpu.VMEM((wide, CHUNK), f32),
            pltpu.VMEM((local_rows, width), bf16),
            dma((COUNT + 1,)),
        ]
        + [dma((COUNT, ZS))] * 5
        + [dma((COUNT, ZS, 2))] * 2
        + [dma((COUNT, 2))] * 2
        + [dma((2, 3))] * 2
        + [dma((3,))] * 2
        + [dma((2,))] * 2
        + [dma((2, ZS))] * 3,
        compiler_params=pltpu.CompilerParams(
            collective_id=0, has_side_effects=True, vmem_limit_bytes=56 * 1024 * 1024
        ),
    )(
        valid_length, features, ln1_gain[None], w_qkv, shards[0], ln2_gain[None], shards[1], w_dw,
        bn_scale[None], bn_shift[None], shards[2],
    )


def per_device(*arguments):
    if lax.axis_size("frames") == 4 * ZS and lax.axis_size("groups") == 2:
        return per_device_kernel(*arguments)
    return per_device_xla(*arguments)


def solution(mesh):
    placed = (
        P(("groups", "frames"), None),
        P("groups"),
        P(),
        P("frames", None),
        P("frames", None),
        P(),
        P("frames", None),
        P(),
        P(),
        P(),
        P("frames", None),
    )
    return jax.shard_map(
        per_device,
        mesh=mesh,
        in_specs=placed,
        out_specs=P(("groups", "frames"), None),
        check_vma=False,
    )
```

```python
import functools
import math

import jax
import jax.numpy as jnp
from jax import lax
from jax.experimental import pallas as pl
from jax.experimental.pallas import tpu as pltpu
from jax.sharding import PartitionSpec as P

HEADS = 4
HD = 128


EPSILON = 1e-05


def extended(cells, sides, width):
    for axis, dim in sides:
        count = lax.axis_size(axis)
        ends = count - 1
        head = lax.slice_in_dim(cells, 0, width, axis=dim)
        tail = lax.slice_in_dim(cells, cells.shape[dim] - width, cells.shape[dim], axis=dim)
        cells = jnp.concatenate(
            [
                lax.ppermute(tail, axis, [(i, (i + 1) % count) for i in range(ends)]),
                cells,
                lax.ppermute(head, axis, [((i + 1) % count, i) for i in range(ends)]),
            ],
            axis=dim,
        )
    return cells


def layer_norm(values, gain):
    values = values.astype(jnp.float32)
    mean = jnp.mean(values, axis=-1, keepdims=True)
    centred = values - mean
    variance = jnp.mean(centred * centred, axis=-1, keepdims=True)
    return (centred * lax.rsqrt(variance + EPSILON) * gain).astype(jnp.bfloat16)


def per_device_xla(
    features, valid_length, ln1_gain, w_qkv, w_out, ln2_gain, w_pw1, w_dw, bn_scale, bn_shift, w_pw2
):
    limit = valid_length[0]
    local_rows = features.shape[0]
    width = features.shape[1]
    att_width = w_qkv.shape[1] // 3
    scale = 1.0 / math.sqrt(HD)
    tails = (
        lax.all_gather(w_out, "frames", axis=0, tiled=True),
        lax.all_gather(w_pw1, "frames", axis=0, tiled=True),
        lax.all_gather(w_pw2, "frames", axis=0, tiled=True),
    )
    full_out, full_pw1, full_pw2 = tails
    normed1 = layer_norm(features, ln1_gain)
    qkv = jnp.dot(
        normed1,
        lax.all_gather(w_qkv, "frames", axis=0, tiled=True),
        preferred_element_type=jnp.float32,
    ).astype(jnp.bfloat16)
    query_heads = qkv[:, :att_width].reshape(local_rows, HEADS, HD)
    keys = qkv[:, att_width : 2 * att_width]
    values = qkv[:, 2 * att_width :]
    maxima = jnp.full((HEADS, local_rows), -1e30, jnp.float32)
    key_rows = lax.all_gather(keys, "frames", axis=0, tiled=True)
    value_rows = lax.all_gather(values, "frames", axis=0, tiled=True)
    count = key_rows.shape[0]
    key_heads = key_rows.reshape(count, HEADS, HD)
    value_heads = value_rows.reshape(count, HEADS, HD)
    scores = (
        jnp.einsum("qhd,khd->hqk", query_heads, key_heads, preferred_element_type=jnp.float32)
        * scale
    )
    position = jnp.arange(count, dtype=jnp.int32)
    valid = (position < limit)[None, None, :]
    scores = jnp.where(valid, scores, -1e30)
    fresh = jnp.maximum(maxima, jnp.max(scores, axis=-1))
    weights = jnp.where(valid, jnp.exp(scores - fresh[..., None]), 0.0)
    totals = jnp.sum(weights, axis=-1)
    update = jnp.einsum(
        "hqk,khd->hqd",
        weights.astype(jnp.bfloat16),
        value_heads,
        preferred_element_type=jnp.float32,
    )
    summed = update
    maxima, totals, summed = (fresh, totals, summed)
    context = (
        (summed / totals[..., None])
        .transpose(1, 0, 2)
        .reshape(local_rows, att_width)
        .astype(jnp.bfloat16)
    )
    attended = features.astype(jnp.float32) + jnp.dot(
        context, full_out, preferred_element_type=jnp.float32
    )
    normed2 = layer_norm(attended, ln2_gain)
    both = jnp.dot(normed2, full_pw1, preferred_element_type=jnp.float32)
    frame_index = lax.axis_index("frames") * local_rows + jnp.arange(local_rows, dtype=jnp.int32)
    frame_valid = (frame_index < limit)[:, None]
    gated = jnp.where(frame_valid, both[:, :width] * jax.nn.sigmoid(both[:, width:]), 0.0).astype(
        jnp.bfloat16
    )
    half_window = (w_dw.shape[0] - 1) // 2
    widened = extended(gated, (("frames", 0),), half_window)
    widened = widened.astype(jnp.float32)
    conv = jnp.zeros((local_rows, width), jnp.float32)
    for tap in range(w_dw.shape[0]):
        conv = conv + w_dw[tap][None, :] * widened[tap : tap + local_rows]
    activated = jax.nn.silu(bn_scale * conv + bn_shift).astype(jnp.bfloat16)
    result = attended + jnp.dot(activated, full_pw2, preferred_element_type=jnp.float32)
    return result.astype(jnp.bfloat16)


ZS = 4
QUAD = 4
CHUNK = 256
PAD = 16
HALO = 8
BLOCK = 176
OUT, PW1, PW2 = range(3)
COUNT = 3


def norm_rows(values, gain):
    values = values.astype(jnp.float32)
    mean = jnp.mean(values, axis=-1, keepdims=True)
    centred = values - mean
    variance = jnp.mean(centred * centred, axis=-1, keepdims=True)
    return (centred * lax.rsqrt(variance + EPSILON) * gain).astype(jnp.bfloat16)


def block_kernel(
    limit_ref, feat_ref, ln1_ref, qkv_ref, out_w_ref, ln2_ref, pw1_ref, dw_ref, bns_ref, bnb_ref, pw2_ref,
    result_ref,
    stage, g_qkv, g_feat, kv, g_out, g_pw1, g_pw2, rows_n, query, ctx, peaks, totals, ctx_out, g_ctx, context, ext, ext_n, attended,
    gate, act,
    local_sem, zp_send, zm_send, z_recv, y_send, y_recv, x_send, x_recv, c_send, c_recv,
    peer_send, peer_recv, feat_send, feat_recv, edge_send, edge_recv, chain_p, chain_m, chain_recv,
    half_send, half_recv,
):
    twin = lax.axis_index("groups")
    me = lax.axis_index("frames")
    z, y, c = me // 4, (me // 2) % 2, me % 2
    p = me % QUAD
    width = ext.shape[1]
    local_rows = feat_ref.shape[0]
    quad_rows = QUAD * local_rows
    gathered = (g_out, g_pw1, g_pw2)
    shards = (out_w_ref, pw1_ref, pw2_ref)
    above, below = {"frames": me + 4}, {"frames": me - 4}
    partners = (QUAD // 2 * (1 - y) + c, 2 * y + 1 - c, QUAD // 2 * (1 - y) + 1 - c)
    quad = [{"frames": z * QUAD + partner} for partner in partners]
    across, core = quad[0], quad[1]
    other = {"groups": 1 - twin}

    own = [
        pltpu.make_async_copy(shards[q], gathered[q].at[z, y, c], local_sem.at[q])
        for q in range(COUNT)
    ]
    own_feat = pltpu.make_async_copy(feat_ref, g_feat.at[p + 1], local_sem.at[COUNT])
    for copy in own + [own_feat]:
        copy.start()
    for head in range(QUAD):
        for kind in range(3):
            stage[head, :, pl.ds(kind * HD, HD)] = qkv_ref[:, pl.ds((kind * QUAD + head) * HD, HD)]
    g_qkv[z, y, c] = stage[p]
    g_feat[0, pl.ds(local_rows - PAD, PAD), :] = jnp.zeros((PAD, width), jnp.bfloat16)
    g_feat[QUAD + 1, pl.ds(0, PAD), :] = jnp.zeros((PAD, width), jnp.bfloat16)

    barrier = pltpu.get_barrier_semaphore()

    def greet(device):
        pl.semaphore_signal(barrier, inc=1, device_id=device, device_id_type=pl.DeviceIdType.MESH)

    for device in quad:
        greet(device)
    greet(other)
    pl.when(z > 0)(lambda: greet(below))
    pl.when(z < ZS - 1)(lambda: greet(above))
    pl.semaphore_wait(barrier, 4 + jnp.where(z > 0, 1, 0) + jnp.where(z < ZS - 1, 1, 0))

    def remote(src, dst, send, recv, device):
        return pltpu.make_async_remote_copy(
            src_ref=src, dst_ref=dst, send_sem=send, recv_sem=recv,
            device_id=device, device_id_type=pl.DeviceIdType.MESH,
        )

    def along_z(q, source, up):
        part = gathered[q].at[source, y, c, twin]
        send = zp_send if up else zm_send
        return remote(part, part, send.at[q, source], z_recv.at[q, source], above if up else below)

    def along_y(q, source, column):
        part = gathered[q].at[source, column, c, twin]
        return remote(part, part, y_send.at[q, source], y_recv.at[q, source], across)

    def own_along_y(q, column):
        part = gathered[q].at[z, column, c]
        return remote(part, part, y_send.at[q, z], y_recv.at[q, z], across)

    def along_x(q, source, column, half):
        part = gathered[q].at[source, column, c, half]
        slot = (q, source, column)
        return remote(part, part, x_send.at[slot], x_recv.at[slot], other)

    def to_core(q, which, half):
        part = gathered[q].at[:, :, which, half]
        return remote(part, part, c_send.at[q, half], c_recv.at[q, half], core)

    def chain(i, source, up):
        part = kv.at[source] if i else g_qkv.at[source, twin]
        send = chain_p if up else chain_m
        return remote(part, part, send.at[i, source], chain_recv.at[i, source], above if up else below)

    def columns_across(source, half):
        part = g_qkv.at[source, half]
        return remote(part, part, half_send.at[source], half_recv.at[source], other)

    def columns_to(i, sender, receiver):
        return remote(stage.at[receiver], g_qkv.at[z, sender // 2, sender % 2], peer_send.at[0, i], peer_recv.at[0, i], quad[i])

    def features_to(i, block):
        part = g_feat.at[block + 1]
        return remote(part, part, feat_send.at[i], feat_recv.at[i], across if i == 0 else core)

    def context_to(i, sender, receiver):
        rows = pl.ds(pl.multiple_of(receiver * local_rows, local_rows), local_rows + 2 * HALO)
        return remote(ctx_out.at[rows], g_ctx.at[sender], peer_send.at[1, i], peer_recv.at[1, i], quad[i])

    def edge(up):
        rows = pl.ds(local_rows - PAD, PAD) if up else pl.ds(0, PAD)
        src, dst = (QUAD, 0) if up else (1, QUAD + 1)
        slot = 0 if up else 1
        return remote(
            g_feat.at[src, rows], g_feat.at[dst, rows], edge_send.at[slot], edge_recv.at[slot],
            above if up else below,
        )

    def spread(piece, item):
        pl.when(z < ZS - 1)(lambda: piece(item, z, True).start())
        pl.when(z > 0)(lambda: piece(item, z, False).start())

    def onward(piece, item, s, after=None):
        @pl.when(z >= s)
        def _():
            piece(item, z - s, True).wait_recv()
            pl.when(z < ZS - 1)(lambda: piece(item, z - s, True).start())
            if after is not None:
                after(z - s)

        @pl.when(z + s <= ZS - 1)
        def _():
            piece(item, z + s, False).wait_recv()
            pl.when(z > 0)(lambda: piece(item, z + s, False).start())
            if after is not None:
                after(z + s)

    def sent(piece, item):
        for s in range(ZS):
            pl.when((z >= s) & (z < ZS - 1))(lambda: piece(item, z - s, True).wait_send())
            if s == 0:
                pl.when(z > 0)(lambda: piece(item, z, False).wait_send())
            else:
                pl.when((z + s <= ZS - 1) & (z > 0))(lambda: piece(item, z + s, False).wait_send())

    def in_round(s, do):
        pl.when(z >= s)(lambda: do(z - s))
        pl.when(z + s <= ZS - 1)(lambda: do(z + s))

    def begin(q):
        own[q].wait()
        spread(along_z, q)

    def begin_across(q):
        own_along_y(q, y).start()

    def columns_on(s):
        onward(chain, 0, s, lambda source: columns_across(source, twin).start())

    def pass_on(q, s):
        def after(source):
            along_y(q, source, y).start()
            along_x(q, source, y, twin).start()

        onward(along_z, q, s, after)

    def cross(q, s):
        def do(source):
            along_y(q, source, 1 - y).wait_recv()
            along_x(q, source, 1 - y, twin).start()

        in_round(s, do)
        if s == ZS - 1:
            own_along_y(q, 1 - y).wait_recv()
            to_core(q, c, twin).start()

    def swap(q):
        def do(source):
            for column in range(2):
                along_x(q, source, column, 1 - twin).wait_recv()

        for s in range(1, ZS):
            in_round(s, do)
        to_core(q, c, 1 - twin).start()

    def arrive(q):
        for half in range(2):
            to_core(q, 1 - c, half).wait_recv()

    def finish(q):
        def do(source):
            along_y(q, source, y).wait_send()
            for column in range(2):
                along_x(q, source, column, twin).wait_send()

        sent(along_z, q)
        own_along_y(q, y).wait_send()
        for s in range(1, ZS):
            in_round(s, do)
        for half in range(2):
            to_core(q, c, half).wait_send()

    def columns(ref, start):
        block = ref[:, :, :, :, :, pl.ds(start, CHUNK)]
        return block.reshape(-1, CHUNK)

    def at(j):
        return pl.multiple_of(j * CHUNK, CHUNK)

    def normalise():
        def some(i, carry):
            rows_n[pl.ds(pl.multiple_of(i * local_rows, local_rows), local_rows), :] = norm_rows(
                g_feat[i + 1], ln1_ref[...]
            )
            return carry

        lax.fori_loop(0, QUAD, some, 0)

    def key_values():
        weight = g_qkv[:, :, :, :, pl.ds(HD, 2 * HD)].reshape(-1, 2 * HD)
        kv[z] = jnp.dot(rows_n[...], weight, preferred_element_type=jnp.float32).astype(jnp.bfloat16)

    def queries():
        weight = g_qkv[:, :, :, :, pl.ds(0, HD)].reshape(-1, HD)
        query[pl.ds(0, quad_rows), :] = jnp.dot(
            rows_n[...], weight, preferred_element_type=jnp.float32
        ).astype(jnp.bfloat16)
        pl.when(z > 0)(lambda: edge(True).wait_recv())
        pl.when(z < ZS - 1)(lambda: edge(False).wait_recv())
        before = g_feat[0, pl.ds(local_rows - PAD, PAD), :].astype(jnp.float32)[PAD - HALO :]
        after = g_feat[QUAD + 1, pl.ds(0, PAD), :].astype(jnp.float32)[:HALO]
        edges = norm_rows(jnp.concatenate([before, after], axis=0), ln1_ref[...])
        query[pl.ds(quad_rows, 2 * HALO), :] = jnp.dot(
            edges, weight, preferred_element_type=jnp.float32
        ).astype(jnp.bfloat16)
        before = g_feat[p, pl.ds(local_rows - PAD, PAD), :].astype(jnp.float32)[PAD - HALO :]
        after = g_feat[p + 2, pl.ds(0, PAD), :].astype(jnp.float32)[:HALO]
        ext[pl.ds(0, HALO), :] = before
        ext[pl.ds(HALO, local_rows), :] = g_feat[p + 1].astype(jnp.float32)
        ext[pl.ds(HALO + local_rows, HALO), :] = after

    nearest = z - 1 + 2 * (1 - (z + 3) // 4)
    farthest = 3 * (1 - z // 2)
    meets = (z, nearest, 6 - z - nearest - farthest, farthest)

    def attend(k):
        source = meets[k]
        keys = kv[source, :, pl.ds(0, HD)]
        values = kv[source, :, pl.ds(HD, HD)]
        factor = math.log2(math.e) / math.sqrt(HD)
        position = source * quad_rows + lax.broadcasted_iota(jnp.int32, (1, quad_rows), 1)
        bias = jnp.where(position < limit_ref[0], 0.0, -1e30)
        for i in range(query.shape[0] // BLOCK):
            rows = pl.ds(i * BLOCK, BLOCK)
            scores = lax.dot_general(
                query[rows, :], keys, (((1,), (1,)), ((), ())), preferred_element_type=jnp.float32
            ) + bias
            peak = jnp.max(scores, axis=-1, keepdims=True)
            if k > 0:
                before = peaks[rows, :][:, :1]
                peak = jnp.maximum(before, peak)
                shrink = jnp.exp2((before - peak) * factor)
            weights = jnp.exp2((scores - peak) * factor)
            total = jnp.sum(weights, axis=-1, keepdims=True)
            summed = jnp.dot(weights.astype(jnp.bfloat16), values, preferred_element_type=jnp.float32)
            if k > 0:
                total = total + totals[rows, :][:, :1] * shrink
                summed = summed + ctx[rows, :] * shrink
            if k < ZS - 1:
                peaks[rows, :] = jnp.broadcast_to(peak, (BLOCK, HD))
                totals[rows, :] = jnp.broadcast_to(total, (BLOCK, HD))
                ctx[rows, :] = summed
            else:
                ctx[rows, :] = summed / total

    def share_context():
        ctx_out[...] = jnp.concatenate(
            [ctx[pl.ds(quad_rows, HALO), :], ctx[pl.ds(0, quad_rows), :], ctx[pl.ds(quad_rows + HALO, HALO), :]], axis=0
        ).astype(jnp.bfloat16)
        for i, partner in enumerate(partners):
            context_to(i, p, partner).start()
        rows = pl.ds(pl.multiple_of(p * local_rows, local_rows), local_rows + 2 * HALO)
        g_ctx[p] = ctx_out[rows, :]

    def collect_context():
        for i, partner in enumerate(partners):
            context_to(i, partner, p).wait_recv()
        for head in range(QUAD):
            context[:, pl.ds(head * HD, HD)] = g_ctx[head]

    def project():
        def some(j, carry):
            product = jnp.dot(context[...], columns(g_out, at(j)), preferred_element_type=jnp.float32)
            attended[:, pl.ds(at(j), CHUNK)] = ext[:, pl.ds(at(j), CHUNK)] + product
            return carry

        lax.fori_loop(0, width // CHUNK, some, 0, unroll=True)
        ext_n[...] = norm_rows(attended[...], ln2_ref[...])

    def convolve():
        def some(j, carry):
            value = jnp.dot(ext_n[...], columns(g_pw1, at(j)), preferred_element_type=jnp.float32)
            gates = jnp.dot(ext_n[...], columns(g_pw1, at(j) + width), preferred_element_type=jnp.float32)
            frame = me * local_rows - HALO + lax.broadcasted_iota(jnp.int32, value.shape, 0)
            valid = (frame >= 0) & (frame < limit_ref[0])
            gated = jnp.where(valid, value * jax.nn.sigmoid(gates), 0.0)
            gate[...] = gated.astype(jnp.bfloat16).astype(jnp.float32)
            taps = dw_ref.shape[0]
            cols = pl.ds(at(j), CHUNK)
            conv = jnp.zeros((local_rows, CHUNK), jnp.float32)
            for tap in range(taps):
                conv = conv + dw_ref[pl.ds(tap, 1), cols] * gate[pl.ds(HALO - taps // 2 + tap, local_rows), :]
            shifted = bns_ref[:, cols] * conv + bnb_ref[:, cols]
            act[:, cols] = (shifted / (1.0 + jnp.exp(-shifted))).astype(jnp.bfloat16)
            return carry

        lax.fori_loop(0, width // CHUNK, some, 0, unroll=True)

    def close():
        def some(j, carry):
            cols = pl.ds(at(j), CHUNK)
            product = jnp.dot(act[...], columns(g_pw2, at(j)), preferred_element_type=jnp.float32)
            result_ref[:, cols] = (attended[pl.ds(HALO, local_rows), cols] + product).astype(jnp.bfloat16)
            return carry

        lax.fori_loop(0, width // CHUNK, some, 0, unroll=True)

    for i, partner in enumerate(partners):
        columns_to(i, p, partner).start()
    own_feat.wait()
    features_to(0, p).start()
    features_to(1, p).start()
    begin(PW1)
    for i, partner in enumerate(partners):
        columns_to(i, partner, p).wait_recv()
    spread(chain, 0)
    begin(OUT)
    begin(PW2)
    features_to(0, partners[0]).wait_recv()
    features_to(2, partners[0]).start()
    for q in (PW1, OUT, PW2):
        begin_across(q)
    columns_on(1)
    features_to(1, partners[1]).wait_recv()
    features_to(2, partners[2]).wait_recv()
    pl.when(z < ZS - 1)(lambda: edge(True).start())
    pl.when(z > 0)(lambda: edge(False).start())
    pass_on(PW1, 1)
    columns_on(2)
    normalise()
    columns_on(3)
    pass_on(OUT, 1)
    pass_on(PW2, 1)
    for s in range(1, ZS):
        in_round(s, lambda source: columns_across(source, 1 - twin).wait_recv())
    key_values()
    spread(chain, 1)
    queries()
    pass_on(PW1, 2)
    cross(PW1, 1)
    pass_on(OUT, 2)
    pass_on(PW2, 2)
    cross(OUT, 1)
    cross(PW2, 1)
    attend(0)
    onward(chain, 1, 1)
    pass_on(PW1, 3)
    pass_on(OUT, 3)
    pass_on(PW2, 3)
    cross(PW1, 2)
    attend(1)
    onward(chain, 1, 2)
    cross(OUT, 2)
    cross(PW2, 2)
    cross(PW1, 3)
    attend(2)
    cross(OUT, 3)
    cross(PW2, 3)
    onward(chain, 1, 3)
    swap(PW1)
    attend(3)
    share_context()
    swap(OUT)
    swap(PW2)
    arrive(OUT)
    collect_context()
    project()
    arrive(PW1)
    convolve()
    arrive(PW2)
    close()

    for q in range(COUNT):
        finish(q)
    for i in range(2):
        sent(chain, i)
    for s in range(1, ZS):
        in_round(s, lambda source: columns_across(source, twin).wait_send())
    for i, partner in enumerate(partners):
        columns_to(i, p, partner).wait_send()
        context_to(i, p, partner).wait_send()
    for i, block in enumerate((p, p, partners[0])):
        features_to(i, block).wait_send()
    pl.when(z < ZS - 1)(lambda: edge(True).wait_send())
    pl.when(z > 0)(lambda: edge(False).wait_send())


def per_device_kernel(
    features, valid_length, ln1_gain, w_qkv, w_out, ln2_gain, w_pw1, w_dw, bn_scale, bn_shift, w_pw2
):
    local_rows, width = features.shape
    att = w_qkv.shape[1] // 3
    wide = local_rows + 2 * HALO

    def halves(weight):
        return weight.reshape(2, weight.shape[0] // 2, weight.shape[1])

    shards = [halves(w) for w in (w_out, w_pw1, w_pw2)]
    grid = (ZS, 2, 2)
    bf16, f32 = jnp.bfloat16, jnp.float32
    dma = pltpu.SemaphoreType.DMA
    hbm = pl.BlockSpec(memory_space=pl.ANY)
    vmem = pl.BlockSpec(memory_space=pltpu.VMEM)
    return pl.pallas_call(
        block_kernel,
        out_shape=jax.ShapeDtypeStruct((local_rows, width), bf16),
        in_specs=[
            pl.BlockSpec(memory_space=pltpu.SMEM), hbm, vmem, vmem, hbm, vmem, hbm, vmem, vmem, vmem, hbm,
        ],
        out_specs=vmem,
        scratch_shapes=[
            pltpu.VMEM((QUAD, w_qkv.shape[0], 3 * HD), bf16),
            pltpu.VMEM((ZS, 2, 2, w_qkv.shape[0], 3 * HD), bf16),
            pltpu.VMEM((QUAD + 2, local_rows, width), bf16),
            pltpu.VMEM((ZS, QUAD * local_rows, 2 * HD), bf16),
            pltpu.VMEM(grid + shards[0].shape, bf16),
            pltpu.VMEM(grid + shards[1].shape, bf16),
            pltpu.VMEM(grid + shards[2].shape, bf16),
            pltpu.VMEM((QUAD * local_rows, width), bf16),
            pltpu.VMEM((QUAD * local_rows + 2 * HALO, HD), bf16),
            pltpu.VMEM((QUAD * local_rows + 2 * HALO, HD), f32),
            pltpu.VMEM((QUAD * local_rows + 2 * HALO, HD), f32),
            pltpu.VMEM((QUAD * local_rows + 2 * HALO, HD), f32),
            pltpu.VMEM((QUAD * local_rows + 2 * HALO, HD), bf16),
            pltpu.VMEM((QUAD, wide, HD), bf16),
            pltpu.VMEM((wide, att), bf16),
            pltpu.VMEM((wide, width), f32),
            pltpu.VMEM((wide, width), bf16),
            pltpu.VMEM((wide, width), f32),
            pltpu.VMEM((wide, CHUNK), f32),
            pltpu.VMEM((local_rows, width), bf16),
            dma((COUNT + 1,)),
        ]
        + [dma((COUNT, ZS))] * 5
        + [dma((COUNT, ZS, 2))] * 2
        + [dma((COUNT, 2))] * 2
        + [dma((2, 3))] * 2
        + [dma((3,))] * 2
        + [dma((2,))] * 2
        + [dma((2, ZS))] * 3
        + [dma((ZS,))] * 2,
        compiler_params=pltpu.CompilerParams(
            collective_id=0, has_side_effects=True, vmem_limit_bytes=56 * 1024 * 1024
        ),
    )(
        valid_length, features, ln1_gain[None], w_qkv, shards[0], ln2_gain[None], shards[1], w_dw,
        bn_scale[None], bn_shift[None], shards[2],
    )


def per_device(*arguments):
    if lax.axis_size("frames") == 4 * ZS and lax.axis_size("groups") == 2:
        return per_device_kernel(*arguments)
    return per_device_xla(*arguments)


def solution(mesh):
    placed = (
        P(("groups", "frames"), None),
        P("groups"),
        P(),
        P("frames", None),
        P("frames", None),
        P(),
        P("frames", None),
        P(),
        P(),
        P(),
        P("frames", None),
    )
    return jax.shard_map(
        per_device,
        mesh=mesh,
        in_specs=placed,
        out_specs=P(("groups", "frames"), None),
        check_vma=False,
    )
```

```python
import functools
import math

import jax
import jax.numpy as jnp
from jax import lax
from jax.experimental import pallas as pl
from jax.experimental.pallas import tpu as pltpu
from jax.sharding import PartitionSpec as P

HEADS = 4
HD = 128


EPSILON = 1e-05


def extended(cells, sides, width):
    for axis, dim in sides:
        count = lax.axis_size(axis)
        ends = count - 1
        head = lax.slice_in_dim(cells, 0, width, axis=dim)
        tail = lax.slice_in_dim(cells, cells.shape[dim] - width, cells.shape[dim], axis=dim)
        cells = jnp.concatenate(
            [
                lax.ppermute(tail, axis, [(i, (i + 1) % count) for i in range(ends)]),
                cells,
                lax.ppermute(head, axis, [((i + 1) % count, i) for i in range(ends)]),
            ],
            axis=dim,
        )
    return cells


def layer_norm(values, gain):
    values = values.astype(jnp.float32)
    mean = jnp.mean(values, axis=-1, keepdims=True)
    centred = values - mean
    variance = jnp.mean(centred * centred, axis=-1, keepdims=True)
    return (centred * lax.rsqrt(variance + EPSILON) * gain).astype(jnp.bfloat16)


def per_device_xla(
    features, valid_length, ln1_gain, w_qkv, w_out, ln2_gain, w_pw1, w_dw, bn_scale, bn_shift, w_pw2
):
    limit = valid_length[0]
    local_rows = features.shape[0]
    width = features.shape[1]
    att_width = w_qkv.shape[1] // 3
    scale = 1.0 / math.sqrt(HD)
    tails = (
        lax.all_gather(w_out, "frames", axis=0, tiled=True),
        lax.all_gather(w_pw1, "frames", axis=0, tiled=True),
        lax.all_gather(w_pw2, "frames", axis=0, tiled=True),
    )
    full_out, full_pw1, full_pw2 = tails
    normed1 = layer_norm(features, ln1_gain)
    qkv = jnp.dot(
        normed1,
        lax.all_gather(w_qkv, "frames", axis=0, tiled=True),
        preferred_element_type=jnp.float32,
    ).astype(jnp.bfloat16)
    query_heads = qkv[:, :att_width].reshape(local_rows, HEADS, HD)
    keys = qkv[:, att_width : 2 * att_width]
    values = qkv[:, 2 * att_width :]
    maxima = jnp.full((HEADS, local_rows), -1e30, jnp.float32)
    key_rows = lax.all_gather(keys, "frames", axis=0, tiled=True)
    value_rows = lax.all_gather(values, "frames", axis=0, tiled=True)
    count = key_rows.shape[0]
    key_heads = key_rows.reshape(count, HEADS, HD)
    value_heads = value_rows.reshape(count, HEADS, HD)
    scores = (
        jnp.einsum("qhd,khd->hqk", query_heads, key_heads, preferred_element_type=jnp.float32)
        * scale
    )
    position = jnp.arange(count, dtype=jnp.int32)
    valid = (position < limit)[None, None, :]
    scores = jnp.where(valid, scores, -1e30)
    fresh = jnp.maximum(maxima, jnp.max(scores, axis=-1))
    weights = jnp.where(valid, jnp.exp(scores - fresh[..., None]), 0.0)
    totals = jnp.sum(weights, axis=-1)
    update = jnp.einsum(
        "hqk,khd->hqd",
        weights.astype(jnp.bfloat16),
        value_heads,
        preferred_element_type=jnp.float32,
    )
    summed = update
    maxima, totals, summed = (fresh, totals, summed)
    context = (
        (summed / totals[..., None])
        .transpose(1, 0, 2)
        .reshape(local_rows, att_width)
        .astype(jnp.bfloat16)
    )
    attended = features.astype(jnp.float32) + jnp.dot(
        context, full_out, preferred_element_type=jnp.float32
    )
    normed2 = layer_norm(attended, ln2_gain)
    both = jnp.dot(normed2, full_pw1, preferred_element_type=jnp.float32)
    frame_index = lax.axis_index("frames") * local_rows + jnp.arange(local_rows, dtype=jnp.int32)
    frame_valid = (frame_index < limit)[:, None]
    gated = jnp.where(frame_valid, both[:, :width] * jax.nn.sigmoid(both[:, width:]), 0.0).astype(
        jnp.bfloat16
    )
    half_window = (w_dw.shape[0] - 1) // 2
    widened = extended(gated, (("frames", 0),), half_window)
    widened = widened.astype(jnp.float32)
    conv = jnp.zeros((local_rows, width), jnp.float32)
    for tap in range(w_dw.shape[0]):
        conv = conv + w_dw[tap][None, :] * widened[tap : tap + local_rows]
    activated = jax.nn.silu(bn_scale * conv + bn_shift).astype(jnp.bfloat16)
    result = attended + jnp.dot(activated, full_pw2, preferred_element_type=jnp.float32)
    return result.astype(jnp.bfloat16)


ZS = 4
QUAD = 4
CHUNK = 256
PAD = 16
HALO = 8
BLOCK = 176
OUT, PW1, PW2 = range(3)
COUNT = 3


def norm_rows(values, gain):
    values = values.astype(jnp.float32)
    mean = jnp.mean(values, axis=-1, keepdims=True)
    centred = values - mean
    variance = jnp.mean(centred * centred, axis=-1, keepdims=True)
    return (centred * lax.rsqrt(variance + EPSILON) * gain).astype(jnp.bfloat16)


def block_kernel(
    limit_ref, feat_ref, ln1_ref, qkv_ref, out_w_ref, ln2_ref, pw1_ref, dw_ref, bns_ref, bnb_ref, pw2_ref,
    result_ref,
    stage, g_qkv, g_feat, kv, g_out, g_pw1, g_pw2, rows_n, query, ctx, peaks, totals, ctx_out, g_ctx, context, ext, ext_n, attended,
    gate, act,
    local_sem, zp_send, zm_send, z_recv, y_send, y_recv, x_send, x_recv, c_send, c_recv,
    peer_send, peer_recv, feat_send, feat_recv, edge_send, edge_recv, chain_p, chain_m, chain_recv,
    half_send, half_recv,
):
    twin = lax.axis_index("groups")
    me = lax.axis_index("frames")
    z, y, c = me // 4, (me // 2) % 2, me % 2
    p = me % QUAD
    width = ext.shape[1]
    local_rows = feat_ref.shape[0]
    quad_rows = QUAD * local_rows
    gathered = (g_out, g_pw1, g_pw2)
    shards = (out_w_ref, pw1_ref, pw2_ref)
    above, below = {"frames": me + 4}, {"frames": me - 4}
    partners = (QUAD // 2 * (1 - y) + c, 2 * y + 1 - c, QUAD // 2 * (1 - y) + 1 - c)
    quad = [{"frames": z * QUAD + partner} for partner in partners]
    across, core = quad[0], quad[1]
    other = {"groups": 1 - twin}

    own = [
        pltpu.make_async_copy(shards[q], gathered[q].at[z, y, c], local_sem.at[q])
        for q in range(COUNT)
    ]
    own_feat = pltpu.make_async_copy(feat_ref, g_feat.at[p + 1], local_sem.at[COUNT])
    for copy in own + [own_feat]:
        copy.start()
    for head in range(QUAD):
        for kind in range(3):
            stage[head, :, pl.ds(kind * HD, HD)] = qkv_ref[:, pl.ds((kind * QUAD + head) * HD, HD)]
    g_qkv[z, y, c] = stage[p]
    g_feat[0, pl.ds(local_rows - PAD, PAD), :] = jnp.zeros((PAD, width), jnp.bfloat16)
    g_feat[QUAD + 1, pl.ds(0, PAD), :] = jnp.zeros((PAD, width), jnp.bfloat16)

    barrier = pltpu.get_barrier_semaphore()

    def greet(device):
        pl.semaphore_signal(barrier, inc=1, device_id=device, device_id_type=pl.DeviceIdType.MESH)

    for device in quad:
        greet(device)
    greet(other)
    pl.when(z > 0)(lambda: greet(below))
    pl.when(z < ZS - 1)(lambda: greet(above))
    pl.semaphore_wait(barrier, 4 + jnp.where(z > 0, 1, 0) + jnp.where(z < ZS - 1, 1, 0))

    def remote(src, dst, send, recv, device):
        return pltpu.make_async_remote_copy(
            src_ref=src, dst_ref=dst, send_sem=send, recv_sem=recv,
            device_id=device, device_id_type=pl.DeviceIdType.MESH,
        )

    def along_z(q, source, up):
        part = gathered[q].at[source, y, c, twin]
        send = zp_send if up else zm_send
        return remote(part, part, send.at[q, source], z_recv.at[q, source], above if up else below)

    def along_y(q, source, column):
        part = gathered[q].at[source, column, c, twin]
        return remote(part, part, y_send.at[q, source], y_recv.at[q, source], across)

    def own_along_y(q, column):
        part = gathered[q].at[z, column, c]
        return remote(part, part, y_send.at[q, z], y_recv.at[q, z], across)

    def along_x(q, source, column, half):
        part = gathered[q].at[source, column, c, half]
        slot = (q, source, column)
        return remote(part, part, x_send.at[slot], x_recv.at[slot], other)

    def to_core(q, which, half):
        part = gathered[q].at[:, :, which, half]
        return remote(part, part, c_send.at[q, half], c_recv.at[q, half], core)

    def chain(i, source, up):
        part = kv.at[source] if i else g_qkv.at[source, twin]
        send = chain_p if up else chain_m
        return remote(part, part, send.at[i, source], chain_recv.at[i, source], above if up else below)

    def columns_across(source, half):
        part = g_qkv.at[source, half]
        return remote(part, part, half_send.at[source], half_recv.at[source], other)

    def columns_to(i, sender, receiver):
        return remote(stage.at[receiver], g_qkv.at[z, sender // 2, sender % 2], peer_send.at[0, i], peer_recv.at[0, i], quad[i])

    def features_to(i, block):
        part = g_feat.at[block + 1]
        return remote(part, part, feat_send.at[i], feat_recv.at[i], across if i == 0 else core)

    def context_to(i, sender, receiver):
        rows = pl.ds(pl.multiple_of(receiver * local_rows, local_rows), local_rows + 2 * HALO)
        return remote(ctx_out.at[rows], g_ctx.at[sender], peer_send.at[1, i], peer_recv.at[1, i], quad[i])

    def edge(up):
        rows = pl.ds(local_rows - PAD, PAD) if up else pl.ds(0, PAD)
        src, dst = (QUAD, 0) if up else (1, QUAD + 1)
        slot = 0 if up else 1
        return remote(
            g_feat.at[src, rows], g_feat.at[dst, rows], edge_send.at[slot], edge_recv.at[slot],
            above if up else below,
        )

    def spread(piece, item):
        pl.when(z < ZS - 1)(lambda: piece(item, z, True).start())
        pl.when(z > 0)(lambda: piece(item, z, False).start())

    def onward(piece, item, s, after=None):
        @pl.when(z >= s)
        def _():
            piece(item, z - s, True).wait_recv()
            pl.when(z < ZS - 1)(lambda: piece(item, z - s, True).start())
            if after is not None:
                after(z - s)

        @pl.when(z + s <= ZS - 1)
        def _():
            piece(item, z + s, False).wait_recv()
            pl.when(z > 0)(lambda: piece(item, z + s, False).start())
            if after is not None:
                after(z + s)

    def sent(piece, item):
        for s in range(ZS):
            pl.when((z >= s) & (z < ZS - 1))(lambda: piece(item, z - s, True).wait_send())
            if s == 0:
                pl.when(z > 0)(lambda: piece(item, z, False).wait_send())
            else:
                pl.when((z + s <= ZS - 1) & (z > 0))(lambda: piece(item, z + s, False).wait_send())

    def in_round(s, do):
        pl.when(z >= s)(lambda: do(z - s))
        pl.when(z + s <= ZS - 1)(lambda: do(z + s))

    def begin(q):
        own[q].wait()
        spread(along_z, q)

    def begin_across(q):
        own_along_y(q, y).start()

    def columns_on(s):
        onward(chain, 0, s, lambda source: columns_across(source, twin).start())

    def pass_on(q, s):
        def after(source):
            along_y(q, source, y).start()
            along_x(q, source, y, twin).start()

        onward(along_z, q, s, after)

    def cross(q, s):
        def do(source):
            along_y(q, source, 1 - y).wait_recv()
            along_x(q, source, 1 - y, twin).start()

        in_round(s, do)
        if s == ZS - 1:
            own_along_y(q, 1 - y).wait_recv()
            to_core(q, c, twin).start()

    def swap(q):
        def do(source):
            for column in range(2):
                along_x(q, source, column, 1 - twin).wait_recv()

        for s in range(1, ZS):
            in_round(s, do)
        to_core(q, c, 1 - twin).start()

    def arrive(q):
        for half in range(2):
            to_core(q, 1 - c, half).wait_recv()

    def finish(q):
        def do(source):
            along_y(q, source, y).wait_send()
            for column in range(2):
                along_x(q, source, column, twin).wait_send()

        sent(along_z, q)
        own_along_y(q, y).wait_send()
        for s in range(1, ZS):
            in_round(s, do)
        for half in range(2):
            to_core(q, c, half).wait_send()

    def columns(ref, start):
        block = ref[:, :, :, :, :, pl.ds(start, CHUNK)]
        return block.reshape(-1, CHUNK)

    def at(j):
        return pl.multiple_of(j * CHUNK, CHUNK)

    def normalise():
        def some(i, carry):
            rows_n[pl.ds(pl.multiple_of(i * local_rows, local_rows), local_rows), :] = norm_rows(
                g_feat[i + 1], ln1_ref[...]
            )
            return carry

        lax.fori_loop(0, QUAD, some, 0)

    def key_values():
        weight = g_qkv[:, :, :, :, pl.ds(HD, 2 * HD)].reshape(-1, 2 * HD)
        kv[z] = jnp.dot(rows_n[...], weight, preferred_element_type=jnp.float32).astype(jnp.bfloat16)

    def queries():
        weight = g_qkv[:, :, :, :, pl.ds(0, HD)].reshape(-1, HD)
        query[pl.ds(0, quad_rows), :] = jnp.dot(
            rows_n[...], weight, preferred_element_type=jnp.float32
        ).astype(jnp.bfloat16)
        pl.when(z > 0)(lambda: edge(True).wait_recv())
        pl.when(z < ZS - 1)(lambda: edge(False).wait_recv())
        before = g_feat[0, pl.ds(local_rows - PAD, PAD), :].astype(jnp.float32)[PAD - HALO :]
        after = g_feat[QUAD + 1, pl.ds(0, PAD), :].astype(jnp.float32)[:HALO]
        edges = norm_rows(jnp.concatenate([before, after], axis=0), ln1_ref[...])
        query[pl.ds(quad_rows, 2 * HALO), :] = jnp.dot(
            edges, weight, preferred_element_type=jnp.float32
        ).astype(jnp.bfloat16)
        before = g_feat[p, pl.ds(local_rows - PAD, PAD), :].astype(jnp.float32)[PAD - HALO :]
        after = g_feat[p + 2, pl.ds(0, PAD), :].astype(jnp.float32)[:HALO]
        ext[pl.ds(0, HALO), :] = before
        ext[pl.ds(HALO, local_rows), :] = g_feat[p + 1].astype(jnp.float32)
        ext[pl.ds(HALO + local_rows, HALO), :] = after

    nearest = z - 1 + 2 * (1 - (z + 3) // 4)
    farthest = 3 * (1 - z // 2)
    meets = (z, nearest, 6 - z - nearest - farthest, farthest)

    def attend(k):
        source = meets[k]
        keys = kv[source, :, pl.ds(0, HD)]
        values = kv[source, :, pl.ds(HD, HD)]
        factor = math.log2(math.e) / math.sqrt(HD)
        position = source * quad_rows + lax.broadcasted_iota(jnp.int32, (1, quad_rows), 1)
        bias = jnp.where(position < limit_ref[0], 0.0, -1e30)
        for i in range(query.shape[0] // BLOCK):
            rows = pl.ds(i * BLOCK, BLOCK)
            scores = lax.dot_general(
                query[rows, :], keys, (((1,), (1,)), ((), ())), preferred_element_type=jnp.float32
            ) + bias
            peak = jnp.max(scores, axis=-1, keepdims=True)
            if k > 0:
                before = peaks[rows, :][:, :1]
                peak = jnp.maximum(before, peak)
                shrink = jnp.exp2((before - peak) * factor)
            weights = jnp.exp2((scores - peak) * factor)
            total = jnp.sum(weights, axis=-1, keepdims=True)
            summed = jnp.dot(weights.astype(jnp.bfloat16), values, preferred_element_type=jnp.float32)
            if k > 0:
                total = total + totals[rows, :][:, :1] * shrink
                summed = summed + ctx[rows, :] * shrink
            if k < ZS - 1:
                peaks[rows, :] = jnp.broadcast_to(peak, (BLOCK, HD))
                totals[rows, :] = jnp.broadcast_to(total, (BLOCK, HD))
                ctx[rows, :] = summed
            else:
                ctx[rows, :] = summed / total

    def share_context():
        ctx_out[...] = jnp.concatenate(
            [ctx[pl.ds(quad_rows, HALO), :], ctx[pl.ds(0, quad_rows), :], ctx[pl.ds(quad_rows + HALO, HALO), :]], axis=0
        ).astype(jnp.bfloat16)
        for i, partner in enumerate(partners):
            context_to(i, p, partner).start()
        rows = pl.ds(pl.multiple_of(p * local_rows, local_rows), local_rows + 2 * HALO)
        g_ctx[p] = ctx_out[rows, :]

    def collect_context():
        for i, partner in enumerate(partners):
            context_to(i, partner, p).wait_recv()
        for head in range(QUAD):
            context[:, pl.ds(head * HD, HD)] = g_ctx[head]

    def project():
        def some(j, carry):
            product = jnp.dot(context[...], columns(g_out, at(j)), preferred_element_type=jnp.float32)
            attended[:, pl.ds(at(j), CHUNK)] = ext[:, pl.ds(at(j), CHUNK)] + product
            return carry

        lax.fori_loop(0, width // CHUNK, some, 0, unroll=True)
        ext_n[...] = norm_rows(attended[...], ln2_ref[...])

    def convolve():
        def some(j, carry):
            value = jnp.dot(ext_n[...], columns(g_pw1, at(j)), preferred_element_type=jnp.float32)
            gates = jnp.dot(ext_n[...], columns(g_pw1, at(j) + width), preferred_element_type=jnp.float32)
            frame = me * local_rows - HALO + lax.broadcasted_iota(jnp.int32, value.shape, 0)
            valid = (frame >= 0) & (frame < limit_ref[0])
            gated = jnp.where(valid, value * jax.nn.sigmoid(gates), 0.0)
            gate[...] = gated.astype(jnp.bfloat16).astype(jnp.float32)
            taps = dw_ref.shape[0]
            cols = pl.ds(at(j), CHUNK)
            conv = jnp.zeros((local_rows, CHUNK), jnp.float32)
            for tap in range(taps):
                conv = conv + dw_ref[pl.ds(tap, 1), cols] * gate[pl.ds(HALO - taps // 2 + tap, local_rows), :]
            shifted = bns_ref[:, cols] * conv + bnb_ref[:, cols]
            act[:, cols] = (shifted / (1.0 + jnp.exp(-shifted))).astype(jnp.bfloat16)
            return carry

        lax.fori_loop(0, width // CHUNK, some, 0, unroll=True)

    def close():
        def some(j, carry):
            cols = pl.ds(at(j), CHUNK)
            product = jnp.dot(act[...], columns(g_pw2, at(j)), preferred_element_type=jnp.float32)
            result_ref[:, cols] = (attended[pl.ds(HALO, local_rows), cols] + product).astype(jnp.bfloat16)
            return carry

        lax.fori_loop(0, width // CHUNK, some, 0, unroll=True)

    for i, partner in enumerate(partners):
        columns_to(i, p, partner).start()
    own_feat.wait()
    features_to(0, p).start()
    features_to(1, p).start()
    begin(PW1)
    for i, partner in enumerate(partners):
        columns_to(i, partner, p).wait_recv()
    spread(chain, 0)
    begin(OUT)
    begin(PW2)
    features_to(0, partners[0]).wait_recv()
    features_to(2, partners[0]).start()
    for q in (PW1, OUT, PW2):
        begin_across(q)
    columns_on(1)
    pass_on(PW1, 1)
    pass_on(OUT, 1)
    pass_on(PW2, 1)
    columns_on(2)
    features_to(1, partners[1]).wait_recv()
    features_to(2, partners[2]).wait_recv()
    pl.when(z < ZS - 1)(lambda: edge(True).start())
    pl.when(z > 0)(lambda: edge(False).start())
    pass_on(PW1, 2)
    pass_on(OUT, 2)
    normalise()
    pass_on(PW2, 2)
    columns_on(3)
    for s in range(1, ZS):
        in_round(s, lambda source: columns_across(source, 1 - twin).wait_recv())
    key_values()
    spread(chain, 1)
    pass_on(PW1, 3)
    pass_on(OUT, 3)
    pass_on(PW2, 3)
    cross(PW1, 1)
    cross(OUT, 1)
    queries()
    cross(PW2, 1)
    cross(PW1, 2)
    cross(OUT, 2)
    cross(PW2, 2)
    attend(0)
    onward(chain, 1, 1)
    cross(PW1, 3)
    cross(OUT, 3)
    cross(PW2, 3)
    attend(1)
    onward(chain, 1, 2)
    attend(2)
    swap(OUT)
    swap(PW1)
    swap(PW2)
    onward(chain, 1, 3)
    attend(3)
    share_context()
    for i, partner in enumerate(partners):
        columns_to(i, p, partner).wait_send()
    for i, block in enumerate((p, p, partners[0])):
        features_to(i, block).wait_send()
    pl.when(z < ZS - 1)(lambda: edge(True).wait_send())
    pl.when(z > 0)(lambda: edge(False).wait_send())
    for s in range(1, ZS):
        in_round(s, lambda source: columns_across(source, twin).wait_send())
    sent(chain, 0)
    arrive(OUT)
    collect_context()
    project()
    finish(OUT)
    arrive(PW1)
    convolve()
    finish(PW1)
    arrive(PW2)
    close()
    finish(PW2)
    sent(chain, 1)
    for i, partner in enumerate(partners):
        context_to(i, p, partner).wait_send()


def per_device_kernel(
    features, valid_length, ln1_gain, w_qkv, w_out, ln2_gain, w_pw1, w_dw, bn_scale, bn_shift, w_pw2
):
    local_rows, width = features.shape
    att = w_qkv.shape[1] // 3
    wide = local_rows + 2 * HALO

    def halves(weight):
        return weight.reshape(2, weight.shape[0] // 2, weight.shape[1])

    shards = [halves(w) for w in (w_out, w_pw1, w_pw2)]
    grid = (ZS, 2, 2)
    bf16, f32 = jnp.bfloat16, jnp.float32
    dma = pltpu.SemaphoreType.DMA
    hbm = pl.BlockSpec(memory_space=pl.ANY)
    vmem = pl.BlockSpec(memory_space=pltpu.VMEM)
    return pl.pallas_call(
        block_kernel,
        out_shape=jax.ShapeDtypeStruct((local_rows, width), bf16),
        in_specs=[
            pl.BlockSpec(memory_space=pltpu.SMEM), hbm, vmem, vmem, hbm, vmem, hbm, vmem, vmem, vmem, hbm,
        ],
        out_specs=vmem,
        scratch_shapes=[
            pltpu.VMEM((QUAD, w_qkv.shape[0], 3 * HD), bf16),
            pltpu.VMEM((ZS, 2, 2, w_qkv.shape[0], 3 * HD), bf16),
            pltpu.VMEM((QUAD + 2, local_rows, width), bf16),
            pltpu.VMEM((ZS, QUAD * local_rows, 2 * HD), bf16),
            pltpu.VMEM(grid + shards[0].shape, bf16),
            pltpu.VMEM(grid + shards[1].shape, bf16),
            pltpu.VMEM(grid + shards[2].shape, bf16),
            pltpu.VMEM((QUAD * local_rows, width), bf16),
            pltpu.VMEM((QUAD * local_rows + 2 * HALO, HD), bf16),
            pltpu.VMEM((QUAD * local_rows + 2 * HALO, HD), f32),
            pltpu.VMEM((QUAD * local_rows + 2 * HALO, HD), f32),
            pltpu.VMEM((QUAD * local_rows + 2 * HALO, HD), f32),
            pltpu.VMEM((QUAD * local_rows + 2 * HALO, HD), bf16),
            pltpu.VMEM((QUAD, wide, HD), bf16),
            pltpu.VMEM((wide, att), bf16),
            pltpu.VMEM((wide, width), f32),
            pltpu.VMEM((wide, width), bf16),
            pltpu.VMEM((wide, width), f32),
            pltpu.VMEM((wide, CHUNK), f32),
            pltpu.VMEM((local_rows, width), bf16),
            dma((COUNT + 1,)),
        ]
        + [dma((COUNT, ZS))] * 5
        + [dma((COUNT, ZS, 2))] * 2
        + [dma((COUNT, 2))] * 2
        + [dma((2, 3))] * 2
        + [dma((3,))] * 2
        + [dma((2,))] * 2
        + [dma((2, ZS))] * 3
        + [dma((ZS,))] * 2,
        compiler_params=pltpu.CompilerParams(
            collective_id=0, has_side_effects=True, vmem_limit_bytes=56 * 1024 * 1024
        ),
    )(
        valid_length, features, ln1_gain[None], w_qkv, shards[0], ln2_gain[None], shards[1], w_dw,
        bn_scale[None], bn_shift[None], shards[2],
    )


def per_device(*arguments):
    if lax.axis_size("frames") == 4 * ZS and lax.axis_size("groups") == 2:
        return per_device_kernel(*arguments)
    return per_device_xla(*arguments)


def solution(mesh):
    placed = (
        P(("groups", "frames"), None),
        P("groups"),
        P(),
        P("frames", None),
        P("frames", None),
        P(),
        P("frames", None),
        P(),
        P(),
        P(),
        P("frames", None),
    )
    return jax.shard_map(
        per_device,
        mesh=mesh,
        in_specs=placed,
        out_specs=P(("groups", "frames"), None),
        check_vma=False,
    )
```

```python
import functools
import math

import jax
import jax.numpy as jnp
from jax import lax
from jax.experimental import pallas as pl
from jax.experimental.pallas import tpu as pltpu
from jax.sharding import PartitionSpec as P

HEADS = 4
HD = 128


EPSILON = 1e-05


def extended(cells, sides, width):
    for axis, dim in sides:
        count = lax.axis_size(axis)
        ends = count - 1
        head = lax.slice_in_dim(cells, 0, width, axis=dim)
        tail = lax.slice_in_dim(cells, cells.shape[dim] - width, cells.shape[dim], axis=dim)
        cells = jnp.concatenate(
            [
                lax.ppermute(tail, axis, [(i, (i + 1) % count) for i in range(ends)]),
                cells,
                lax.ppermute(head, axis, [((i + 1) % count, i) for i in range(ends)]),
            ],
            axis=dim,
        )
    return cells


def layer_norm(values, gain):
    values = values.astype(jnp.float32)
    mean = jnp.mean(values, axis=-1, keepdims=True)
    centred = values - mean
    variance = jnp.mean(centred * centred, axis=-1, keepdims=True)
    return (centred * lax.rsqrt(variance + EPSILON) * gain).astype(jnp.bfloat16)


def per_device_xla(
    features, valid_length, ln1_gain, w_qkv, w_out, ln2_gain, w_pw1, w_dw, bn_scale, bn_shift, w_pw2
):
    limit = valid_length[0]
    local_rows = features.shape[0]
    width = features.shape[1]
    att_width = w_qkv.shape[1] // 3
    scale = 1.0 / math.sqrt(HD)
    tails = (
        lax.all_gather(w_out, "frames", axis=0, tiled=True),
        lax.all_gather(w_pw1, "frames", axis=0, tiled=True),
        lax.all_gather(w_pw2, "frames", axis=0, tiled=True),
    )
    full_out, full_pw1, full_pw2 = tails
    normed1 = layer_norm(features, ln1_gain)
    qkv = jnp.dot(
        normed1,
        lax.all_gather(w_qkv, "frames", axis=0, tiled=True),
        preferred_element_type=jnp.float32,
    ).astype(jnp.bfloat16)
    query_heads = qkv[:, :att_width].reshape(local_rows, HEADS, HD)
    keys = qkv[:, att_width : 2 * att_width]
    values = qkv[:, 2 * att_width :]
    maxima = jnp.full((HEADS, local_rows), -1e30, jnp.float32)
    key_rows = lax.all_gather(keys, "frames", axis=0, tiled=True)
    value_rows = lax.all_gather(values, "frames", axis=0, tiled=True)
    count = key_rows.shape[0]
    key_heads = key_rows.reshape(count, HEADS, HD)
    value_heads = value_rows.reshape(count, HEADS, HD)
    scores = (
        jnp.einsum("qhd,khd->hqk", query_heads, key_heads, preferred_element_type=jnp.float32)
        * scale
    )
    position = jnp.arange(count, dtype=jnp.int32)
    valid = (position < limit)[None, None, :]
    scores = jnp.where(valid, scores, -1e30)
    fresh = jnp.maximum(maxima, jnp.max(scores, axis=-1))
    weights = jnp.where(valid, jnp.exp(scores - fresh[..., None]), 0.0)
    totals = jnp.sum(weights, axis=-1)
    update = jnp.einsum(
        "hqk,khd->hqd",
        weights.astype(jnp.bfloat16),
        value_heads,
        preferred_element_type=jnp.float32,
    )
    summed = update
    maxima, totals, summed = (fresh, totals, summed)
    context = (
        (summed / totals[..., None])
        .transpose(1, 0, 2)
        .reshape(local_rows, att_width)
        .astype(jnp.bfloat16)
    )
    attended = features.astype(jnp.float32) + jnp.dot(
        context, full_out, preferred_element_type=jnp.float32
    )
    normed2 = layer_norm(attended, ln2_gain)
    both = jnp.dot(normed2, full_pw1, preferred_element_type=jnp.float32)
    frame_index = lax.axis_index("frames") * local_rows + jnp.arange(local_rows, dtype=jnp.int32)
    frame_valid = (frame_index < limit)[:, None]
    gated = jnp.where(frame_valid, both[:, :width] * jax.nn.sigmoid(both[:, width:]), 0.0).astype(
        jnp.bfloat16
    )
    half_window = (w_dw.shape[0] - 1) // 2
    widened = extended(gated, (("frames", 0),), half_window)
    widened = widened.astype(jnp.float32)
    conv = jnp.zeros((local_rows, width), jnp.float32)
    for tap in range(w_dw.shape[0]):
        conv = conv + w_dw[tap][None, :] * widened[tap : tap + local_rows]
    activated = jax.nn.silu(bn_scale * conv + bn_shift).astype(jnp.bfloat16)
    result = attended + jnp.dot(activated, full_pw2, preferred_element_type=jnp.float32)
    return result.astype(jnp.bfloat16)


ZS = 4
QUAD = 4
CHUNK = 256
PAD = 16
HALO = 8
BLOCK = 176
OUT, PW1, PW2 = range(3)
COUNT = 3


def norm_rows(values, gain):
    values = values.astype(jnp.float32)
    mean = jnp.mean(values, axis=-1, keepdims=True)
    centred = values - mean
    variance = jnp.mean(centred * centred, axis=-1, keepdims=True)
    return (centred * lax.rsqrt(variance + EPSILON) * gain).astype(jnp.bfloat16)


def block_kernel(
    limit_ref, feat_ref, ln1_ref, qkv_ref, out_w_ref, ln2_ref, pw1_ref, dw_ref, bns_ref, bnb_ref, pw2_ref,
    result_ref,
    stage, g_qkv, g_feat, kv, g_out, g_pw1, g_pw2, rows_n, query, ctx, peaks, totals, ctx_out, g_ctx, context, ext, ext_n, attended,
    gate, act,
    local_sem, zp_send, zm_send, z_recv, y_send, y_recv, x_send, x_recv, c_send, c_recv,
    peer_send, peer_recv, feat_send, feat_recv, edge_send, edge_recv, chain_p, chain_m, chain_recv,
    half_send, half_recv,
):
    twin = lax.axis_index("groups")
    me = lax.axis_index("frames")
    z, y, c = me // 4, (me // 2) % 2, me % 2
    p = me % QUAD
    width = ext.shape[1]
    local_rows = feat_ref.shape[0]
    quad_rows = QUAD * local_rows
    gathered = (g_out, g_pw1, g_pw2)
    shards = (out_w_ref, pw1_ref, pw2_ref)
    above, below = {"frames": me + 4}, {"frames": me - 4}
    partners = (QUAD // 2 * (1 - y) + c, 2 * y + 1 - c, QUAD // 2 * (1 - y) + 1 - c)
    quad = [{"frames": z * QUAD + partner} for partner in partners]
    across, core = quad[0], quad[1]
    other = {"groups": 1 - twin}

    own = [
        pltpu.make_async_copy(shards[q], gathered[q].at[z, y, c], local_sem.at[q])
        for q in range(COUNT)
    ]
    own_feat = pltpu.make_async_copy(feat_ref, g_feat.at[p + 1], local_sem.at[COUNT])
    for copy in own + [own_feat]:
        copy.start()
    for head in range(QUAD):
        for kind in range(3):
            stage[head, :, pl.ds(kind * HD, HD)] = qkv_ref[:, pl.ds((kind * QUAD + head) * HD, HD)]
    g_qkv[z, y, c] = stage[p]
    g_feat[0, pl.ds(local_rows - PAD, PAD), :] = jnp.zeros((PAD, width), jnp.bfloat16)
    g_feat[QUAD + 1, pl.ds(0, PAD), :] = jnp.zeros((PAD, width), jnp.bfloat16)

    barrier = pltpu.get_barrier_semaphore()

    def greet(device):
        pl.semaphore_signal(barrier, inc=1, device_id=device, device_id_type=pl.DeviceIdType.MESH)

    for device in quad:
        greet(device)
    greet(other)
    pl.when(z > 0)(lambda: greet(below))
    pl.when(z < ZS - 1)(lambda: greet(above))
    pl.semaphore_wait(barrier, 4 + jnp.where(z > 0, 1, 0) + jnp.where(z < ZS - 1, 1, 0))

    def remote(src, dst, send, recv, device):
        return pltpu.make_async_remote_copy(
            src_ref=src, dst_ref=dst, send_sem=send, recv_sem=recv,
            device_id=device, device_id_type=pl.DeviceIdType.MESH,
        )

    def along_z(q, source, up):
        part = gathered[q].at[source, y, c, twin]
        send = zp_send if up else zm_send
        return remote(part, part, send.at[q, source], z_recv.at[q, source], above if up else below)

    def along_y(q, source, column):
        part = gathered[q].at[source, column, c, twin]
        return remote(part, part, y_send.at[q, source], y_recv.at[q, source], across)

    def own_along_y(q, column):
        part = gathered[q].at[z, column, c]
        return remote(part, part, y_send.at[q, z], y_recv.at[q, z], across)

    def along_x(q, source, column, half):
        part = gathered[q].at[source, column, c, half]
        slot = (q, source, column)
        return remote(part, part, x_send.at[slot], x_recv.at[slot], other)

    def to_core(q, which, half):
        part = gathered[q].at[:, :, which, half]
        return remote(part, part, c_send.at[q, half], c_recv.at[q, half], core)

    def chain(i, source, up):
        part = kv.at[source] if i else g_qkv.at[source, twin]
        send = chain_p if up else chain_m
        return remote(part, part, send.at[i, source], chain_recv.at[i, source], above if up else below)

    def columns_across(source, half):
        part = g_qkv.at[source, half]
        return remote(part, part, half_send.at[source], half_recv.at[source], other)

    def columns_to(i, sender, receiver):
        return remote(stage.at[receiver], g_qkv.at[z, sender // 2, sender % 2], peer_send.at[0, i], peer_recv.at[0, i], quad[i])

    def features_to(i, block):
        part = g_feat.at[block + 1]
        return remote(part, part, feat_send.at[i], feat_recv.at[i], across if i == 0 else core)

    def context_to(i, sender, receiver):
        rows = pl.ds(pl.multiple_of(receiver * local_rows, local_rows), local_rows + 2 * HALO)
        return remote(ctx_out.at[rows], g_ctx.at[sender], peer_send.at[1, i], peer_recv.at[1, i], quad[i])

    def edge(up):
        rows = pl.ds(local_rows - PAD, PAD) if up else pl.ds(0, PAD)
        src, dst = (QUAD, 0) if up else (1, QUAD + 1)
        slot = 0 if up else 1
        return remote(
            g_feat.at[src, rows], g_feat.at[dst, rows], edge_send.at[slot], edge_recv.at[slot],
            above if up else below,
        )

    def spread(piece, item):
        pl.when(z < ZS - 1)(lambda: piece(item, z, True).start())
        pl.when(z > 0)(lambda: piece(item, z, False).start())

    def onward(piece, item, s, after=None):
        @pl.when(z >= s)
        def _():
            piece(item, z - s, True).wait_recv()
            pl.when(z < ZS - 1)(lambda: piece(item, z - s, True).start())
            if after is not None:
                after(z - s)

        @pl.when(z + s <= ZS - 1)
        def _():
            piece(item, z + s, False).wait_recv()
            pl.when(z > 0)(lambda: piece(item, z + s, False).start())
            if after is not None:
                after(z + s)

    def sent(piece, item):
        for s in range(ZS):
            pl.when((z >= s) & (z < ZS - 1))(lambda: piece(item, z - s, True).wait_send())
            if s == 0:
                pl.when(z > 0)(lambda: piece(item, z, False).wait_send())
            else:
                pl.when((z + s <= ZS - 1) & (z > 0))(lambda: piece(item, z + s, False).wait_send())

    def in_round(s, do):
        pl.when(z >= s)(lambda: do(z - s))
        pl.when(z + s <= ZS - 1)(lambda: do(z + s))

    def begin(q):
        own[q].wait()
        spread(along_z, q)

    def begin_across(q):
        own_along_y(q, y).start()

    def columns_on(s):
        onward(chain, 0, s, lambda source: columns_across(source, twin).start())

    def pass_on(q, s):
        def after(source):
            along_y(q, source, y).start()
            along_x(q, source, y, twin).start()

        onward(along_z, q, s, after)

    def cross(q, s):
        def do(source):
            along_y(q, source, 1 - y).wait_recv()
            along_x(q, source, 1 - y, twin).start()

        in_round(s, do)
        if s == ZS - 1:
            own_along_y(q, 1 - y).wait_recv()
            to_core(q, c, twin).start()

    def swap(q):
        def do(source):
            for column in range(2):
                along_x(q, source, column, 1 - twin).wait_recv()

        for s in range(1, ZS):
            in_round(s, do)
        to_core(q, c, 1 - twin).start()

    def arrive(q):
        for half in range(2):
            to_core(q, 1 - c, half).wait_recv()

    def finish(q):
        def do(source):
            along_y(q, source, y).wait_send()
            for column in range(2):
                along_x(q, source, column, twin).wait_send()

        sent(along_z, q)
        own_along_y(q, y).wait_send()
        for s in range(1, ZS):
            in_round(s, do)
        for half in range(2):
            to_core(q, c, half).wait_send()

    def columns(ref, start):
        block = ref[:, :, :, :, :, pl.ds(start, CHUNK)]
        return block.reshape(-1, CHUNK)

    def at(j):
        return pl.multiple_of(j * CHUNK, CHUNK)

    def normalise():
        def some(i, carry):
            rows_n[pl.ds(pl.multiple_of(i * local_rows, local_rows), local_rows), :] = norm_rows(
                g_feat[i + 1], ln1_ref[...]
            )
            return carry

        lax.fori_loop(0, QUAD, some, 0)

    def key_values():
        weight = g_qkv[:, :, :, :, pl.ds(HD, 2 * HD)].reshape(-1, 2 * HD)
        kv[z] = jnp.dot(rows_n[...], weight, preferred_element_type=jnp.float32).astype(jnp.bfloat16)

    def queries():
        weight = g_qkv[:, :, :, :, pl.ds(0, HD)].reshape(-1, HD)
        query[pl.ds(0, quad_rows), :] = jnp.dot(
            rows_n[...], weight, preferred_element_type=jnp.float32
        ).astype(jnp.bfloat16)
        pl.when(z > 0)(lambda: edge(True).wait_recv())
        pl.when(z < ZS - 1)(lambda: edge(False).wait_recv())
        before = g_feat[0, pl.ds(local_rows - PAD, PAD), :].astype(jnp.float32)[PAD - HALO :]
        after = g_feat[QUAD + 1, pl.ds(0, PAD), :].astype(jnp.float32)[:HALO]
        edges = norm_rows(jnp.concatenate([before, after], axis=0), ln1_ref[...])
        query[pl.ds(quad_rows, 2 * HALO), :] = jnp.dot(
            edges, weight, preferred_element_type=jnp.float32
        ).astype(jnp.bfloat16)
        before = g_feat[p, pl.ds(local_rows - PAD, PAD), :].astype(jnp.float32)[PAD - HALO :]
        after = g_feat[p + 2, pl.ds(0, PAD), :].astype(jnp.float32)[:HALO]
        ext[pl.ds(0, HALO), :] = before
        ext[pl.ds(HALO, local_rows), :] = g_feat[p + 1].astype(jnp.float32)
        ext[pl.ds(HALO + local_rows, HALO), :] = after

    nearest = z - 1 + 2 * (1 - (z + 3) // 4)
    farthest = 3 * (1 - z // 2)
    meets = (z, nearest, 6 - z - nearest - farthest, farthest)

    def attend(k):
        source = meets[k]
        keys = kv[source, :, pl.ds(0, HD)]
        values = kv[source, :, pl.ds(HD, HD)]
        factor = math.log2(math.e) / math.sqrt(HD)
        position = source * quad_rows + lax.broadcasted_iota(jnp.int32, (1, quad_rows), 1)
        bias = jnp.where(position < limit_ref[0], 0.0, -1e30)
        for i in range(query.shape[0] // BLOCK):
            rows = pl.ds(i * BLOCK, BLOCK)
            scores = lax.dot_general(
                query[rows, :], keys, (((1,), (1,)), ((), ())), preferred_element_type=jnp.float32
            ) + bias
            peak = jnp.max(scores, axis=-1, keepdims=True)
            if k > 0:
                before = peaks[rows, :][:, :1]
                peak = jnp.maximum(before, peak)
                shrink = jnp.exp2((before - peak) * factor)
            weights = jnp.exp2((scores - peak) * factor)
            total = jnp.sum(weights, axis=-1, keepdims=True)
            summed = jnp.dot(weights.astype(jnp.bfloat16), values, preferred_element_type=jnp.float32)
            if k > 0:
                total = total + totals[rows, :][:, :1] * shrink
                summed = summed + ctx[rows, :] * shrink
            if k < ZS - 1:
                peaks[rows, :] = jnp.broadcast_to(peak, (BLOCK, HD))
                totals[rows, :] = jnp.broadcast_to(total, (BLOCK, HD))
                ctx[rows, :] = summed
            else:
                ctx[rows, :] = summed / total

    def share_context():
        ctx_out[...] = jnp.concatenate(
            [ctx[pl.ds(quad_rows, HALO), :], ctx[pl.ds(0, quad_rows), :], ctx[pl.ds(quad_rows + HALO, HALO), :]], axis=0
        ).astype(jnp.bfloat16)
        for i, partner in enumerate(partners):
            context_to(i, p, partner).start()
        rows = pl.ds(pl.multiple_of(p * local_rows, local_rows), local_rows + 2 * HALO)
        g_ctx[p] = ctx_out[rows, :]

    def collect_context():
        for i, partner in enumerate(partners):
            context_to(i, partner, p).wait_recv()
        for head in range(QUAD):
            context[:, pl.ds(head * HD, HD)] = g_ctx[head]

    def project():
        def some(j, carry):
            product = jnp.dot(context[...], columns(g_out, at(j)), preferred_element_type=jnp.float32)
            attended[:, pl.ds(at(j), CHUNK)] = ext[:, pl.ds(at(j), CHUNK)] + product
            return carry

        lax.fori_loop(0, width // CHUNK, some, 0, unroll=True)
        ext_n[...] = norm_rows(attended[...], ln2_ref[...])

    def convolve():
        def some(j, carry):
            value = jnp.dot(ext_n[...], columns(g_pw1, at(j)), preferred_element_type=jnp.float32)
            gates = jnp.dot(ext_n[...], columns(g_pw1, at(j) + width), preferred_element_type=jnp.float32)
            frame = me * local_rows - HALO + lax.broadcasted_iota(jnp.int32, value.shape, 0)
            valid = (frame >= 0) & (frame < limit_ref[0])
            gated = jnp.where(valid, value * jax.nn.sigmoid(gates), 0.0)
            gate[...] = gated.astype(jnp.bfloat16).astype(jnp.float32)
            taps = dw_ref.shape[0]
            cols = pl.ds(at(j), CHUNK)
            conv = jnp.zeros((local_rows, CHUNK), jnp.float32)
            for tap in range(taps):
                conv = conv + dw_ref[pl.ds(tap, 1), cols] * gate[pl.ds(HALO - taps // 2 + tap, local_rows), :]
            shifted = bns_ref[:, cols] * conv + bnb_ref[:, cols]
            act[:, cols] = (shifted / (1.0 + jnp.exp(-shifted))).astype(jnp.bfloat16)
            return carry

        lax.fori_loop(0, width // CHUNK, some, 0, unroll=True)

    def close():
        def some(j, carry):
            cols = pl.ds(at(j), CHUNK)
            product = jnp.dot(act[...], columns(g_pw2, at(j)), preferred_element_type=jnp.float32)
            result_ref[:, cols] = (attended[pl.ds(HALO, local_rows), cols] + product).astype(jnp.bfloat16)
            return carry

        lax.fori_loop(0, width // CHUNK, some, 0, unroll=True)

    for i, partner in enumerate(partners):
        columns_to(i, p, partner).start()
    own_feat.wait()
    features_to(0, p).start()
    features_to(1, p).start()
    begin(PW1)
    for i, partner in enumerate(partners):
        columns_to(i, partner, p).wait_recv()
    spread(chain, 0)
    begin(OUT)
    features_to(0, partners[0]).wait_recv()
    features_to(2, partners[0]).start()
    begin_across(PW1)
    begin_across(OUT)
    columns_on(1)
    pass_on(PW1, 1)
    features_to(1, partners[1]).wait_recv()
    features_to(2, partners[2]).wait_recv()
    pl.when(z < ZS - 1)(lambda: edge(True).start())
    pl.when(z > 0)(lambda: edge(False).start())
    columns_on(2)
    pass_on(OUT, 1)
    normalise()
    columns_on(3)
    pass_on(PW1, 2)
    pass_on(OUT, 2)
    for s in range(1, ZS):
        in_round(s, lambda source: columns_across(source, 1 - twin).wait_recv())
    key_values()
    spread(chain, 1)
    cross(PW1, 1)
    pass_on(PW1, 3)
    pass_on(OUT, 3)
    cross(OUT, 1)
    queries()
    cross(PW1, 2)
    cross(OUT, 2)
    attend(0)
    onward(chain, 1, 1)
    begin(PW2)
    begin_across(PW2)
    cross(PW1, 3)
    cross(OUT, 3)
    attend(1)
    onward(chain, 1, 2)
    pass_on(PW2, 1)
    attend(2)
    swap(OUT)
    swap(PW1)
    onward(chain, 1, 3)
    pass_on(PW2, 2)
    cross(PW2, 1)
    attend(3)
    share_context()
    pass_on(PW2, 3)
    cross(PW2, 2)
    arrive(OUT)
    collect_context()
    cross(PW2, 3)
    project()
    swap(PW2)
    finish(OUT)
    arrive(PW1)
    convolve()
    finish(PW1)
    for i, partner in enumerate(partners):
        columns_to(i, p, partner).wait_send()
    for i, block in enumerate((p, p, partners[0])):
        features_to(i, block).wait_send()
    pl.when(z < ZS - 1)(lambda: edge(True).wait_send())
    pl.when(z > 0)(lambda: edge(False).wait_send())
    for s in range(1, ZS):
        in_round(s, lambda source: columns_across(source, twin).wait_send())
    sent(chain, 0)
    arrive(PW2)
    close()
    finish(PW2)
    sent(chain, 1)
    for i, partner in enumerate(partners):
        context_to(i, p, partner).wait_send()


def per_device_kernel(
    features, valid_length, ln1_gain, w_qkv, w_out, ln2_gain, w_pw1, w_dw, bn_scale, bn_shift, w_pw2
):
    local_rows, width = features.shape
    att = w_qkv.shape[1] // 3
    wide = local_rows + 2 * HALO

    def halves(weight):
        return weight.reshape(2, weight.shape[0] // 2, weight.shape[1])

    shards = [halves(w) for w in (w_out, w_pw1, w_pw2)]
    grid = (ZS, 2, 2)
    bf16, f32 = jnp.bfloat16, jnp.float32
    dma = pltpu.SemaphoreType.DMA
    hbm = pl.BlockSpec(memory_space=pl.ANY)
    vmem = pl.BlockSpec(memory_space=pltpu.VMEM)
    return pl.pallas_call(
        block_kernel,
        out_shape=jax.ShapeDtypeStruct((local_rows, width), bf16),
        in_specs=[
            pl.BlockSpec(memory_space=pltpu.SMEM), hbm, vmem, vmem, hbm, vmem, hbm, vmem, vmem, vmem, hbm,
        ],
        out_specs=vmem,
        scratch_shapes=[
            pltpu.VMEM((QUAD, w_qkv.shape[0], 3 * HD), bf16),
            pltpu.VMEM((ZS, 2, 2, w_qkv.shape[0], 3 * HD), bf16),
            pltpu.VMEM((QUAD + 2, local_rows, width), bf16),
            pltpu.VMEM((ZS, QUAD * local_rows, 2 * HD), bf16),
            pltpu.VMEM(grid + shards[0].shape, bf16),
            pltpu.VMEM(grid + shards[1].shape, bf16),
            pltpu.VMEM(grid + shards[2].shape, bf16),
            pltpu.VMEM((QUAD * local_rows, width), bf16),
            pltpu.VMEM((QUAD * local_rows + 2 * HALO, HD), bf16),
            pltpu.VMEM((QUAD * local_rows + 2 * HALO, HD), f32),
            pltpu.VMEM((QUAD * local_rows + 2 * HALO, HD), f32),
            pltpu.VMEM((QUAD * local_rows + 2 * HALO, HD), f32),
            pltpu.VMEM((QUAD * local_rows + 2 * HALO, HD), bf16),
            pltpu.VMEM((QUAD, wide, HD), bf16),
            pltpu.VMEM((wide, att), bf16),
            pltpu.VMEM((wide, width), f32),
            pltpu.VMEM((wide, width), bf16),
            pltpu.VMEM((wide, width), f32),
            pltpu.VMEM((wide, CHUNK), f32),
            pltpu.VMEM((local_rows, width), bf16),
            dma((COUNT + 1,)),
        ]
        + [dma((COUNT, ZS))] * 5
        + [dma((COUNT, ZS, 2))] * 2
        + [dma((COUNT, 2))] * 2
        + [dma((2, 3))] * 2
        + [dma((3,))] * 2
        + [dma((2,))] * 2
        + [dma((2, ZS))] * 3
        + [dma((ZS,))] * 2,
        compiler_params=pltpu.CompilerParams(
            collective_id=0, has_side_effects=True, vmem_limit_bytes=56 * 1024 * 1024
        ),
    )(
        valid_length, features, ln1_gain[None], w_qkv, shards[0], ln2_gain[None], shards[1], w_dw,
        bn_scale[None], bn_shift[None], shards[2],
    )


def per_device(*arguments):
    if lax.axis_size("frames") == 4 * ZS and lax.axis_size("groups") == 2:
        return per_device_kernel(*arguments)
    return per_device_xla(*arguments)


def solution(mesh):
    placed = (
        P(("groups", "frames"), None),
        P("groups"),
        P(),
        P("frames", None),
        P("frames", None),
        P(),
        P("frames", None),
        P(),
        P(),
        P(),
        P("frames", None),
    )
    return jax.shard_map(
        per_device,
        mesh=mesh,
        in_specs=placed,
        out_specs=P(("groups", "frames"), None),
        check_vma=False,
    )
```

```python
import functools
import math

import jax
import jax.numpy as jnp
from jax import lax
from jax.experimental import pallas as pl
from jax.experimental.pallas import tpu as pltpu
from jax.sharding import PartitionSpec as P

HEADS = 4
HD = 128


EPSILON = 1e-05


def extended(cells, sides, width):
    for axis, dim in sides:
        count = lax.axis_size(axis)
        ends = count - 1
        head = lax.slice_in_dim(cells, 0, width, axis=dim)
        tail = lax.slice_in_dim(cells, cells.shape[dim] - width, cells.shape[dim], axis=dim)
        cells = jnp.concatenate(
            [
                lax.ppermute(tail, axis, [(i, (i + 1) % count) for i in range(ends)]),
                cells,
                lax.ppermute(head, axis, [((i + 1) % count, i) for i in range(ends)]),
            ],
            axis=dim,
        )
    return cells


def layer_norm(values, gain):
    values = values.astype(jnp.float32)
    mean = jnp.mean(values, axis=-1, keepdims=True)
    centred = values - mean
    variance = jnp.mean(centred * centred, axis=-1, keepdims=True)
    return (centred * lax.rsqrt(variance + EPSILON) * gain).astype(jnp.bfloat16)


def per_device_xla(
    features, valid_length, ln1_gain, w_qkv, w_out, ln2_gain, w_pw1, w_dw, bn_scale, bn_shift, w_pw2
):
    limit = valid_length[0]
    local_rows = features.shape[0]
    width = features.shape[1]
    att_width = w_qkv.shape[1] // 3
    scale = 1.0 / math.sqrt(HD)
    tails = (
        lax.all_gather(w_out, "frames", axis=0, tiled=True),
        lax.all_gather(w_pw1, "frames", axis=0, tiled=True),
        lax.all_gather(w_pw2, "frames", axis=0, tiled=True),
    )
    full_out, full_pw1, full_pw2 = tails
    normed1 = layer_norm(features, ln1_gain)
    qkv = jnp.dot(
        normed1,
        lax.all_gather(w_qkv, "frames", axis=0, tiled=True),
        preferred_element_type=jnp.float32,
    ).astype(jnp.bfloat16)
    query_heads = qkv[:, :att_width].reshape(local_rows, HEADS, HD)
    keys = qkv[:, att_width : 2 * att_width]
    values = qkv[:, 2 * att_width :]
    maxima = jnp.full((HEADS, local_rows), -1e30, jnp.float32)
    key_rows = lax.all_gather(keys, "frames", axis=0, tiled=True)
    value_rows = lax.all_gather(values, "frames", axis=0, tiled=True)
    count = key_rows.shape[0]
    key_heads = key_rows.reshape(count, HEADS, HD)
    value_heads = value_rows.reshape(count, HEADS, HD)
    scores = (
        jnp.einsum("qhd,khd->hqk", query_heads, key_heads, preferred_element_type=jnp.float32)
        * scale
    )
    position = jnp.arange(count, dtype=jnp.int32)
    valid = (position < limit)[None, None, :]
    scores = jnp.where(valid, scores, -1e30)
    fresh = jnp.maximum(maxima, jnp.max(scores, axis=-1))
    weights = jnp.where(valid, jnp.exp(scores - fresh[..., None]), 0.0)
    totals = jnp.sum(weights, axis=-1)
    update = jnp.einsum(
        "hqk,khd->hqd",
        weights.astype(jnp.bfloat16),
        value_heads,
        preferred_element_type=jnp.float32,
    )
    summed = update
    maxima, totals, summed = (fresh, totals, summed)
    context = (
        (summed / totals[..., None])
        .transpose(1, 0, 2)
        .reshape(local_rows, att_width)
        .astype(jnp.bfloat16)
    )
    attended = features.astype(jnp.float32) + jnp.dot(
        context, full_out, preferred_element_type=jnp.float32
    )
    normed2 = layer_norm(attended, ln2_gain)
    both = jnp.dot(normed2, full_pw1, preferred_element_type=jnp.float32)
    frame_index = lax.axis_index("frames") * local_rows + jnp.arange(local_rows, dtype=jnp.int32)
    frame_valid = (frame_index < limit)[:, None]
    gated = jnp.where(frame_valid, both[:, :width] * jax.nn.sigmoid(both[:, width:]), 0.0).astype(
        jnp.bfloat16
    )
    half_window = (w_dw.shape[0] - 1) // 2
    widened = extended(gated, (("frames", 0),), half_window)
    widened = widened.astype(jnp.float32)
    conv = jnp.zeros((local_rows, width), jnp.float32)
    for tap in range(w_dw.shape[0]):
        conv = conv + w_dw[tap][None, :] * widened[tap : tap + local_rows]
    activated = jax.nn.silu(bn_scale * conv + bn_shift).astype(jnp.bfloat16)
    result = attended + jnp.dot(activated, full_pw2, preferred_element_type=jnp.float32)
    return result.astype(jnp.bfloat16)


ZS = 4
QUAD = 4
CHUNK = 256
PAD = 16
HALO = 8
BLOCK = 176
REST = 0
COUNT = 1


def norm_rows(values, gain):
    values = values.astype(jnp.float32)
    mean = jnp.mean(values, axis=-1, keepdims=True)
    centred = values - mean
    variance = jnp.mean(centred * centred, axis=-1, keepdims=True)
    return (centred * lax.rsqrt(variance + EPSILON) * gain).astype(jnp.bfloat16)


def block_kernel(
    limit_ref, feat_ref, ln1_ref, qkv_ref, out_w_ref, ln2_ref, pw1_ref, dw_ref, bns_ref, bnb_ref, pw2_ref,
    result_ref,
    stage, g_qkv, g_feat, kv, g_rest, rows_n, query, ctx, peaks, totals, ctx_out, g_ctx, context, ext, ext_n, attended,
    gate, act,
    local_sem, zp_send, zm_send, z_recv, y_send, y_recv, x_send, x_recv, c_send, c_recv,
    peer_send, peer_recv, feat_send, feat_recv, edge_send, edge_recv, chain_p, chain_m, chain_recv,
    half_send, half_recv,
):
    twin = lax.axis_index("groups")
    me = lax.axis_index("frames")
    z, y, c = me // 4, (me // 2) % 2, me % 2
    p = me % QUAD
    width = ext.shape[1]
    local_rows = feat_ref.shape[0]
    quad_rows = QUAD * local_rows
    gathered = (g_rest,)
    above, below = {"frames": me + 4}, {"frames": me - 4}
    partners = (QUAD // 2 * (1 - y) + c, 2 * y + 1 - c, QUAD // 2 * (1 - y) + 1 - c)
    quad = [{"frames": z * QUAD + partner} for partner in partners]
    across, core = quad[0], quad[1]
    other = {"groups": 1 - twin}

    counts = (out_w_ref.shape[1], pw1_ref.shape[1], pw1_ref.shape[1], pw2_ref.shape[1])
    starts = [sum(counts[:i]) for i in range(4)]
    own = []
    for half in range(2):
        pieces = (
            out_w_ref.at[half],
            pw1_ref.at[half, :, pl.ds(0, width)],
            pw1_ref.at[half, :, pl.ds(width, width)],
            pw2_ref.at[half],
        )
        for i in range(4):
            part = g_rest.at[z, y, c, half, pl.ds(starts[i], counts[i])]
            own.append(pltpu.make_async_copy(pieces[i], part, local_sem.at[4 * half + i]))
    own_feat = pltpu.make_async_copy(feat_ref, g_feat.at[p + 1], local_sem.at[8])
    for copy in own + [own_feat]:
        copy.start()
    for head in range(QUAD):
        for kind in range(3):
            stage[head, :, pl.ds(kind * HD, HD)] = qkv_ref[:, pl.ds((kind * QUAD + head) * HD, HD)]
    g_qkv[z, y, c] = stage[p]
    g_feat[0, pl.ds(local_rows - PAD, PAD), :] = jnp.zeros((PAD, width), jnp.bfloat16)
    g_feat[QUAD + 1, pl.ds(0, PAD), :] = jnp.zeros((PAD, width), jnp.bfloat16)

    barrier = pltpu.get_barrier_semaphore()

    def greet(device):
        pl.semaphore_signal(barrier, inc=1, device_id=device, device_id_type=pl.DeviceIdType.MESH)

    for device in quad:
        greet(device)
    greet(other)
    pl.when(z > 0)(lambda: greet(below))
    pl.when(z < ZS - 1)(lambda: greet(above))
    pl.semaphore_wait(barrier, 4 + jnp.where(z > 0, 1, 0) + jnp.where(z < ZS - 1, 1, 0))

    def remote(src, dst, send, recv, device):
        return pltpu.make_async_remote_copy(
            src_ref=src, dst_ref=dst, send_sem=send, recv_sem=recv,
            device_id=device, device_id_type=pl.DeviceIdType.MESH,
        )

    def along_z(q, source, up):
        part = gathered[q].at[source, y, c, twin]
        send = zp_send if up else zm_send
        return remote(part, part, send.at[q, source], z_recv.at[q, source], above if up else below)

    def along_y(q, source, column):
        part = gathered[q].at[source, column, c, twin]
        return remote(part, part, y_send.at[q, source], y_recv.at[q, source], across)

    def own_along_y(q, column):
        part = gathered[q].at[z, column, c]
        return remote(part, part, y_send.at[q, z], y_recv.at[q, z], across)

    def along_x(q, source, column, half):
        part = gathered[q].at[source, column, c, half]
        slot = (q, source, column)
        return remote(part, part, x_send.at[slot], x_recv.at[slot], other)

    def to_core(q, which, half):
        part = gathered[q].at[:, :, which, half]
        return remote(part, part, c_send.at[q, half], c_recv.at[q, half], core)

    def chain(i, source, up):
        part = kv.at[source] if i else g_qkv.at[source, twin]
        send = chain_p if up else chain_m
        return remote(part, part, send.at[i, source], chain_recv.at[i, source], above if up else below)

    def columns_across(source, half):
        part = g_qkv.at[source, half]
        return remote(part, part, half_send.at[source], half_recv.at[source], other)

    def columns_to(i, sender, receiver):
        return remote(stage.at[receiver], g_qkv.at[z, sender // 2, sender % 2], peer_send.at[0, i], peer_recv.at[0, i], quad[i])

    def features_to(i, block):
        part = g_feat.at[block + 1]
        return remote(part, part, feat_send.at[i], feat_recv.at[i], across if i == 0 else core)

    def context_to(i, sender, receiver):
        rows = pl.ds(pl.multiple_of(receiver * local_rows, local_rows), local_rows + 2 * HALO)
        return remote(ctx_out.at[rows], g_ctx.at[sender], peer_send.at[1, i], peer_recv.at[1, i], quad[i])

    def edge(up):
        rows = pl.ds(local_rows - PAD, PAD) if up else pl.ds(0, PAD)
        src, dst = (QUAD, 0) if up else (1, QUAD + 1)
        slot = 0 if up else 1
        return remote(
            g_feat.at[src, rows], g_feat.at[dst, rows], edge_send.at[slot], edge_recv.at[slot],
            above if up else below,
        )

    def spread(piece, item):
        pl.when(z < ZS - 1)(lambda: piece(item, z, True).start())
        pl.when(z > 0)(lambda: piece(item, z, False).start())

    def onward(piece, item, s, after=None):
        @pl.when(z >= s)
        def _():
            piece(item, z - s, True).wait_recv()
            pl.when(z < ZS - 1)(lambda: piece(item, z - s, True).start())
            if after is not None:
                after(z - s)

        @pl.when(z + s <= ZS - 1)
        def _():
            piece(item, z + s, False).wait_recv()
            pl.when(z > 0)(lambda: piece(item, z + s, False).start())
            if after is not None:
                after(z + s)

    def sent(piece, item):
        for s in range(ZS):
            pl.when((z >= s) & (z < ZS - 1))(lambda: piece(item, z - s, True).wait_send())
            if s == 0:
                pl.when(z > 0)(lambda: piece(item, z, False).wait_send())
            else:
                pl.when((z + s <= ZS - 1) & (z > 0))(lambda: piece(item, z + s, False).wait_send())

    def in_round(s, do):
        pl.when(z >= s)(lambda: do(z - s))
        pl.when(z + s <= ZS - 1)(lambda: do(z + s))

    def begin(q):
        for copy in own:
            copy.wait()
        spread(along_z, q)

    def begin_across(q):
        own_along_y(q, y).start()

    def columns_on(s):
        onward(chain, 0, s, lambda source: columns_across(source, twin).start())

    def pass_on(q, s):
        def after(source):
            along_y(q, source, y).start()
            along_x(q, source, y, twin).start()

        onward(along_z, q, s, after)

    def cross(q, s):
        def do(source):
            along_y(q, source, 1 - y).wait_recv()
            along_x(q, source, 1 - y, twin).start()

        in_round(s, do)
        if s == ZS - 1:
            own_along_y(q, 1 - y).wait_recv()
            to_core(q, c, twin).start()

    def swap(q):
        def do(source):
            for column in range(2):
                along_x(q, source, column, 1 - twin).wait_recv()

        for s in range(1, ZS):
            in_round(s, do)
        to_core(q, c, 1 - twin).start()

    def arrive(q):
        for half in range(2):
            to_core(q, 1 - c, half).wait_recv()

    def finish(q):
        def do(source):
            along_y(q, source, y).wait_send()
            for column in range(2):
                along_x(q, source, column, twin).wait_send()

        sent(along_z, q)
        own_along_y(q, y).wait_send()
        for s in range(1, ZS):
            in_round(s, do)
        for half in range(2):
            to_core(q, c, half).wait_send()

    def columns(i, start):
        block = g_rest[:, :, :, :, pl.ds(starts[i], counts[i]), pl.ds(start, CHUNK)]
        return block.reshape(-1, CHUNK)

    def at(j):
        return pl.multiple_of(j * CHUNK, CHUNK)

    def normalise():
        def some(i, carry):
            rows_n[pl.ds(pl.multiple_of(i * local_rows, local_rows), local_rows), :] = norm_rows(
                g_feat[i + 1], ln1_ref[...]
            )
            return carry

        lax.fori_loop(0, QUAD, some, 0)

    def key_values():
        weight = g_qkv[:, :, :, :, pl.ds(HD, 2 * HD)].reshape(-1, 2 * HD)
        kv[z] = jnp.dot(rows_n[...], weight, preferred_element_type=jnp.float32).astype(jnp.bfloat16)

    def queries():
        weight = g_qkv[:, :, :, :, pl.ds(0, HD)].reshape(-1, HD)
        query[pl.ds(0, quad_rows), :] = jnp.dot(
            rows_n[...], weight, preferred_element_type=jnp.float32
        ).astype(jnp.bfloat16)
        pl.when(z > 0)(lambda: edge(True).wait_recv())
        pl.when(z < ZS - 1)(lambda: edge(False).wait_recv())
        before = g_feat[0, pl.ds(local_rows - PAD, PAD), :].astype(jnp.float32)[PAD - HALO :]
        after = g_feat[QUAD + 1, pl.ds(0, PAD), :].astype(jnp.float32)[:HALO]
        edges = norm_rows(jnp.concatenate([before, after], axis=0), ln1_ref[...])
        query[pl.ds(quad_rows, 2 * HALO), :] = jnp.dot(
            edges, weight, preferred_element_type=jnp.float32
        ).astype(jnp.bfloat16)
        before = g_feat[p, pl.ds(local_rows - PAD, PAD), :].astype(jnp.float32)[PAD - HALO :]
        after = g_feat[p + 2, pl.ds(0, PAD), :].astype(jnp.float32)[:HALO]
        ext[pl.ds(0, HALO), :] = before
        ext[pl.ds(HALO, local_rows), :] = g_feat[p + 1].astype(jnp.float32)
        ext[pl.ds(HALO + local_rows, HALO), :] = after

    nearest = z - 1 + 2 * (1 - (z + 3) // 4)
    farthest = 3 * (1 - z // 2)
    meets = (z, nearest, 6 - z - nearest - farthest, farthest)

    def attend(k):
        source = meets[k]
        keys = kv[source, :, pl.ds(0, HD)]
        values = jnp.concatenate([kv[source, :, pl.ds(HD, HD)], jnp.ones((quad_rows, HD), jnp.bfloat16)], axis=1)
        factor = math.log2(math.e) / math.sqrt(HD)
        position = source * quad_rows + lax.broadcasted_iota(jnp.int32, (1, quad_rows), 1)
        bias = jnp.where(position < limit_ref[0], 0.0, -1e30)
        for i in range(query.shape[0] // BLOCK):
            rows = pl.ds(i * BLOCK, BLOCK)
            scores = lax.dot_general(
                query[rows, :], keys, (((1,), (1,)), ((), ())), preferred_element_type=jnp.float32
            ) + bias
            peak = jnp.max(scores, axis=-1, keepdims=True)
            if k > 0:
                before = peaks[rows, :][:, :1]
                peak = jnp.maximum(before, peak)
                shrink = jnp.exp2((before - peak) * factor)
            weights = jnp.exp2((scores - peak) * factor)
            summed = jnp.dot(weights.astype(jnp.bfloat16), values, preferred_element_type=jnp.float32)
            summed, total = summed[:, :HD], summed[:, HD:]
            if k > 0:
                total = total + totals[rows, :] * shrink
                summed = summed + ctx[rows, :] * shrink
            if k < ZS - 1:
                peaks[rows, :] = jnp.broadcast_to(peak, (BLOCK, HD))
                totals[rows, :] = total
                ctx[rows, :] = summed
            else:
                ctx[rows, :] = summed / total

    def share_context():
        ctx_out[...] = jnp.concatenate(
            [ctx[pl.ds(quad_rows, HALO), :], ctx[pl.ds(0, quad_rows), :], ctx[pl.ds(quad_rows + HALO, HALO), :]], axis=0
        ).astype(jnp.bfloat16)
        for i, partner in enumerate(partners):
            context_to(i, p, partner).start()
        rows = pl.ds(pl.multiple_of(p * local_rows, local_rows), local_rows + 2 * HALO)
        g_ctx[p] = ctx_out[rows, :]

    def collect_context():
        for i, partner in enumerate(partners):
            context_to(i, partner, p).wait_recv()
        for head in range(QUAD):
            context[:, pl.ds(head * HD, HD)] = g_ctx[head]

    def project():
        def some(j, carry):
            product = jnp.dot(context[...], columns(0, at(j)), preferred_element_type=jnp.float32)
            attended[:, pl.ds(at(j), CHUNK)] = ext[:, pl.ds(at(j), CHUNK)] + product
            return carry

        lax.fori_loop(0, width // CHUNK, some, 0, unroll=True)
        ext_n[...] = norm_rows(attended[...], ln2_ref[...])

    def convolve():
        def some(j, carry):
            value = jnp.dot(ext_n[...], columns(1, at(j)), preferred_element_type=jnp.float32)
            gates = jnp.dot(ext_n[...], columns(2, at(j)), preferred_element_type=jnp.float32)
            frame = me * local_rows - HALO + lax.broadcasted_iota(jnp.int32, value.shape, 0)
            valid = (frame >= 0) & (frame < limit_ref[0])
            gated = jnp.where(valid, value * jax.nn.sigmoid(gates), 0.0)
            gate[...] = gated.astype(jnp.bfloat16).astype(jnp.float32)
            taps = dw_ref.shape[0]
            cols = pl.ds(at(j), CHUNK)
            conv = jnp.zeros((local_rows, CHUNK), jnp.float32)
            for tap in range(taps):
                conv = conv + dw_ref[pl.ds(tap, 1), cols] * gate[pl.ds(HALO - taps // 2 + tap, local_rows), :]
            shifted = bns_ref[:, cols] * conv + bnb_ref[:, cols]
            act[:, cols] = (shifted / (1.0 + jnp.exp(-shifted))).astype(jnp.bfloat16)
            return carry

        lax.fori_loop(0, width // CHUNK, some, 0, unroll=True)

    def close():
        def some(j, carry):
            cols = pl.ds(at(j), CHUNK)
            product = jnp.dot(act[...], columns(3, at(j)), preferred_element_type=jnp.float32)
            result_ref[:, cols] = (attended[pl.ds(HALO, local_rows), cols] + product).astype(jnp.bfloat16)
            return carry

        lax.fori_loop(0, width // CHUNK, some, 0, unroll=True)

    for i, partner in enumerate(partners):
        columns_to(i, p, partner).start()
    own_feat.wait()
    features_to(0, p).start()
    features_to(1, p).start()
    begin(REST)
    for i, partner in enumerate(partners):
        columns_to(i, partner, p).wait_recv()
    spread(chain, 0)
    features_to(0, partners[0]).wait_recv()
    features_to(2, partners[0]).start()
    begin_across(REST)
    columns_on(1)
    pass_on(REST, 1)
    features_to(1, partners[1]).wait_recv()
    features_to(2, partners[2]).wait_recv()
    pl.when(z < ZS - 1)(lambda: edge(True).start())
    pl.when(z > 0)(lambda: edge(False).start())
    columns_on(2)
    normalise()
    columns_on(3)
    pass_on(REST, 2)
    for s in range(1, ZS):
        in_round(s, lambda source: columns_across(source, 1 - twin).wait_recv())
    key_values()
    spread(chain, 1)
    cross(REST, 1)
    queries()
    attend(0)
    pass_on(REST, 3)
    cross(REST, 2)
    onward(chain, 1, 1)
    attend(1)
    cross(REST, 3)
    onward(chain, 1, 2)
    attend(2)
    swap(REST)
    onward(chain, 1, 3)
    attend(3)
    share_context()
    for i, partner in enumerate(partners):
        columns_to(i, p, partner).wait_send()
    for i, block in enumerate((p, p, partners[0])):
        features_to(i, block).wait_send()
    pl.when(z < ZS - 1)(lambda: edge(True).wait_send())
    pl.when(z > 0)(lambda: edge(False).wait_send())
    for s in range(1, ZS):
        in_round(s, lambda source: columns_across(source, twin).wait_send())
    sent(chain, 0)
    arrive(REST)
    collect_context()
    project()
    convolve()
    close()
    finish(REST)
    sent(chain, 1)
    for i, partner in enumerate(partners):
        context_to(i, p, partner).wait_send()


def per_device_kernel(
    features, valid_length, ln1_gain, w_qkv, w_out, ln2_gain, w_pw1, w_dw, bn_scale, bn_shift, w_pw2
):
    local_rows, width = features.shape
    att = w_qkv.shape[1] // 3
    wide = local_rows + 2 * HALO

    def halves(weight):
        return weight.reshape(2, weight.shape[0] // 2, weight.shape[1])

    shards = [halves(w) for w in (w_out, w_pw1, w_pw2)]
    grid = (ZS, 2, 2)
    bf16, f32 = jnp.bfloat16, jnp.float32
    dma = pltpu.SemaphoreType.DMA
    hbm = pl.BlockSpec(memory_space=pl.ANY)
    vmem = pl.BlockSpec(memory_space=pltpu.VMEM)
    return pl.pallas_call(
        block_kernel,
        out_shape=jax.ShapeDtypeStruct((local_rows, width), bf16),
        in_specs=[
            pl.BlockSpec(memory_space=pltpu.SMEM), hbm, vmem, vmem, hbm, vmem, hbm, vmem, vmem, vmem, hbm,
        ],
        out_specs=vmem,
        scratch_shapes=[
            pltpu.VMEM((QUAD, w_qkv.shape[0], 3 * HD), bf16),
            pltpu.VMEM((ZS, 2, 2, w_qkv.shape[0], 3 * HD), bf16),
            pltpu.VMEM((QUAD + 2, local_rows, width), bf16),
            pltpu.VMEM((ZS, QUAD * local_rows, 2 * HD), bf16),
            pltpu.VMEM(grid + (2, sum(w.shape[1] for w in shards) + shards[1].shape[1], width), bf16),
            pltpu.VMEM((QUAD * local_rows, width), bf16),
            pltpu.VMEM((QUAD * local_rows + 2 * HALO, HD), bf16),
            pltpu.VMEM((QUAD * local_rows + 2 * HALO, HD), f32),
            pltpu.VMEM((QUAD * local_rows + 2 * HALO, HD), f32),
            pltpu.VMEM((QUAD * local_rows + 2 * HALO, HD), f32),
            pltpu.VMEM((QUAD * local_rows + 2 * HALO, HD), bf16),
            pltpu.VMEM((QUAD, wide, HD), bf16),
            pltpu.VMEM((wide, att), bf16),
            pltpu.VMEM((wide, width), f32),
            pltpu.VMEM((wide, width), bf16),
            pltpu.VMEM((wide, width), f32),
            pltpu.VMEM((wide, CHUNK), f32),
            pltpu.VMEM((local_rows, width), bf16),
            dma((9,)),
        ]
        + [dma((COUNT, ZS))] * 5
        + [dma((COUNT, ZS, 2))] * 2
        + [dma((COUNT, 2))] * 2
        + [dma((2, 3))] * 2
        + [dma((3,))] * 2
        + [dma((2,))] * 2
        + [dma((2, ZS))] * 3
        + [dma((ZS,))] * 2,
        compiler_params=pltpu.CompilerParams(
            collective_id=0, has_side_effects=True, vmem_limit_bytes=56 * 1024 * 1024
        ),
    )(
        valid_length, features, ln1_gain[None], w_qkv, shards[0], ln2_gain[None], shards[1], w_dw,
        bn_scale[None], bn_shift[None], shards[2],
    )


def per_device(*arguments):
    if lax.axis_size("frames") == 4 * ZS and lax.axis_size("groups") == 2:
        return per_device_kernel(*arguments)
    return per_device_xla(*arguments)


def solution(mesh):
    placed = (
        P(("groups", "frames"), None),
        P("groups"),
        P(),
        P("frames", None),
        P("frames", None),
        P(),
        P("frames", None),
        P(),
        P(),
        P(),
        P("frames", None),
    )
    return jax.shard_map(
        per_device,
        mesh=mesh,
        in_specs=placed,
        out_specs=P(("groups", "frames"), None),
        check_vma=False,
    )
```

```python
import functools
import math

import jax
import jax.numpy as jnp
from jax import lax
from jax.experimental import pallas as pl
from jax.experimental.pallas import tpu as pltpu
from jax.sharding import PartitionSpec as P

HEADS = 4
HD = 128


EPSILON = 1e-05


def extended(cells, sides, width):
    for axis, dim in sides:
        count = lax.axis_size(axis)
        ends = count - 1
        head = lax.slice_in_dim(cells, 0, width, axis=dim)
        tail = lax.slice_in_dim(cells, cells.shape[dim] - width, cells.shape[dim], axis=dim)
        cells = jnp.concatenate(
            [
                lax.ppermute(tail, axis, [(i, (i + 1) % count) for i in range(ends)]),
                cells,
                lax.ppermute(head, axis, [((i + 1) % count, i) for i in range(ends)]),
            ],
            axis=dim,
        )
    return cells


def layer_norm(values, gain):
    values = values.astype(jnp.float32)
    mean = jnp.mean(values, axis=-1, keepdims=True)
    centred = values - mean
    variance = jnp.mean(centred * centred, axis=-1, keepdims=True)
    return (centred * lax.rsqrt(variance + EPSILON) * gain).astype(jnp.bfloat16)


def per_device_xla(
    features, valid_length, ln1_gain, w_qkv, w_out, ln2_gain, w_pw1, w_dw, bn_scale, bn_shift, w_pw2
):
    limit = valid_length[0]
    local_rows = features.shape[0]
    width = features.shape[1]
    att_width = w_qkv.shape[1] // 3
    scale = 1.0 / math.sqrt(HD)
    tails = (
        lax.all_gather(w_out, "frames", axis=0, tiled=True),
        lax.all_gather(w_pw1, "frames", axis=0, tiled=True),
        lax.all_gather(w_pw2, "frames", axis=0, tiled=True),
    )
    full_out, full_pw1, full_pw2 = tails
    normed1 = layer_norm(features, ln1_gain)
    qkv = jnp.dot(
        normed1,
        lax.all_gather(w_qkv, "frames", axis=0, tiled=True),
        preferred_element_type=jnp.float32,
    ).astype(jnp.bfloat16)
    query_heads = qkv[:, :att_width].reshape(local_rows, HEADS, HD)
    keys = qkv[:, att_width : 2 * att_width]
    values = qkv[:, 2 * att_width :]
    maxima = jnp.full((HEADS, local_rows), -1e30, jnp.float32)
    key_rows = lax.all_gather(keys, "frames", axis=0, tiled=True)
    value_rows = lax.all_gather(values, "frames", axis=0, tiled=True)
    count = key_rows.shape[0]
    key_heads = key_rows.reshape(count, HEADS, HD)
    value_heads = value_rows.reshape(count, HEADS, HD)
    scores = (
        jnp.einsum("qhd,khd->hqk", query_heads, key_heads, preferred_element_type=jnp.float32)
        * scale
    )
    position = jnp.arange(count, dtype=jnp.int32)
    valid = (position < limit)[None, None, :]
    scores = jnp.where(valid, scores, -1e30)
    fresh = jnp.maximum(maxima, jnp.max(scores, axis=-1))
    weights = jnp.where(valid, jnp.exp(scores - fresh[..., None]), 0.0)
    totals = jnp.sum(weights, axis=-1)
    update = jnp.einsum(
        "hqk,khd->hqd",
        weights.astype(jnp.bfloat16),
        value_heads,
        preferred_element_type=jnp.float32,
    )
    summed = update
    maxima, totals, summed = (fresh, totals, summed)
    context = (
        (summed / totals[..., None])
        .transpose(1, 0, 2)
        .reshape(local_rows, att_width)
        .astype(jnp.bfloat16)
    )
    attended = features.astype(jnp.float32) + jnp.dot(
        context, full_out, preferred_element_type=jnp.float32
    )
    normed2 = layer_norm(attended, ln2_gain)
    both = jnp.dot(normed2, full_pw1, preferred_element_type=jnp.float32)
    frame_index = lax.axis_index("frames") * local_rows + jnp.arange(local_rows, dtype=jnp.int32)
    frame_valid = (frame_index < limit)[:, None]
    gated = jnp.where(frame_valid, both[:, :width] * jax.nn.sigmoid(both[:, width:]), 0.0).astype(
        jnp.bfloat16
    )
    half_window = (w_dw.shape[0] - 1) // 2
    widened = extended(gated, (("frames", 0),), half_window)
    widened = widened.astype(jnp.float32)
    conv = jnp.zeros((local_rows, width), jnp.float32)
    for tap in range(w_dw.shape[0]):
        conv = conv + w_dw[tap][None, :] * widened[tap : tap + local_rows]
    activated = jax.nn.silu(bn_scale * conv + bn_shift).astype(jnp.bfloat16)
    result = attended + jnp.dot(activated, full_pw2, preferred_element_type=jnp.float32)
    return result.astype(jnp.bfloat16)


ZS = 4
QUAD = 4
CHUNK = 256
PAD = 16
HALO = 8
BLOCK = 176
REST = 0
COUNT = 1


def norm_rows(values, gain):
    values = values.astype(jnp.float32)
    mean = jnp.mean(values, axis=-1, keepdims=True)
    centred = values - mean
    variance = jnp.mean(centred * centred, axis=-1, keepdims=True)
    return (centred * lax.rsqrt(variance + EPSILON) * gain).astype(jnp.bfloat16)


def block_kernel(
    limit_ref, feat_ref, ln1_ref, qkv_ref, out_w_ref, ln2_ref, pw1_ref, dw_ref, bns_ref, bnb_ref, pw2_ref,
    result_ref,
    stage, g_qkv, g_feat, kv, g_rest, rows_n, query, ctx, peaks, totals, ctx_out, g_ctx, context, ext, ext_n, attended,
    gate, act,
    local_sem, zp_send, zm_send, z_recv, y_send, y_recv, x_send, x_recv, c_send, c_recv,
    peer_send, peer_recv, feat_send, feat_recv, edge_send, edge_recv, chain_p, chain_m, chain_recv,
    half_send, half_recv,
):
    twin = lax.axis_index("groups")
    me = lax.axis_index("frames")
    z, y, c = me // 4, (me // 2) % 2, me % 2
    p = me % QUAD
    width = ext.shape[1]
    local_rows = feat_ref.shape[0]
    quad_rows = QUAD * local_rows
    gathered = (g_rest,)
    above, below = {"frames": me + 4}, {"frames": me - 4}
    partners = (QUAD // 2 * (1 - y) + c, 2 * y + 1 - c, QUAD // 2 * (1 - y) + 1 - c)
    quad = [{"frames": z * QUAD + partner} for partner in partners]
    across, core = quad[0], quad[1]
    other = {"groups": 1 - twin}

    counts = (out_w_ref.shape[1], pw1_ref.shape[1], pw1_ref.shape[1], pw2_ref.shape[1])
    starts = [sum(counts[:i]) for i in range(4)]
    own = []
    for half in range(2):
        pieces = (
            out_w_ref.at[half],
            pw1_ref.at[half, :, pl.ds(0, width)],
            pw1_ref.at[half, :, pl.ds(width, width)],
            pw2_ref.at[half],
        )
        for i in range(4):
            part = g_rest.at[z, y, c, half, pl.ds(starts[i], counts[i])]
            own.append(pltpu.make_async_copy(pieces[i], part, local_sem.at[4 * half + i]))
    own_feat = pltpu.make_async_copy(feat_ref, g_feat.at[p + 1], local_sem.at[8])
    for copy in own + [own_feat]:
        copy.start()
    for head in range(QUAD):
        for kind in range(3):
            stage[head, :, pl.ds(kind * HD, HD)] = qkv_ref[:, pl.ds((kind * QUAD + head) * HD, HD)]
    g_qkv[z, y, c] = stage[p]
    g_feat[0, pl.ds(local_rows - PAD, PAD), :] = jnp.zeros((PAD, width), jnp.bfloat16)
    g_feat[QUAD + 1, pl.ds(0, PAD), :] = jnp.zeros((PAD, width), jnp.bfloat16)

    barrier = pltpu.get_barrier_semaphore()

    def greet(device):
        pl.semaphore_signal(barrier, inc=1, device_id=device, device_id_type=pl.DeviceIdType.MESH)

    for device in quad:
        greet(device)
    greet(other)
    pl.when(z > 0)(lambda: greet(below))
    pl.when(z < ZS - 1)(lambda: greet(above))
    pl.semaphore_wait(barrier, 4 + jnp.where(z > 0, 1, 0) + jnp.where(z < ZS - 1, 1, 0))

    def remote(src, dst, send, recv, device):
        return pltpu.make_async_remote_copy(
            src_ref=src, dst_ref=dst, send_sem=send, recv_sem=recv,
            device_id=device, device_id_type=pl.DeviceIdType.MESH,
        )

    def along_z(q, source, up):
        part = gathered[q].at[source, y, c, twin]
        send = zp_send if up else zm_send
        return remote(part, part, send.at[q, source], z_recv.at[q, source], above if up else below)

    def along_y(q, source, column):
        part = gathered[q].at[source, column, c, twin]
        return remote(part, part, y_send.at[q, source], y_recv.at[q, source], across)

    def own_along_y(q, column):
        part = gathered[q].at[z, column, c]
        return remote(part, part, y_send.at[q, z], y_recv.at[q, z], across)

    def along_x(q, source, column, half):
        part = gathered[q].at[source, column, c, half]
        slot = (q, source, column)
        return remote(part, part, x_send.at[slot], x_recv.at[slot], other)

    def to_core(q, which, half):
        part = gathered[q].at[:, :, which, half]
        return remote(part, part, c_send.at[q, half], c_recv.at[q, half], core)

    def chain(i, source, up):
        part = kv.at[source] if i else g_qkv.at[source, twin]
        send = chain_p if up else chain_m
        return remote(part, part, send.at[i, source], chain_recv.at[i, source], above if up else below)

    def columns_across(source, half):
        part = g_qkv.at[source, half]
        return remote(part, part, half_send.at[source], half_recv.at[source], other)

    def columns_to(i, sender, receiver):
        return remote(stage.at[receiver], g_qkv.at[z, sender // 2, sender % 2], peer_send.at[0, i], peer_recv.at[0, i], quad[i])

    def features_to(i, block):
        part = g_feat.at[block + 1]
        return remote(part, part, feat_send.at[i], feat_recv.at[i], across if i == 0 else core)

    def context_to(i, sender, receiver):
        rows = pl.ds(pl.multiple_of(receiver * local_rows, local_rows), local_rows + 2 * HALO)
        return remote(ctx_out.at[rows], g_ctx.at[sender], peer_send.at[1, i], peer_recv.at[1, i], quad[i])

    def edge(up):
        rows = pl.ds(local_rows - PAD, PAD) if up else pl.ds(0, PAD)
        src, dst = (QUAD, 0) if up else (1, QUAD + 1)
        slot = 0 if up else 1
        return remote(
            g_feat.at[src, rows], g_feat.at[dst, rows], edge_send.at[slot], edge_recv.at[slot],
            above if up else below,
        )

    def spread(piece, item):
        pl.when(z < ZS - 1)(lambda: piece(item, z, True).start())
        pl.when(z > 0)(lambda: piece(item, z, False).start())

    def onward(piece, item, s, after=None):
        @pl.when(z >= s)
        def _():
            piece(item, z - s, True).wait_recv()
            pl.when(z < ZS - 1)(lambda: piece(item, z - s, True).start())
            if after is not None:
                after(z - s)

        @pl.when(z + s <= ZS - 1)
        def _():
            piece(item, z + s, False).wait_recv()
            pl.when(z > 0)(lambda: piece(item, z + s, False).start())
            if after is not None:
                after(z + s)

    def sent(piece, item):
        for s in range(ZS):
            pl.when((z >= s) & (z < ZS - 1))(lambda: piece(item, z - s, True).wait_send())
            if s == 0:
                pl.when(z > 0)(lambda: piece(item, z, False).wait_send())
            else:
                pl.when((z + s <= ZS - 1) & (z > 0))(lambda: piece(item, z + s, False).wait_send())

    def in_round(s, do):
        pl.when(z >= s)(lambda: do(z - s))
        pl.when(z + s <= ZS - 1)(lambda: do(z + s))

    def begin(q):
        for copy in own:
            copy.wait()
        spread(along_z, q)

    def begin_across(q):
        own_along_y(q, y).start()

    def columns_on(s):
        onward(chain, 0, s, lambda source: columns_across(source, twin).start())

    def pass_on(q, s):
        def after(source):
            along_y(q, source, y).start()
            along_x(q, source, y, twin).start()

        onward(along_z, q, s, after)

    def cross(q, s):
        def do(source):
            along_y(q, source, 1 - y).wait_recv()
            along_x(q, source, 1 - y, twin).start()

        in_round(s, do)
        if s == ZS - 1:
            own_along_y(q, 1 - y).wait_recv()
            to_core(q, c, twin).start()

    def swap(q):
        def do(source):
            for column in range(2):
                along_x(q, source, column, 1 - twin).wait_recv()

        for s in range(1, ZS):
            in_round(s, do)
        to_core(q, c, 1 - twin).start()

    def arrive(q):
        for half in range(2):
            to_core(q, 1 - c, half).wait_recv()

    def finish(q):
        def do(source):
            along_y(q, source, y).wait_send()
            for column in range(2):
                along_x(q, source, column, twin).wait_send()

        sent(along_z, q)
        own_along_y(q, y).wait_send()
        for s in range(1, ZS):
            in_round(s, do)
        for half in range(2):
            to_core(q, c, half).wait_send()

    def columns(i, start):
        block = g_rest[:, :, :, :, pl.ds(starts[i], counts[i]), pl.ds(start, CHUNK)]
        return block.reshape(-1, CHUNK)

    def at(j):
        return pl.multiple_of(j * CHUNK, CHUNK)

    def normalise():
        def some(i, carry):
            rows_n[pl.ds(pl.multiple_of(i * local_rows, local_rows), local_rows), :] = norm_rows(
                g_feat[i + 1], ln1_ref[...]
            )
            return carry

        lax.fori_loop(0, QUAD, some, 0)

    def key_values():
        weight = g_qkv[:, :, :, :, pl.ds(HD, 2 * HD)].reshape(-1, 2 * HD)
        kv[z] = jnp.dot(rows_n[...], weight, preferred_element_type=jnp.float32).astype(jnp.bfloat16)

    def queries():
        weight = g_qkv[:, :, :, :, pl.ds(0, HD)].reshape(-1, HD)
        query[pl.ds(0, quad_rows), :] = jnp.dot(
            rows_n[...], weight, preferred_element_type=jnp.float32
        ).astype(jnp.bfloat16)
        pl.when(z > 0)(lambda: edge(True).wait_recv())
        pl.when(z < ZS - 1)(lambda: edge(False).wait_recv())
        before = g_feat[0, pl.ds(local_rows - PAD, PAD), :].astype(jnp.float32)[PAD - HALO :]
        after = g_feat[QUAD + 1, pl.ds(0, PAD), :].astype(jnp.float32)[:HALO]
        edges = norm_rows(jnp.concatenate([before, after], axis=0), ln1_ref[...])
        query[pl.ds(quad_rows, 2 * HALO), :] = jnp.dot(
            edges, weight, preferred_element_type=jnp.float32
        ).astype(jnp.bfloat16)
        before = g_feat[p, pl.ds(local_rows - PAD, PAD), :].astype(jnp.float32)[PAD - HALO :]
        after = g_feat[p + 2, pl.ds(0, PAD), :].astype(jnp.float32)[:HALO]
        ext[pl.ds(0, HALO), :] = before
        ext[pl.ds(HALO, local_rows), :] = g_feat[p + 1].astype(jnp.float32)
        ext[pl.ds(HALO + local_rows, HALO), :] = after

    nearest = z - 1 + 2 * (1 - (z + 3) // 4)
    farthest = 3 * (1 - z // 2)
    meets = (z, nearest, 6 - z - nearest - farthest, farthest)

    def attend(k):
        source = meets[k]
        keys = kv[source, :, pl.ds(0, HD)]
        values = jnp.concatenate([kv[source, :, pl.ds(HD, HD)], jnp.ones((quad_rows, HD), jnp.bfloat16)], axis=1)
        factor = math.log2(math.e) / math.sqrt(HD)
        position = source * quad_rows + lax.broadcasted_iota(jnp.int32, (1, quad_rows), 1)
        bias = jnp.where(position < limit_ref[0], 0.0, -1e30)
        for i in range(query.shape[0] // BLOCK):
            rows = pl.ds(i * BLOCK, BLOCK)
            scores = lax.dot_general(
                query[rows, :], keys, (((1,), (1,)), ((), ())), preferred_element_type=jnp.float32
            ) + bias
            peak = jnp.max(scores, axis=-1, keepdims=True)
            if k > 0:
                before = peaks[rows, :][:, :1]
                peak = jnp.maximum(before, peak)
                shrink = jnp.exp2((before - peak) * factor)
            weights = jnp.exp2((scores - peak) * factor)
            summed = jnp.dot(weights.astype(jnp.bfloat16), values, preferred_element_type=jnp.float32)
            summed, total = summed[:, :HD], summed[:, HD:]
            if k > 0:
                total = total + totals[rows, :] * shrink
                summed = summed + ctx[rows, :] * shrink
            if k < ZS - 1:
                peaks[rows, :] = jnp.broadcast_to(peak, (BLOCK, HD))
                totals[rows, :] = total
                ctx[rows, :] = summed
            else:
                ctx[rows, :] = summed / total

    def share_context():
        ctx_out[...] = jnp.concatenate(
            [ctx[pl.ds(quad_rows, HALO), :], ctx[pl.ds(0, quad_rows), :], ctx[pl.ds(quad_rows + HALO, HALO), :]], axis=0
        ).astype(jnp.bfloat16)
        for i, partner in enumerate(partners):
            context_to(i, p, partner).start()
        rows = pl.ds(pl.multiple_of(p * local_rows, local_rows), local_rows + 2 * HALO)
        g_ctx[p] = ctx_out[rows, :]

    def collect_context():
        for i, partner in enumerate(partners):
            context_to(i, partner, p).wait_recv()
        for head in range(QUAD):
            context[:, pl.ds(head * HD, HD)] = g_ctx[head]

    def project():
        def some(j, carry):
            product = jnp.dot(context[...], columns(0, at(j)), preferred_element_type=jnp.float32)
            attended[:, pl.ds(at(j), CHUNK)] = ext[:, pl.ds(at(j), CHUNK)] + product
            return carry

        lax.fori_loop(0, width // CHUNK, some, 0, unroll=True)
        ext_n[...] = norm_rows(attended[...], ln2_ref[...])

    def convolve():
        def some(j, carry):
            value = jnp.dot(ext_n[...], columns(1, at(j)), preferred_element_type=jnp.float32)
            gates = jnp.dot(ext_n[...], columns(2, at(j)), preferred_element_type=jnp.float32)
            frame = me * local_rows - HALO + lax.broadcasted_iota(jnp.int32, value.shape, 0)
            valid = (frame >= 0) & (frame < limit_ref[0])
            gated = jnp.where(valid, value * jax.nn.sigmoid(gates), 0.0)
            gate[...] = gated.astype(jnp.bfloat16).astype(jnp.float32)
            taps = dw_ref.shape[0]
            cols = pl.ds(at(j), CHUNK)
            conv = jnp.zeros((local_rows, CHUNK), jnp.float32)
            for tap in range(taps):
                conv = conv + dw_ref[pl.ds(tap, 1), cols] * gate[pl.ds(HALO - taps // 2 + tap, local_rows), :]
            shifted = bns_ref[:, cols] * conv + bnb_ref[:, cols]
            act[:, cols] = (shifted / (1.0 + jnp.exp(-shifted))).astype(jnp.bfloat16)
            return carry

        lax.fori_loop(0, width // CHUNK, some, 0, unroll=True)

    def close():
        def some(j, carry):
            cols = pl.ds(at(j), CHUNK)
            product = jnp.dot(act[...], columns(3, at(j)), preferred_element_type=jnp.float32)
            result_ref[:, cols] = (attended[pl.ds(HALO, local_rows), cols] + product).astype(jnp.bfloat16)
            return carry

        lax.fori_loop(0, width // CHUNK, some, 0, unroll=True)

    for i, partner in enumerate(partners):
        columns_to(i, p, partner).start()
    own_feat.wait()
    features_to(0, p).start()
    features_to(1, p).start()
    begin(REST)
    for i, partner in enumerate(partners):
        columns_to(i, partner, p).wait_recv()
    spread(chain, 0)
    features_to(0, partners[0]).wait_recv()
    features_to(2, partners[0]).start()
    begin_across(REST)
    columns_on(1)
    features_to(1, partners[1]).wait_recv()
    features_to(2, partners[2]).wait_recv()
    pl.when(z < ZS - 1)(lambda: edge(True).start())
    pl.when(z > 0)(lambda: edge(False).start())
    columns_on(2)
    pass_on(REST, 1)
    normalise()
    columns_on(3)
    for s in range(1, ZS):
        in_round(s, lambda source: columns_across(source, 1 - twin).wait_recv())
    key_values()
    spread(chain, 1)
    pass_on(REST, 2)
    cross(REST, 1)
    queries()
    onward(chain, 1, 1)
    attend(0)
    pass_on(REST, 3)
    cross(REST, 2)
    onward(chain, 1, 2)
    attend(1)
    cross(REST, 3)
    attend(2)
    swap(REST)
    onward(chain, 1, 3)
    attend(3)
    share_context()
    for i, partner in enumerate(partners):
        columns_to(i, p, partner).wait_send()
    for i, block in enumerate((p, p, partners[0])):
        features_to(i, block).wait_send()
    pl.when(z < ZS - 1)(lambda: edge(True).wait_send())
    pl.when(z > 0)(lambda: edge(False).wait_send())
    for s in range(1, ZS):
        in_round(s, lambda source: columns_across(source, twin).wait_send())
    sent(chain, 0)
    arrive(REST)
    collect_context()
    project()
    convolve()
    finish(REST)
    sent(chain, 1)
    close()
    for i, partner in enumerate(partners):
        context_to(i, p, partner).wait_send()


def per_device_kernel(
    features, valid_length, ln1_gain, w_qkv, w_out, ln2_gain, w_pw1, w_dw, bn_scale, bn_shift, w_pw2
):
    local_rows, width = features.shape
    att = w_qkv.shape[1] // 3
    wide = local_rows + 2 * HALO

    def halves(weight):
        return weight.reshape(2, weight.shape[0] // 2, weight.shape[1])

    shards = [halves(w) for w in (w_out, w_pw1, w_pw2)]
    grid = (ZS, 2, 2)
    bf16, f32 = jnp.bfloat16, jnp.float32
    dma = pltpu.SemaphoreType.DMA
    hbm = pl.BlockSpec(memory_space=pl.ANY)
    vmem = pl.BlockSpec(memory_space=pltpu.VMEM)
    return pl.pallas_call(
        block_kernel,
        out_shape=jax.ShapeDtypeStruct((local_rows, width), bf16),
        in_specs=[
            pl.BlockSpec(memory_space=pltpu.SMEM), hbm, vmem, vmem, hbm, vmem, hbm, vmem, vmem, vmem, hbm,
        ],
        out_specs=vmem,
        scratch_shapes=[
            pltpu.VMEM((QUAD, w_qkv.shape[0], 3 * HD), bf16),
            pltpu.VMEM((ZS, 2, 2, w_qkv.shape[0], 3 * HD), bf16),
            pltpu.VMEM((QUAD + 2, local_rows, width), bf16),
            pltpu.VMEM((ZS, QUAD * local_rows, 2 * HD), bf16),
            pltpu.VMEM(grid + (2, sum(w.shape[1] for w in shards) + shards[1].shape[1], width), bf16),
            pltpu.VMEM((QUAD * local_rows, width), bf16),
            pltpu.VMEM((QUAD * local_rows + 2 * HALO, HD), bf16),
            pltpu.VMEM((QUAD * local_rows + 2 * HALO, HD), f32),
            pltpu.VMEM((QUAD * local_rows + 2 * HALO, HD), f32),
            pltpu.VMEM((QUAD * local_rows + 2 * HALO, HD), f32),
            pltpu.VMEM((QUAD * local_rows + 2 * HALO, HD), bf16),
            pltpu.VMEM((QUAD, wide, HD), bf16),
            pltpu.VMEM((wide, att), bf16),
            pltpu.VMEM((wide, width), f32),
            pltpu.VMEM((wide, width), bf16),
            pltpu.VMEM((wide, width), f32),
            pltpu.VMEM((wide, CHUNK), f32),
            pltpu.VMEM((local_rows, width), bf16),
            dma((9,)),
        ]
        + [dma((COUNT, ZS))] * 5
        + [dma((COUNT, ZS, 2))] * 2
        + [dma((COUNT, 2))] * 2
        + [dma((2, 3))] * 2
        + [dma((3,))] * 2
        + [dma((2,))] * 2
        + [dma((2, ZS))] * 3
        + [dma((ZS,))] * 2,
        compiler_params=pltpu.CompilerParams(
            collective_id=0, has_side_effects=True, vmem_limit_bytes=56 * 1024 * 1024
        ),
    )(
        valid_length, features, ln1_gain[None], w_qkv, shards[0], ln2_gain[None], shards[1], w_dw,
        bn_scale[None], bn_shift[None], shards[2],
    )


def per_device(*arguments):
    if lax.axis_size("frames") == 4 * ZS and lax.axis_size("groups") == 2:
        return per_device_kernel(*arguments)
    return per_device_xla(*arguments)


def solution(mesh):
    placed = (
        P(("groups", "frames"), None),
        P("groups"),
        P(),
        P("frames", None),
        P("frames", None),
        P(),
        P("frames", None),
        P(),
        P(),
        P(),
        P("frames", None),
    )
    return jax.shard_map(
        per_device,
        mesh=mesh,
        in_specs=placed,
        out_specs=P(("groups", "frames"), None),
        check_vma=False,
    )
```
